32 devices in a mesh: section: 4 (over y, x), row: 8 (over z, core).
Axes of the slice: x: 2, y: 2, z: 4, core: 2. Of those that a mesh axis runs over, the one named last changes fastest.
Arguments:
- tokens: int32 [4, 16, 128], P(None, 'row'), may hold values from 0 to 32
- embed: bfloat16 [33, 768], replicated, may hold values from -6 to 6
- ln_gain: float32 [4, 768], P('section'), may hold values from 0.5 to 1.5
- w_qkv: bfloat16 [4, 768, 2304], P('section'), may hold values from -0.21875 to 0.21875
- w_out: bfloat16 [4, 768, 768], P('section'), may hold values from -0.21875 to 0.21875
- out_grad: bfloat16 [4, 16, 128, 768], P(None, 'row'), may hold values from -0.01977539 to 0.01977539
Outputs:
- grad_qkv: float32 [4, 768, 2304], P('section', 'row')
- grad_out: float32 [4, 768, 768], P('section', 'row')
- grad_gain: float32 [4, 768], P('section', 'row')
The draws below stay inside these ranges and needn't reach their ends.
All inputs are finite; a program needn't handle non-finite values.
Results may differ from the reference program's by a relative error of at most 0.04.
Values may be sent and summed in bfloat16 or wider, within the bound.
No kernel may reach another device: no remote copies, remote signals or barrier semaphores. Data moves between devices by JAX's collectives and lax.ppermute only.
A program may use at most 192 MiB of HBM per device.

```python
import jax
import jax.numpy as jnp
from jax import lax

D = 768
HEADS = 12
HEAD_DIM = 64
VOCAB = 33
SEQ = 128
MICRO = 4
LAYERS = 4
ROWS = 16


def touch_ends(values, own_key, low, high):
    longest = values.shape.index(max(values.shape))
    spots = []
    for shift in (0, 1):
        where = [jax.random.randint(jax.random.fold_in(own_key, axis), (), 0, length) for axis, length in enumerate(values.shape)]
        where[longest] = (where[longest] + shift) % values.shape[longest]
        spots.append(tuple(where))
    return values.at[spots[0]].set(low).at[spots[1]].set(high)


def steps_of(stream_key, dims, pieces, least, top_value):
    factor_of = 1.0
    for dim, shards_of in pieces:
        draws = jax.random.uniform(jax.random.fold_in(jax.random.fold_in(stream_key, 6), dim), (shards_of,), jnp.float32, least / len(pieces), top_value / len(pieces))
        factor_of = factor_of * jnp.repeat(jnp.exp(draws), dims[dim] // shards_of).reshape((-1,) + (1,) * (len(dims) - 1 - dim))
    return factor_of


def normal_values(rng, shape, scale, limit, shards=(), held_as=jnp.bfloat16):
    array = jax.random.normal(rng, shape, jnp.float32) * scale
    if len(shards) > 0:
        array = steps_of(rng, shape, shards, -0.22, 0.18) * array
    return jnp.clip(array, min=-limit, max=limit).astype(held_as)


def setup_inputs(seed: int = 0) -> dict:
    seeds = jax.random.split(jax.random.key(seed), 7)
    tokens = touch_ends(jax.random.randint(seeds[0], (MICRO, ROWS, SEQ), 0, VOCAB), jax.random.fold_in(seeds[0], 1), 0, VOCAB - 1).astype(jnp.int32)
    embed = normal_values(seeds[1], (VOCAB, D), 1.0, 6.0)
    ln_gain = jnp.clip(1.0 + 0.1 * jax.random.normal(seeds[2], (LAYERS, D), jnp.float32), 0.5, 1.5)
    w_qkv = normal_values(seeds[3], (LAYERS, D, 3 * D), D ** -0.5, 0.21875, ((0, 4),))
    w_out = normal_values(seeds[4], (LAYERS, D, D), D ** -0.5, 0.21875, ((0, 4),))
    out_grad = normal_values(seeds[5], (MICRO, ROWS, SEQ, D), (0.3 * (MICRO * ROWS * SEQ) ** -0.5), 0.01977539, ((1, 8),))
    return dict(tokens=tokens, embed=embed, ln_gain=ln_gain, w_qkv=w_qkv, w_out=w_out, out_grad=out_grad)


def norm_rows(x, gain):
    values = x.astype(jnp.float32)
    centred = values - lax.optimization_barrier(jnp.mean(values, axis=-1, keepdims=True))
    spread = lax.optimization_barrier(jnp.mean(centred * centred, axis=-1, keepdims=True))
    return (centred * lax.rsqrt(spread + 1e-05) * gain).astype(jnp.bfloat16)

def split_heads(qkv):
    parts = qkv.reshape(qkv.shape[0], qkv.shape[1], 3, HEADS, HEAD_DIM)
    return (parts[:, :, 0], parts[:, :, 1], parts[:, :, 2])

def layer_forward(x, gain, wqkv, wout, scale):
    nrows, seq, width = x.shape
    normed = norm_rows(x, gain)
    qkv = jnp.dot(normed.reshape(-1, width), wqkv, preferred_element_type=jnp.float32).astype(jnp.bfloat16)
    qkv = qkv.reshape(nrows, seq, 3 * width)
    query, keys, values = split_heads(qkv)
    logits = scale * jnp.einsum('rihd,rjhd->ihj', query.astype(jnp.float32), keys.astype(jnp.float32))
    probs = jax.nn.softmax(logits, axis=-1).astype(jnp.bfloat16)
    mixed = jnp.einsum('ihj,rjhd->rihd', probs.astype(jnp.float32), values.astype(jnp.float32)).astype(jnp.bfloat16)
    mixed = mixed.reshape(-1, width)
    output = x + jnp.dot(mixed, wout, preferred_element_type=jnp.float32).reshape(nrows, seq, width)
    return (output, probs, qkv)

def layer_backward(x, gain, wqkv, wout, probs, qkv, upstream, scale):
    nrows, seq, width = x.shape
    query, keys, values = split_heads(qkv)
    normed, norm_back = jax.vjp(norm_rows, x, gain)
    mixed = jnp.einsum('ihj,rjhd->rihd', probs.astype(jnp.float32), values.astype(jnp.float32)).astype(jnp.bfloat16)
    flat_up = upstream.astype(jnp.bfloat16).reshape(-1, width)
    g_out = jnp.dot(mixed.reshape(-1, width).T, flat_up, preferred_element_type=jnp.float32)
    d_mixed = jnp.dot(flat_up, wout.T, preferred_element_type=jnp.float32).astype(jnp.bfloat16)
    d_mixed = d_mixed.reshape(nrows, seq, HEADS, HEAD_DIM)
    d_probs = jnp.einsum('rihd,rjhd->ihj', d_mixed.astype(jnp.float32), values.astype(jnp.float32))
    prob_f = probs.astype(jnp.float32)
    d_logits = (prob_f * (d_probs - lax.optimization_barrier(jnp.sum(d_probs * prob_f, axis=-1, keepdims=True)))).astype(jnp.bfloat16)
    d_values = jnp.einsum('ihj,rihd->rjhd', prob_f, d_mixed.astype(jnp.float32)).astype(jnp.bfloat16)
    d_query = (scale * jnp.einsum('ihj,rjhd->rihd', d_logits.astype(jnp.float32), keys.astype(jnp.float32))).astype(jnp.bfloat16)
    d_keys = (scale * jnp.einsum('ihj,rihd->rjhd', d_logits.astype(jnp.float32), query.astype(jnp.float32))).astype(jnp.bfloat16)
    d_qkv = jnp.stack([d_query, d_keys, d_values], axis=2).reshape(-1, 3 * width)
    g_qkv = jnp.dot(normed.reshape(-1, width).T, d_qkv, preferred_element_type=jnp.float32)
    d_normed = jnp.dot(d_qkv, wqkv.T, preferred_element_type=jnp.float32).astype(jnp.bfloat16)
    d_input, g_gain = norm_back(d_normed.reshape(nrows, seq, width))
    d_x = upstream + d_input
    return (d_x, g_qkv, g_out, g_gain)

def reference(tokens, embed, ln_gain, w_qkv, w_out, out_grad):
    scale = HEAD_DIM ** (-0.5) / ROWS ** 0.5
    grad_qkv = jnp.zeros(w_qkv.shape, jnp.float32)
    grad_out = jnp.zeros(w_out.shape, jnp.float32)
    grad_gain = jnp.zeros(ln_gain.shape, jnp.float32)
    for micro in range(MICRO):
        state = jnp.take(embed, tokens[micro], axis=0).astype(jnp.float32)
        inputs_kept = []
        probs_kept = []
        qkv_kept = []
        for layer in range(LAYERS):
            inputs_kept.append(state)
            state, probs, qkv = layer_forward(state, ln_gain[layer], w_qkv[layer], w_out[layer], scale)
            probs_kept.append(probs)
            qkv_kept.append(qkv)
        upstream = out_grad[micro].astype(jnp.float32)
        for layer in reversed(range(LAYERS)):
            upstream, g_qkv, g_out, g_gain = layer_backward(inputs_kept[layer], ln_gain[layer], w_qkv[layer], w_out[layer], probs_kept[layer], qkv_kept[layer], upstream, scale)
            grad_qkv = grad_qkv.at[layer].add(g_qkv)
            grad_out = grad_out.at[layer].add(g_out)
            grad_gain = grad_gain.at[layer].add(g_gain)
    return (grad_qkv, grad_out, grad_gain)
```

```python
import functools
import math

import jax
import jax.numpy as jnp
from jax import lax
from jax.experimental import pallas as pl
from jax.experimental.pallas import tpu as pltpu
from jax.sharding import PartitionSpec as P

HEADS = 12
HEAD_DIM = 64
PACK = 128 // HEAD_DIM
F32 = jnp.float32
BF16 = jnp.bfloat16
VMEM_LIMIT = 48 * 1024 * 1024
NT = (((1,), (1,)), ((), ()))
TN = (((0,), (0,)), ((), ()))


def mm(a, b):
    return jnp.dot(a, b, preferred_element_type=F32)


def mm_nt(a, b):
    return lax.dot_general(a, b, NT, preferred_element_type=F32)


def lane_masks(lanes):
    place = lax.broadcasted_iota(jnp.int32, (1, lanes), 1) % (PACK * HEAD_DIM) // HEAD_DIM
    return [(place == n).astype(F32).astype(BF16) for n in range(PACK)]


def rows_to_lanes(ref, seq, first):
    width = PACK * HEAD_DIM
    count = ref.shape[0] // seq
    return jnp.concatenate(
        [ref[r * seq : (r + 1) * seq, first : first + width] for r in range(count)], axis=1
    )


def heads_to_rows(cat, masks):
    return jnp.concatenate([cat * mask for mask in masks], axis=0)


def lanes_to_rows(ref, seq, first, value):
    width = PACK * HEAD_DIM
    for r in range(ref.shape[0] // seq):
        ref[r * seq : (r + 1) * seq, first : first + width] = value[:, r * width : (r + 1) * width]


class Weights:
    def __init__(self, choice, member, own, pieces, columns, dst, sems):
        self.choice, self.member, self.own, self.pieces = choice, member, own, pieces
        self.columns, self.dst, self.sems = columns, dst, sems

    def each(self, act):
        @pl.when(self.choice == 0)
        def _():
            act(pltpu.make_async_copy(self.own.at[0], self.dst, self.sems.at[0]))

        for offset, group in self.pieces.items():

            @pl.when(self.choice == offset)
            def _(group=group):
                seen = 0
                for ref in group:
                    rows = ref.shape[1]
                    for n in range(ref.shape[0]):
                        start = pl.multiple_of((self.member ^ seen) * rows, rows)
                        act(
                            pltpu.make_async_copy(
                                ref.at[n, :, self.columns],
                                self.dst.at[pl.ds(start, rows)],
                                self.sems.at[seen],
                            )
                        )
                        seen += 1

    def start(self):
        self.each(lambda copy: copy.start())

    def wait(self):
        self.each(lambda copy: copy.wait())


def take_pieces(it, layout):
    return {offset: [next(it) for _ in range(count)] for offset, count in layout}


def softmax_heads(la, lb, scale, keep):
    seq = la.shape[0]
    for h in range(HEADS):
        at = slice(h * seq, (h + 1) * seq)
        logits = (la[:, at] + lb[:, at]) * scale
        e = jnp.exp(logits - jnp.max(logits, axis=-1, keepdims=True))
        keep(h, e / jnp.sum(e, axis=-1, keepdims=True))


def norm_parts(x):
    centred = x - jnp.mean(x, axis=-1, keepdims=True)
    spread = jnp.mean(centred * centred, axis=-1, keepdims=True)
    rstd = lax.rsqrt(spread + 1e-05)
    return centred * rstd, rstd


def pair_scores(ref_a, first_a, ref_b, first_b, out, out_rows, seq, masks, begin):
    width = PACK * HEAD_DIM
    for p in range(HEADS // PACK):
        a = rows_to_lanes(ref_a, seq, first_a + p * width)
        b = heads_to_rows(rows_to_lanes(ref_b, seq, first_b + p * width), masks)
        at = slice(p * PACK * seq, (p + 1) * PACK * seq)
        part = mm_nt(a, b)

        @pl.when(begin)
        def _():
            out[out_rows, at] = part

        @pl.when(jnp.logical_not(begin))
        def _():
            out[out_rows, at] += part


def pair_mix(weights, ref_b, first_b, out, first_out, scale, seq, masks):
    width = PACK * HEAD_DIM
    for p in range(HEADS // PACK):
        b = heads_to_rows(rows_to_lanes(ref_b, seq, first_b + p * width), masks)
        value = mm(weights[:, p * PACK * seq : (p + 1) * PACK * seq], b)
        if scale is not None:
            value = value * scale
        lanes_to_rows(out, seq, first_out + p * width, value.astype(BF16))


def forward_kernel(has_prev, has_top, layout, scale, seq, width, info, *refs):
    it = iter(refs)
    if has_prev:
        la, lb, v_prev = next(it), next(it), next(it)
    x_in, gain = next(it), next(it)
    top = next(it) if has_top else None
    own_q, own_o = next(it), next(it)
    pieces = take_pieces(it, layout)
    if has_prev:
        probs_out, mixed_out, x_out = next(it), next(it), next(it)
    h_out, qkv_out, score_out = next(it), next(it), next(it)
    if has_top:
        dmix_out = next(it)
    wq, sem_q = next(it), next(it)
    if has_prev:
        wo, sem_o = next(it), next(it)
    if has_top:
        wt, sem_t = next(it), next(it)
    step = pl.program_id(0)
    masks = lane_masks(PACK * HEAD_DIM * (x_in.shape[0] // seq))
    qcols, ocols = slice(0, 3 * width), slice(3 * width, 4 * width)

    @pl.when(step == 0)
    def _():
        jobs = []
        if has_prev:
            jobs.append(Weights(info[1], info[2], own_o, pieces, ocols, wo, sem_o))
        jobs.append(Weights(info[0], info[2], own_q, pieces, qcols, wq, sem_q))
        if has_top:
            jobs.append(Weights(info[0], info[2], own_o, pieces, ocols, wt, sem_t))
        for job in jobs:
            job.start()
        if has_prev:

            def keep(h, value):
                probs_out[:, h * seq : (h + 1) * seq] = value.astype(BF16)

            softmax_heads(la, lb, scale, keep)
        for job in jobs:
            job.wait()

    if has_prev:
        pair_mix(probs_out, v_prev, 0, mixed_out, 0, None, seq, masks)
        x = x_in[...] + mm(mixed_out[...], wo[...])
        x_out[...] = x
    else:
        x = x_in[...]
    hat, _ = norm_parts(x)
    h = (hat * gain[...]).astype(BF16)
    h_out[...] = h
    for t in range(3):
        at = slice(t * width, (t + 1) * width)
        qkv_out[:, at] = mm(h, wq[:, at]).astype(BF16)
    begin = step == 0
    pair_scores(qkv_out, 0, qkv_out, width, score_out, slice(0, seq), seq, masks, begin)
    if has_top:
        dmix_out[...] = mm_nt(top[...], wt[...]).astype(BF16)
        pair_scores(
            dmix_out, 0, qkv_out, 2 * width, score_out, slice(seq, 2 * seq), seq, masks, begin
        )


def backward_kernel(is_top, is_last, layout, scale, seq, width, info, *refs):
    it = iter(refs)
    sa, sb = next(it), next(it)
    if not is_top:
        probs = next(it)
    qkv, dmix, x_in, gain = next(it), next(it), next(it), next(it)
    if not is_last:
        dy, v_prev = next(it), next(it)
    own_q, own_o = next(it), next(it)
    pieces = take_pieces(it, layout)
    dqkv_out, gain_out = next(it), next(it)
    if is_top:
        mixed_out = next(it)
    if not is_last:
        dy_out, dyb_out, dmix_out, score_out = next(it), next(it), next(it), next(it)
    dl, dlt, pt = next(it), next(it), next(it)
    if is_top:
        probs = next(it)
    wq, sem_q = next(it), next(it)
    if not is_last:
        wo, sem_o = next(it), next(it)
    step = pl.program_id(0)
    masks = lane_masks(PACK * HEAD_DIM * (x_in.shape[0] // seq))
    qcols, ocols = slice(0, 3 * width), slice(3 * width, 4 * width)

    @pl.when(step == 0)
    def _():
        jobs = [Weights(info[0], info[2], own_q, pieces, qcols, wq, sem_q)]
        if not is_last:
            jobs.append(Weights(info[1], info[2], own_o, pieces, ocols, wo, sem_o))
        for job in jobs:
            job.start()
        if is_top:

            def keep(h, value):
                probs[:, h * seq : (h + 1) * seq] = value.astype(BF16)

            softmax_heads(sa.at[0:seq], sb.at[0:seq], scale, keep)
        first = seq if is_top else 0
        for h in range(HEADS):
            at = slice(h * seq, (h + 1) * seq)
            prob = probs[:, at].astype(F32)
            d_prob = sa[first : first + seq, at] + sb[first : first + seq, at]
            d_logit = prob * (d_prob - jnp.sum(d_prob * prob, axis=-1, keepdims=True))
            dl[:, at] = d_logit.astype(BF16)
            dlt[:, at] = jnp.transpose(d_logit).astype(BF16)
            pt[:, at] = jnp.transpose(prob).astype(BF16)
        for job in jobs:
            job.wait()

    if is_top:
        pair_mix(probs, qkv, 2 * width, mixed_out, 0, None, seq, masks)
    pair_mix(dl, qkv, width, dqkv_out, 0, scale, seq, masks)
    pair_mix(dlt, qkv, 0, dqkv_out, width, scale, seq, masks)
    pair_mix(pt, dmix, 0, dqkv_out, 2 * width, None, seq, masks)
    d_h = mm_nt(dqkv_out[...], wq[...]).astype(BF16).astype(F32)
    hat, rstd = norm_parts(x_in[...])
    part = jnp.sum(d_h * hat, axis=0, keepdims=True)

    @pl.when(step == 0)
    def _():
        gain_out[...] = part

    @pl.when(step > 0)
    def _():
        gain_out[...] += part

    if not is_last:
        d_hat = d_h * gain[...]
        mean_d = jnp.mean(d_hat, axis=-1, keepdims=True)
        mean_dh = jnp.mean(d_hat * hat, axis=-1, keepdims=True)
        d_x = dy[...].astype(F32) + rstd * (d_hat - mean_d - hat * mean_dh)
        dy_out[...] = d_x
        dyb_out[...] = d_x.astype(BF16)
        dmix_out[...] = mm_nt(dyb_out[...], wo[...]).astype(BF16)
        pair_scores(dmix_out, 0, v_prev, 0, score_out, slice(0, seq), seq, masks, step == 0)


class Chain:
    def __init__(self, section, member, n_group, own, gathered, seq, width, rows, scale):
        self.section, self.member, self.n_group = section, member, n_group
        self.own, self.seq, self.width, self.rows = own, seq, width, rows
        self.scale = scale
        self.layout = tuple((offset, len(group)) for offset, group in gathered.items())
        self.weights = [own[0], own[1]] + [a for group in gathered.values() for a in group]
        per_step = 4 if rows % 4 == 0 else (2 if rows % 2 == 0 else 1)
        self.chunk = per_step * seq
        self.steps = rows // per_step

    def info(self, now, other):
        return jnp.stack(
            [self.section ^ now, self.section ^ other, self.member]
        ).astype(jnp.int32)

    def whole(self, rows, lanes):
        return pl.BlockSpec((rows, lanes), lambda i, s: (0, 0))

    def tile(self, lanes, column=0):
        return pl.BlockSpec((self.chunk, lanes), lambda i, s: (i, column))

    def call(self, body, name, info, ins, in_specs, outs, out_specs, scratch, flops):
        size = sum(math.prod(o.shape) * o.dtype.itemsize for o in outs)
        size += sum(math.prod(a.shape) * a.dtype.itemsize for a in ins)
        any_spec = pl.BlockSpec(memory_space=pl.ANY)
        return pl.pallas_call(
            body,
            name=name,
            out_shape=outs,
            grid_spec=pltpu.PrefetchScalarGridSpec(
                num_scalar_prefetch=1,
                grid=(self.steps,),
                in_specs=in_specs + [any_spec] * len(self.weights),
                out_specs=out_specs,
                scratch_shapes=scratch,
            ),
            compiler_params=pltpu.CompilerParams(
                dimension_semantics=("arbitrary",), vmem_limit_bytes=VMEM_LIMIT
            ),
            cost_estimate=pl.CostEstimate(flops=flops, bytes_accessed=size, transcendentals=0),
        )(info, *ins, *self.weights)

    def wq_scratch(self):
        return [
            pltpu.VMEM((self.width, 3 * self.width), BF16),
            pltpu.SemaphoreType.DMA((self.n_group,)),
        ]

    def wo_scratch(self):
        return [
            pltpu.VMEM((self.width, self.width), BF16),
            pltpu.SemaphoreType.DMA((self.n_group,)),
        ]

    def forward(self, layer, x, gain, prev, top):
        seq, width = self.seq, self.width
        n = self.rows * seq
        hw = HEADS * seq
        ins, in_specs, outs, out_specs = [], [], [], []
        if prev is not None:
            ins += [prev[0], prev[1], prev[2]]
            in_specs += [self.whole(seq, hw), self.whole(seq, hw), self.tile(width, 2)]
            outs += [
                jax.ShapeDtypeStruct((seq, hw), BF16),
                jax.ShapeDtypeStruct((n, width), BF16),
                jax.ShapeDtypeStruct((n, width), F32),
            ]
            out_specs += [self.whole(seq, hw), self.tile(width), self.tile(width)]
        ins += [x, gain]
        in_specs += [self.tile(width), self.whole(1, width)]
        score_rows = seq
        if top is not None:
            ins.append(top)
            in_specs.append(self.tile(width))
            score_rows = 2 * seq
        outs += [
            jax.ShapeDtypeStruct((n, width), BF16),
            jax.ShapeDtypeStruct((n, 3 * width), BF16),
            jax.ShapeDtypeStruct((score_rows, hw), F32),
        ]
        out_specs += [self.tile(width), self.tile(3 * width), self.whole(score_rows, hw)]
        scratch = self.wq_scratch()
        if prev is not None:
            scratch += self.wo_scratch()
        if top is not None:
            outs.append(jax.ShapeDtypeStruct((n, width), BF16))
            out_specs.append(self.tile(width))
            scratch += self.wo_scratch()
        body = functools.partial(
            forward_kernel, prev is not None, top is not None, self.layout, self.scale, seq, width
        )
        return self.call(
            body,
            f"layer_in_{layer}",
            self.info(layer, max(layer - 1, 0)),
            ins,
            in_specs,
            outs,
            out_specs,
            scratch,
            2 * n * width * width * 5,
        )

    def backward(self, layer, scores, probs, qkv, dmix, x, gain, dy, v_prev):
        seq, width = self.seq, self.width
        n = self.rows * seq
        hw = HEADS * seq
        is_top, is_last = probs is None, layer == 0
        score_rows = scores[0].shape[0]
        ins = [scores[0], scores[1]]
        in_specs = [self.whole(score_rows, hw)] * 2
        if not is_top:
            ins.append(probs)
            in_specs.append(self.whole(seq, hw))
        ins += [qkv, dmix, x, gain]
        in_specs += [self.tile(3 * width), self.tile(width), self.tile(width), self.whole(1, width)]
        outs = [jax.ShapeDtypeStruct((n, 3 * width), BF16), jax.ShapeDtypeStruct((1, width), F32)]
        out_specs = [self.tile(3 * width), self.whole(1, width)]
        scratch = [pltpu.VMEM((seq, hw), BF16)] * 3
        if is_top:
            outs.append(jax.ShapeDtypeStruct((n, width), BF16))
            out_specs.append(self.tile(width))
            scratch.append(pltpu.VMEM((seq, hw), BF16))
        scratch = scratch + self.wq_scratch()
        if not is_last:
            ins += [dy, v_prev]
            in_specs += [self.tile(width), self.tile(width, 2)]
            outs += [
                jax.ShapeDtypeStruct((n, width), F32),
                jax.ShapeDtypeStruct((n, width), BF16),
                jax.ShapeDtypeStruct((n, width), BF16),
                jax.ShapeDtypeStruct((seq, hw), F32),
            ]
            out_specs += [self.tile(width)] * 3 + [self.whole(seq, hw)]
            scratch = scratch + self.wo_scratch()
        body = functools.partial(
            backward_kernel, is_top, is_last, self.layout, self.scale, seq, width
        )
        return self.call(
            body,
            f"layer_back_{layer}",
            self.info(layer, max(layer - 1, 0)),
            ins,
            in_specs,
            outs,
            out_specs,
            scratch,
            2 * n * width * width * 5,
        )


def group_swap(value, n_row, n_group):
    other = jnp.zeros_like(value)
    bit = 1
    while bit < n_group:
        if bit > 1:
            value = value + other
        other = lax.ppermute(value, "row", [(r, r ^ bit) for r in range(n_row)])
        bit *= 2
    return value, other


def gather_weights(wqkv, wout, n_section, n_row, n_group, member):
    width = wqkv.shape[0]
    part = width // n_group
    mine = jnp.concatenate(
        [
            lax.dynamic_slice_in_dim(wqkv, member * part, part, 0),
            lax.dynamic_slice_in_dim(wout, member * part, part, 0),
        ],
        axis=1,
    )
    got = {0: mine}
    for offset in sorted(range(1, n_section), key=lambda n: (n.bit_count(), n)):
        low = offset & -offset
        rest = offset ^ low
        if rest == 0:
            got[offset] = lax.ppermute(
                mine, "section", [(s, s ^ offset) for s in range(n_section)]
            )
        else:
            sends = jnp.where(member % 2 == 0, got[rest], got[low])
            perm = [
                (s * n_row + r, (s ^ (low if r % n_group % 2 == 0 else rest)) * n_row + r)
                for s in range(n_section)
                for r in range(n_row)
            ]
            got[offset] = lax.ppermute(sends, ("section", "row"), perm)
    pieces = {}
    for offset in range(1, n_section):
        have = [got[offset][None]]
        bit = 1
        while bit < n_group:
            send = have[0] if len(have) == 1 else jnp.concatenate(have, axis=0)
            have.append(lax.ppermute(send, "row", [(r, r ^ bit) for r in range(n_row)]))
            bit *= 2
        pieces[offset] = have
    return pieces


def local(tokens, embed, ln_gain, w_qkv, w_out, out_grad):
    n_section = lax.axis_size("section")
    n_row = lax.axis_size("row")
    section = lax.axis_index("section")
    place = lax.axis_index("row")
    micro, rows_here, seq = tokens.shape
    width = embed.shape[1]
    n_group = n_row // micro
    member = place % n_group
    rows = rows_here * micro
    scale = HEAD_DIM ** (-0.5) / math.sqrt(rows_here * n_row)
    gathered = gather_weights(w_qkv[0], w_out[0], n_section, n_row, n_group, member)
    same = [[m * n_group + g for m in range(micro)] for g in range(n_group)]
    exchange = functools.partial(
        lax.all_to_all,
        axis_name="row",
        split_axis=0,
        concat_axis=0,
        axis_index_groups=same,
        tiled=True,
    )
    tok = exchange(tokens).reshape(-1)
    top_grad = exchange(out_grad).reshape(rows * seq, width)
    gains = lax.all_gather(ln_gain[0], "section", axis=0, tiled=False)
    table = (jnp.arange(embed.shape[0], dtype=jnp.int32)[:, None] == tok[None, :]).astype(BF16)
    x = lax.dot_general(table, embed, TN, preferred_element_type=F32)

    chain = Chain(
        section, member, n_group, (w_qkv, w_out), gathered, seq, width, rows, scale
    )
    xs, hs, qkvs, probs, mixed = [], [], [], [], []
    scores = None
    dmix = None
    for layer in range(n_section):
        gain = gains[layer][None]
        prev = None if layer == 0 else (scores[0], scores[1], qkvs[-1])
        top = top_grad if layer == n_section - 1 else None
        outs = list(chain.forward(layer, x, gain, prev, top))
        if prev is not None:
            probs.append(outs.pop(0))
            mixed.append(outs.pop(0))
            x = outs.pop(0)
        if top is not None:
            dmix = outs.pop()
        xs.append(x)
        hs.append(outs[0])
        qkvs.append(outs[1])
        scores = group_swap(outs[2], n_row, n_group)
    probs.append(None)
    mixed.append(None)

    dy = top_grad
    ups = [None] * n_section
    dqkvs = [None] * n_section
    gain_parts = [None] * n_section
    ups[-1] = top_grad
    for layer in reversed(range(n_section)):
        v_prev = qkvs[layer - 1] if layer > 0 else None
        outs = list(
            chain.backward(
                layer, scores, probs[layer], qkvs[layer], dmix, xs[layer], gains[layer][None], dy, v_prev
            )
        )
        dqkvs[layer], gain_parts[layer] = outs[0], outs[1]
        outs = outs[2:]
        if probs[layer] is None:
            mixed[layer] = outs.pop(0)
        if layer > 0:
            dy, ups[layer - 1], dmix = outs[0], outs[1], outs[2]
            scores = group_swap(outs[3], n_row, n_group)

    def own_grads(layer):
        def run():
            g_qkv = lax.dot_general(hs[layer], dqkvs[layer], TN, preferred_element_type=F32)
            g_out = lax.dot_general(mixed[layer], ups[layer], TN, preferred_element_type=F32)
            return g_qkv.astype(BF16), g_out.astype(BF16), gain_parts[layer][0]

        return run

    g_qkv, g_out, g_gain = lax.switch(section, [own_grads(n) for n in range(n_section)])
    g_all = jnp.concatenate([g_qkv, g_out], axis=1)
    g_all = lax.psum_scatter(g_all, "row", scatter_dimension=0, tiled=True).astype(F32)
    g_gain = lax.psum_scatter(g_gain[None], "row", scatter_dimension=1, tiled=True)
    return (g_all[None, :, : 3 * width], g_all[None, :, 3 * width :], g_gain)


def solution(mesh):
    in_specs = (
        P(None, "row", None),
        P(),
        P("section", None),
        P("section", None, None),
        P("section", None, None),
        P(None, "row", None, None),
    )
    out_specs = (P("section", "row", None), P("section", "row", None), P("section", "row"))
    return jax.shard_map(local, mesh=mesh, in_specs=in_specs, out_specs=out_specs, check_vma=False)
```

```python
import functools
import math

import jax
import jax.numpy as jnp
from jax import lax
from jax.experimental import pallas as pl
from jax.experimental.pallas import tpu as pltpu
from jax.sharding import PartitionSpec as P

HEADS = 12
HEAD_DIM = 64
PACK = 2
F32 = jnp.float32
BF16 = jnp.bfloat16
VMEM_LIMIT = 48 * 1024 * 1024
NT = (((1,), (1,)), ((), ()))
TN = (((0,), (0,)), ((), ()))


def mm(a, b):
    return jnp.dot(a, b, preferred_element_type=F32)


def mm_nt(a, b):
    return lax.dot_general(a, b, NT, preferred_element_type=F32)


def head_lanes(ref, seq, head):
    width = PACK * HEAD_DIM
    first = head * width
    return jnp.concatenate(
        [ref[r * seq : (r + 1) * seq, first : first + width] for r in range(ref.shape[0] // seq)],
        axis=1,
    )


def regroup(blocks):
    return [
        jnp.concatenate([block[:, n * HEAD_DIM : (n + 1) * HEAD_DIM] for block in blocks], axis=1)
        for n in range(PACK)
    ]


def pack_rows(value, out, first, seq):
    width = PACK * HEAD_DIM
    for pair in range(value.shape[0] // seq // PACK):
        for p in range(value.shape[1] // width):
            blocks = [
                value[(pair * PACK + r) * seq : (pair * PACK + r + 1) * seq, p * width : (p + 1) * width]
                for r in range(PACK)
            ]
            for n, block in enumerate(regroup(blocks)):
                at = (first + p * PACK + n) * width
                out[pair * seq : (pair + 1) * seq, at : at + width] = block


class Weights:
    def __init__(self, choices, member, own, stages, columns, dst, sems):
        self.choices, self.member, self.own, self.stages = choices, member, own, stages
        self.columns, self.dst, self.sems = columns, dst, sems

    def each(self, act):
        @pl.when(self.choices[0] == 0)
        def _():
            act(pltpu.make_async_copy(self.own.at[0], self.dst, self.sems.at[0]))

        for stage, group in enumerate(self.stages):
            for parity in range(min(2, self.sems.shape[0])):

                @pl.when(self.choices[parity] == stage + 1)
                def _(group=group, parity=parity):
                    seen = 0
                    for ref in group:
                        rows = ref.shape[1]
                        for n in range(ref.shape[0]):
                            if seen % 2 == parity:
                                start = pl.multiple_of((self.member ^ seen) * rows, rows)
                                act(
                                    pltpu.make_async_copy(
                                        ref.at[n, :, self.columns],
                                        self.dst.at[pl.ds(start, rows)],
                                        self.sems.at[seen],
                                    )
                                )
                            seen += 1

    def start(self):
        self.each(lambda copy: copy.start())

    def wait(self):
        self.each(lambda copy: copy.wait())


def take_stages(it, layout):
    return [[next(it) for _ in range(count)] for count in layout]


def softmax_heads(la, lb, scale, keep):
    seq = la.shape[0]
    for h in range(HEADS):
        at = slice(h * seq, (h + 1) * seq)
        logits = (la[:, at] + lb[:, at]) * scale
        e = jnp.exp(logits - jnp.max(logits, axis=-1, keepdims=True))
        keep(h, e / jnp.sum(e, axis=-1, keepdims=True))


def norm_parts(x):
    centred = x - jnp.mean(x, axis=-1, keepdims=True)
    spread = jnp.mean(centred * centred, axis=-1, keepdims=True)
    rstd = lax.rsqrt(spread + 1e-05)
    return centred * rstd, rstd


def scores(ref_a, first_a, ref_b, first_b, out, out_row, seq, begin):
    parts = [
        mm_nt(head_lanes(ref_a, seq, first_a + h), head_lanes(ref_b, seq, first_b + h))
        for h in range(HEADS)
    ]
    rows = slice(out_row, out_row + seq)

    @pl.when(begin)
    def _():
        for h, part in enumerate(parts):
            out[rows, h * seq : (h + 1) * seq] = part

    @pl.when(jnp.logical_not(begin))
    def _():
        for h, part in enumerate(parts):
            out[rows, h * seq : (h + 1) * seq] += part


def mix(weights, ref_b, first_b, out, first_out, scale, seq):
    width = PACK * HEAD_DIM
    for p in range(HEADS // PACK):
        values = []
        for h in range(p * PACK, (p + 1) * PACK):
            value = mm(weights[:, h * seq : (h + 1) * seq], head_lanes(ref_b, seq, first_b + h))
            values.append((value if scale is None else value * scale).astype(BF16))
        at = first_out + p * width
        for pair in range(ref_b.shape[0] // seq):
            blocks = [value[:, pair * width : (pair + 1) * width] for value in values]
            for n, block in enumerate(regroup(blocks)):
                row = (pair * PACK + n) * seq
                out[row : row + seq, at : at + width] = block


def forward_kernel(has_prev, has_top, info, *refs, layout, scale, seq, width):
    it = iter(refs)
    if has_prev:
        la, lb, v_prev = next(it), next(it), next(it)
    x_in, gain = next(it), next(it)
    top = next(it) if has_top else None
    own_q, own_o = next(it), next(it)
    stages = take_stages(it, layout)
    if has_prev:
        probs_out, mixed_out, x_out = next(it), next(it), next(it)
    h_out, qkv_out, score_out = next(it), next(it), next(it)
    if has_top:
        dmix_out = next(it)
    wq, sem_q = next(it), next(it)
    if has_prev:
        wo, sem_o = next(it), next(it)
    if has_top:
        wt, sem_t = next(it), next(it)
    step = pl.program_id(0)
    qcols, ocols = slice(0, 3 * width), slice(3 * width, 4 * width)
    now, before = (info[0], info[1]), (info[2], info[3])
    get_q = Weights(now, info[4], own_q, stages, qcols, wq, sem_q)
    if has_prev:
        get_o = Weights(before, info[4], own_o, stages, ocols, wo, sem_o)
    if has_top:
        get_t = Weights(now, info[4], own_o, stages, ocols, wt, sem_t)

    @pl.when(step == 0)
    def _():
        if has_prev:
            get_o.start()
        get_q.start()
        if has_top:
            get_t.start()
        if has_prev:

            def keep(h, value):
                probs_out[:, h * seq : (h + 1) * seq] = value.astype(BF16)

            softmax_heads(la, lb, scale, keep)

    if has_prev:
        mix(probs_out, v_prev, 0, mixed_out, 0, None, seq)
        pl.when(step == 0)(get_o.wait)
        x = x_in[...] + mm(mixed_out[...], wo[...])
        x_out[...] = x
    else:
        x = x_in[...]
    hat, _ = norm_parts(x)
    h = (hat * gain[...]).astype(BF16)
    h_out[...] = h
    pl.when(step == 0)(get_q.wait)
    for t in range(3):
        part = mm(h_out[...], wq[:, t * width : (t + 1) * width]).astype(BF16)
        pack_rows(part, qkv_out, t * HEADS, seq)
    begin = step == 0
    scores(qkv_out, 0, qkv_out, HEADS, score_out, 0, seq, begin)
    if has_top:
        pl.when(step == 0)(get_t.wait)
        pack_rows(mm_nt(top[...], wt[...]).astype(BF16), dmix_out, 0, seq)
        scores(dmix_out, 0, qkv_out, 2 * HEADS, score_out, seq, seq, begin)


def backward_kernel(is_top, is_last, info, *refs, layout, scale, seq, width):
    it = iter(refs)
    sa, sb = next(it), next(it)
    if not is_top:
        probs = next(it)
    qkv, dmix = next(it), next(it)
    if not is_last:
        x_in, gain, dy, v_prev = next(it), next(it), next(it), next(it)
    own_q, own_o = next(it), next(it)
    stages = take_stages(it, layout)
    dqkv_out = next(it)
    if is_top:
        mixed_out = next(it)
    if not is_last:
        gain_out = next(it)
        dy_out, dyb_out, dmix_out, score_out = next(it), next(it), next(it), next(it)
    dl, dlt, pt = next(it), next(it), next(it)
    if is_top:
        probs = next(it)
    step = pl.program_id(0)
    if not is_last:
        wq, sem_q, wo, sem_o = next(it), next(it), next(it), next(it)
        qcols, ocols = slice(0, 3 * width), slice(3 * width, 4 * width)
        get_q = Weights((info[0], info[1]), info[4], own_q, stages, qcols, wq, sem_q)
        get_o = Weights((info[2], info[3]), info[4], own_o, stages, ocols, wo, sem_o)

    @pl.when(step == 0)
    def _():
        if not is_last:
            get_q.start()
            get_o.start()
        if is_top:

            def keep(h, value):
                probs[:, h * seq : (h + 1) * seq] = value.astype(BF16)

            softmax_heads(sa.at[0:seq], sb.at[0:seq], scale, keep)
        first = seq if is_top else 0
        for h in range(HEADS):
            at = slice(h * seq, (h + 1) * seq)
            prob = probs[:, at].astype(F32)
            d_prob = sa[first : first + seq, at] + sb[first : first + seq, at]
            d_logit = prob * (d_prob - jnp.sum(d_prob * prob, axis=-1, keepdims=True))
            dl[:, at] = d_logit.astype(BF16)
            dlt[:, at] = jnp.transpose(d_logit).astype(BF16)
            pt[:, at] = jnp.transpose(prob).astype(BF16)

    if is_top:
        mix(probs, qkv, 2 * HEADS, mixed_out, 0, None, seq)
    mix(dl, qkv, HEADS, dqkv_out, 0, scale, seq)
    mix(dlt, qkv, 0, dqkv_out, width, scale, seq)
    mix(pt, dmix, 0, dqkv_out, 2 * width, None, seq)
    if not is_last:
        pl.when(step == 0)(get_q.wait)
        d_h = mm_nt(dqkv_out[...], wq[...]).astype(BF16).astype(F32)
        hat, rstd = norm_parts(x_in[...])
        add_gain(gain_out, d_h, hat, step)
        d_hat = d_h * gain[...]
        mean_d = jnp.mean(d_hat, axis=-1, keepdims=True)
        mean_dh = jnp.mean(d_hat * hat, axis=-1, keepdims=True)
        d_x = dy[...].astype(F32) + rstd * (d_hat - mean_d - hat * mean_dh)
        dy_out[...] = d_x
        dyb_out[...] = d_x.astype(BF16)
        pl.when(step == 0)(get_o.wait)
        pack_rows(mm_nt(dyb_out[...], wo[...]).astype(BF16), dmix_out, 0, seq)
        scores(dmix_out, 0, v_prev, 0, score_out, 0, seq, step == 0)


def add_gain(gain_out, d_h, hat, step):
    part = jnp.sum(d_h * hat, axis=0, keepdims=True)

    @pl.when(step == 0)
    def _():
        gain_out[...] = part

    @pl.when(step > 0)
    def _():
        gain_out[...] += part


def gain_kernel(info, *refs, layout, width):
    it = iter(refs)
    dqkv, x_in, own_q, _ = next(it), next(it), next(it), next(it)
    stages = take_stages(it, layout)
    gain_out, wq, sem_q = next(it), next(it), next(it)
    step = pl.program_id(0)
    get_q = Weights(
        (info[0], info[1]), info[4], own_q, stages, slice(0, 3 * width), wq, sem_q
    )
    pl.when(step == 0)(get_q.start)
    hat, _ = norm_parts(x_in[...])
    pl.when(step == 0)(get_q.wait)
    d_h = mm_nt(dqkv[...], wq[...]).astype(BF16).astype(F32)
    add_gain(gain_out, d_h, hat, step)


class Chain:
    def __init__(self, fetched, member, n_group, own, seq, width, rows, scale):
        self.fetched, self.member, self.n_group = fetched, member, n_group
        self.own, self.seq, self.width, self.rows = own, seq, width, rows
        self.scale = scale
        per_step = 4 if rows % 4 == 0 else 2
        self.chunk = per_step * seq
        self.steps = rows // per_step

    def info(self, now, other):
        picks = self.fetched.choices(now) + self.fetched.choices(other) + [self.member]
        return jnp.stack(picks).astype(jnp.int32)

    def whole(self, rows, lanes):
        return pl.BlockSpec((rows, lanes), lambda i, s: (0, 0))

    def tile(self, lanes, column=0, part=1):
        return pl.BlockSpec((self.chunk // part, lanes), lambda i, s: (i, column))

    def packed(self, heads, column=0):
        return self.tile(heads * PACK * HEAD_DIM, column, PACK)

    def call(self, make_body, name, info, stages, ins, in_specs, outs, out_specs, scratch, flops):
        size = sum(math.prod(o.shape) * o.dtype.itemsize for o in outs)
        size += sum(math.prod(a.shape) * a.dtype.itemsize for a in ins)
        any_spec = pl.BlockSpec(memory_space=pl.ANY)
        groups = self.fetched.stages[:stages]
        weights = [*self.own] + [a for group in groups for a in group]
        return pl.pallas_call(
            make_body(layout=tuple(len(group) for group in groups)),
            name=name,
            out_shape=outs,
            grid_spec=pltpu.PrefetchScalarGridSpec(
                num_scalar_prefetch=1,
                grid=(self.steps,),
                in_specs=in_specs + [any_spec] * len(weights),
                out_specs=out_specs,
                scratch_shapes=scratch,
            ),
            compiler_params=pltpu.CompilerParams(
                dimension_semantics=("arbitrary",), vmem_limit_bytes=VMEM_LIMIT
            ),
            cost_estimate=pl.CostEstimate(flops=flops, bytes_accessed=size, transcendentals=0),
        )(info, *ins, *weights)

    def weight_scratch(self, columns):
        return [
            pltpu.VMEM((self.width, columns * self.width), BF16),
            pltpu.SemaphoreType.DMA((self.n_group,)),
        ]

    def forward(self, layer, x, gain, prev, top):
        seq, width = self.seq, self.width
        n = self.rows * seq
        hw = HEADS * seq
        ins, in_specs, outs, out_specs = [], [], [], []
        if prev is not None:
            ins += [prev[0], prev[1], prev[2]]
            in_specs += [self.whole(seq, hw), self.whole(seq, hw), self.packed(HEADS, 2)]
            outs += [
                jax.ShapeDtypeStruct((seq, hw), BF16),
                jax.ShapeDtypeStruct((n, width), BF16),
                jax.ShapeDtypeStruct((n, width), F32),
            ]
            out_specs += [self.whole(seq, hw), self.tile(width), self.tile(width)]
        ins += [x, gain]
        in_specs += [self.tile(width), self.whole(1, width)]
        score_rows = seq
        if top is not None:
            ins.append(top)
            in_specs.append(self.tile(width))
            score_rows = 2 * seq
        outs += [
            jax.ShapeDtypeStruct((n, width), BF16),
            jax.ShapeDtypeStruct((n // PACK, 3 * PACK * width), BF16),
            jax.ShapeDtypeStruct((score_rows, hw), F32),
        ]
        out_specs += [self.tile(width), self.packed(3 * HEADS), self.whole(score_rows, hw)]
        scratch = self.weight_scratch(3)
        if prev is not None:
            scratch += self.weight_scratch(1)
        if top is not None:
            outs.append(jax.ShapeDtypeStruct((n // PACK, PACK * width), BF16))
            out_specs.append(self.packed(HEADS))
            scratch += self.weight_scratch(1)
        body = functools.partial(
            functools.partial,
            forward_kernel,
            prev is not None,
            top is not None,
            scale=self.scale,
            seq=seq,
            width=width,
        )
        return self.call(
            body,
            f"layer_in_{layer}",
            self.info(layer, max(layer - 1, 0)),
            self.fetched.first_stages if layer == 0 else None,
            ins,
            in_specs,
            outs,
            out_specs,
            scratch,
            2 * n * width * width * 5,
        )

    def backward(self, layer, scores, probs, qkv, dmix, x, gain, dy, v_prev):
        seq, width = self.seq, self.width
        n = self.rows * seq
        hw = HEADS * seq
        is_top, is_last = probs is None, layer == 0
        score_rows = scores[0].shape[0]
        ins = [scores[0], scores[1]]
        in_specs = [self.whole(score_rows, hw)] * 2
        if not is_top:
            ins.append(probs)
            in_specs.append(self.whole(seq, hw))
        ins += [qkv, dmix]
        in_specs += [self.packed(3 * HEADS), self.packed(HEADS)]
        outs = [jax.ShapeDtypeStruct((n, 3 * width), BF16)]
        out_specs = [self.tile(3 * width)]
        scratch = [pltpu.VMEM((seq, hw), BF16)] * 3
        if is_top:
            outs.append(jax.ShapeDtypeStruct((n, width), BF16))
            out_specs.append(self.tile(width))
            scratch.append(pltpu.VMEM((seq, hw), BF16))
        if not is_last:
            ins += [x, gain, dy, v_prev]
            in_specs += [self.tile(width), self.whole(1, width)]
            in_specs += [self.tile(width), self.packed(HEADS, 2)]
            outs += [
                jax.ShapeDtypeStruct((1, width), F32),
                jax.ShapeDtypeStruct((n, width), F32),
                jax.ShapeDtypeStruct((n, width), BF16),
                jax.ShapeDtypeStruct((n // PACK, PACK * width), BF16),
                jax.ShapeDtypeStruct((seq, hw), F32),
            ]
            out_specs += [self.whole(1, width)] + [self.tile(width)] * 2
            out_specs += [self.packed(HEADS), self.whole(seq, hw)]
            scratch = scratch + self.weight_scratch(3) + self.weight_scratch(1)
        body = functools.partial(
            functools.partial,
            backward_kernel,
            is_top,
            is_last,
            scale=self.scale,
            seq=seq,
            width=width,
        )
        return self.call(
            body,
            f"layer_back_{layer}",
            self.info(layer, max(layer - 1, 0)),
            0 if is_last else None,
            ins,
            in_specs,
            outs,
            out_specs,
            scratch,
            2 * n * width * width * 5,
        )

    def gain_grad(self, layer, dqkv, x):
        width = self.width
        n = self.rows * self.seq
        return self.call(
            functools.partial(functools.partial, gain_kernel, width=width),
            f"gain_back_{layer}",
            self.info(layer, layer),
            None,
            [dqkv, x],
            [self.tile(3 * width), self.tile(width)],
            [jax.ShapeDtypeStruct((1, width), F32)],
            [self.whole(1, width)],
            self.weight_scratch(3),
            2 * n * width * width * 3,
        )[0]


def group_swap(value, n_row, n_group):
    other = jnp.zeros_like(value)
    bit = 1
    while bit < n_group:
        if bit > 1:
            value = value + other
        other = lax.ppermute(value, "row", [(r, r ^ bit) for r in range(n_row)])
        bit *= 2
    return value, other


class Fetched:
    first_stages = 2

    def __init__(self, wqkv, wout, section, n_section, n_row, n_group, member):
        assert n_section == 4
        self.section, self.n_row, self.n_group, self.member = section, n_row, n_group, member
        self.last = n_section - 1
        part = wqkv.shape[0] // n_group
        self.mine = jnp.concatenate(
            [
                lax.dynamic_slice_in_dim(wqkv, member * part, part, 0),
                lax.dynamic_slice_in_dim(wout, member * part, part, 0),
            ],
            axis=1,
        )
        even = member % 2 == 0
        self.to_last = section == (self.last ^ jnp.where(even, 2, 1))
        self.got = self.hop(self.mine, 1)
        self.stages = [self.share(self.got)]

    def hop(self, value, even_bit):
        perm = [
            (s * self.n_row + r, (s ^ (even_bit if r % 2 == 0 else 3 - even_bit)) * self.n_row + r)
            for s in range(self.last + 1)
            for r in range(self.n_row)
        ]
        return lax.ppermute(value, ("section", "row"), perm)

    def finish(self, *ready):
        second, *ready = lax.optimization_barrier(
            (jnp.where(self.to_last, self.got, self.mine), *ready)
        )
        second = self.hop(second, 2)
        third, second = lax.optimization_barrier(
            (jnp.where(self.to_last, self.mine, self.got), second)
        )
        third = self.hop(third, 2)
        self.stages += [self.share(second), self.share(third)]
        return ready

    def share(self, value):
        have = [value[None]]
        bit = 1
        while bit < self.n_group:
            send = have[0] if len(have) == 1 else jnp.concatenate(have, axis=0)
            have.append(lax.ppermute(send, "row", [(r, r ^ bit) for r in range(self.n_row)]))
            bit *= 2
        return have

    def choices(self, layer):
        offset = self.section ^ layer
        at_last = self.section == self.last
        picks = []
        for parity in (self.member % 2, 1 - self.member % 2):
            first = jnp.where(parity == 0, 1, 2)
            second = jnp.where(at_last, 3, 3 - first)
            pick = jnp.where(offset == first, 1, jnp.where(offset == second, 2, 3))
            picks.append(jnp.where(offset == 0, 0, pick))
        return picks


def local(tokens, embed, ln_gain, w_qkv, w_out, out_grad):
    n_section = lax.axis_size("section")
    n_row = lax.axis_size("row")
    section = lax.axis_index("section")
    place = lax.axis_index("row")
    micro, rows_here, seq = tokens.shape
    width = embed.shape[1]
    n_group = n_row // micro
    member = place % n_group
    rows = rows_here * micro
    scale = HEAD_DIM ** (-0.5) / math.sqrt(rows_here * n_row)
    fetched = Fetched(w_qkv[0], w_out[0], section, n_section, n_row, n_group, member)
    same = [[m * n_group + g for m in range(micro)] for g in range(n_group)]
    exchange = functools.partial(
        lax.all_to_all,
        axis_name="row",
        split_axis=0,
        concat_axis=0,
        axis_index_groups=same,
        tiled=True,
    )
    tok = exchange(tokens).reshape(-1)
    top_grad = exchange(out_grad).reshape(rows * seq, width)
    gains = lax.all_gather(ln_gain[0], "section", axis=0, tiled=False)
    table = (jnp.arange(embed.shape[0], dtype=jnp.int32)[:, None] == tok[None, :]).astype(BF16)
    x = lax.dot_general(table, embed, TN, preferred_element_type=F32)

    x, gains = fetched.finish(x, gains)
    chain = Chain(fetched, member, n_group, (w_qkv, w_out), seq, width, rows, scale)
    xs, hs, qkvs, probs, mixed = [], [], [], [], []
    scores = None
    dmix = None
    for layer in range(n_section):
        gain = gains[layer][None]
        prev = None if layer == 0 else (scores[0], scores[1], qkvs[-1])
        top = top_grad if layer == n_section - 1 else None
        outs = list(chain.forward(layer, x, gain, prev, top))
        if prev is not None:
            probs.append(outs.pop(0))
            mixed.append(outs.pop(0))
            x = outs.pop(0)
        if top is not None:
            dmix = outs.pop()
        xs.append(x)
        hs.append(outs[0])
        qkvs.append(outs[1])
        scores = group_swap(outs[2], n_row, n_group)
    probs.append(None)
    mixed.append(None)

    dy = top_grad
    ups = [None] * n_section
    dqkvs = [None] * n_section
    gain_parts = [None] * n_section
    ups[-1] = top_grad
    for layer in reversed(range(n_section)):
        v_prev = qkvs[layer - 1] if layer > 0 else None
        outs = list(
            chain.backward(
                layer, scores, probs[layer], qkvs[layer], dmix, xs[layer], gains[layer][None], dy, v_prev
            )
        )
        dqkvs[layer] = outs.pop(0)
        if probs[layer] is None:
            mixed[layer] = outs.pop(0)
        if layer > 0:
            gain_parts[layer], dy, ups[layer - 1], dmix, part = outs
            scores = group_swap(part, n_row, n_group)

    def own_grads(layer):
        def run():
            g_qkv = lax.dot_general(hs[layer], dqkvs[layer], TN, preferred_element_type=F32)
            g_out = lax.dot_general(mixed[layer], ups[layer], TN, preferred_element_type=F32)
            return jnp.concatenate([g_qkv.astype(BF16), g_out.astype(BF16)], axis=1)

        return run

    g_all = lax.switch(section, [own_grads(n) for n in range(n_section)])
    g_all = lax.psum_scatter(g_all, "row", scatter_dimension=0, tiled=True).astype(F32)
    gain_parts[0] = chain.gain_grad(0, dqkvs[0], xs[0])
    g_gain = lax.select_n(section, *gain_parts)
    bit = 1
    while bit < n_row:
        g_gain = g_gain + lax.ppermute(g_gain, "row", [(r, r ^ bit) for r in range(n_row)])
        bit *= 2
    g_gain = lax.dynamic_slice_in_dim(g_gain, place * (width // n_row), width // n_row, 1)
    return (g_all[None, :, : 3 * width], g_all[None, :, 3 * width :], g_gain)


def solution(mesh):
    in_specs = (
        P(None, "row", None),
        P(),
        P("section", None),
        P("section", None, None),
        P("section", None, None),
        P(None, "row", None, None),
    )
    out_specs = (P("section", "row", None), P("section", "row", None), P("section", "row"))
    return jax.shard_map(local, mesh=mesh, in_specs=in_specs, out_specs=out_specs, check_vma=False)
```

```python
import functools
import math

import jax
import jax.numpy as jnp
from jax import lax
from jax.experimental import pallas as pl
from jax.experimental.pallas import tpu as pltpu
from jax.sharding import PartitionSpec as P

HEADS = 12
HEAD_DIM = 64
PACK = 2
BLOCKS = 3
DIRECT, ACROSS, FULL = range(3)
F32 = jnp.float32
BF16 = jnp.bfloat16
VMEM_LIMIT = 60 * 1024 * 1024
NT = (((1,), (1,)), ((), ()))
TN = (((0,), (0,)), ((), ()))


def mm(a, b):
    return jnp.dot(a, b, preferred_element_type=F32)


def mm_nt(a, b):
    return lax.dot_general(a, b, NT, preferred_element_type=F32)


def head_lanes(ref, seq, head):
    width = PACK * HEAD_DIM
    first = head * width
    return jnp.concatenate(
        [ref[r * seq : (r + 1) * seq, first : first + width] for r in range(ref.shape[0] // seq)],
        axis=1,
    )


def regroup(blocks):
    return [
        jnp.concatenate([block[:, n * HEAD_DIM : (n + 1) * HEAD_DIM] for block in blocks], axis=1)
        for n in range(PACK)
    ]


def pack_rows(value, out, first, seq):
    width = PACK * HEAD_DIM
    for pair in range(value.shape[0] // seq // PACK):
        for p in range(value.shape[1] // width):
            blocks = [
                value[(pair * PACK + r) * seq : (pair * PACK + r + 1) * seq, p * width : (p + 1) * width]
                for r in range(PACK)
            ]
            for n, block in enumerate(regroup(blocks)):
                at = (first + p * PACK + n) * width
                out[pair * seq : (pair + 1) * seq, at : at + width] = block


class Weights:
    def __init__(self, info, first, own, stages, columns, dst, sems):
        self.choices = (info[first], info[first + 1])
        self.member, self.half = info[4], info[5]
        self.own, self.stages = own, stages
        self.columns, self.dst, self.sems = columns, dst, sems

    def each(self, act):
        @pl.when(self.choices[0] == 0)
        def _():
            act(pltpu.make_async_copy(self.own.at[0], self.dst, self.sems.at[0]))

        for stage, group in enumerate(self.stages):
            for parity in range(2):

                @pl.when(self.choices[parity] == stage + 1)
                def _(group=group, parity=parity):
                    for kind, refs in group:
                        self.shares(kind, refs, parity, act)

    def shares(self, kind, refs, parity, act):
        group = self.sems.shape[0] // BLOCKS
        block = self.dst.shape[0] // group // BLOCKS
        places = {DIRECT: (self.half, 2), ACROSS: (1 - self.half,), FULL: (0, 1, 2)}[kind]
        sems = {DIRECT: (0, 1), ACROSS: (2,), FULL: (0, 1, 2)}[kind]
        seen = 0
        for ref in refs:
            for n in range(ref.shape[0]):
                if seen % 2 == parity:
                    base = (self.member ^ seen) * BLOCKS
                    for j, place in enumerate(places):
                        start = pl.multiple_of((base + place) * block, block)
                        act(
                            pltpu.make_async_copy(
                                ref.at[n, j * block : (j + 1) * block, self.columns],
                                self.dst.at[pl.ds(start, block)],
                                self.sems.at[seen * BLOCKS + sems[j]],
                            )
                        )
                seen += 1

    def start(self):
        self.each(lambda copy: copy.start())

    def wait(self):
        self.each(lambda copy: copy.wait())


def take_stages(it, layout):
    return [[(kind, [next(it) for _ in range(count)]) for kind, count in group] for group in layout]


def softmax_heads(la, lb, scale, keep):
    seq = la.shape[0]
    for h in range(HEADS):
        at = slice(h * seq, (h + 1) * seq)
        logits = (la[:, at] + lb[:, at]) * scale
        e = jnp.exp(logits - jnp.max(logits, axis=-1, keepdims=True))
        keep(h, e / jnp.sum(e, axis=-1, keepdims=True))


def norm_parts(x):
    centred = x - jnp.mean(x, axis=-1, keepdims=True)
    spread = jnp.mean(centred * centred, axis=-1, keepdims=True)
    rstd = lax.rsqrt(spread + 1e-05)
    return centred * rstd, rstd


def scores(ref_a, first_a, ref_b, first_b, out, out_row, seq, begin):
    parts = [
        mm_nt(head_lanes(ref_a, seq, first_a + h), head_lanes(ref_b, seq, first_b + h))
        for h in range(HEADS)
    ]
    rows = slice(out_row, out_row + seq)

    @pl.when(begin)
    def _():
        for h, part in enumerate(parts):
            out[rows, h * seq : (h + 1) * seq] = part

    @pl.when(jnp.logical_not(begin))
    def _():
        for h, part in enumerate(parts):
            out[rows, h * seq : (h + 1) * seq] += part


def mix(weights, ref_b, first_b, out, first_out, scale, seq):
    width = PACK * HEAD_DIM
    for p in range(HEADS // PACK):
        values = []
        for h in range(p * PACK, (p + 1) * PACK):
            value = mm(weights[:, h * seq : (h + 1) * seq], head_lanes(ref_b, seq, first_b + h))
            values.append((value if scale is None else value * scale).astype(BF16))
        at = first_out + p * width
        for pair in range(ref_b.shape[0] // seq):
            blocks = [value[:, pair * width : (pair + 1) * width] for value in values]
            for n, block in enumerate(regroup(blocks)):
                row = (pair * PACK + n) * seq
                out[row : row + seq, at : at + width] = block


def forward_kernel(has_prev, has_top, info, *refs, layout, scale, seq, width):
    it = iter(refs)
    if has_prev:
        la, lb, v_prev = next(it), next(it), next(it)
    x_in, gain = next(it), next(it)
    top = next(it) if has_top else None
    own_q, own_o = next(it), next(it)
    stages = take_stages(it, layout)
    if has_prev:
        probs_out, x_out = next(it), next(it)
    qkv_out, score_out = next(it), next(it)
    if has_top:
        dmix_out = next(it)
    wq, sem_q = next(it), next(it)
    if has_prev:
        wo, sem_o, mixed = next(it), next(it), next(it)
    if has_top:
        wt, sem_t = next(it), next(it)
    step = pl.program_id(0)
    qcols, ocols = slice(0, 3 * width), slice(3 * width, 4 * width)
    get_q = Weights(info, 0, own_q, stages, qcols, wq, sem_q)
    if has_prev:
        get_o = Weights(info, 2, own_o, stages, ocols, wo, sem_o)
    if has_top:
        get_t = Weights(info, 0, own_o, stages, ocols, wt, sem_t)

    @pl.when(step == 0)
    def _():
        if has_prev:
            get_o.start()
        get_q.start()
        if has_top:
            get_t.start()
        if has_prev:

            def keep(h, value):
                probs_out[:, h * seq : (h + 1) * seq] = value.astype(BF16)

            softmax_heads(la, lb, scale, keep)

    if has_prev:
        mix(probs_out, v_prev, 0, mixed, 0, None, seq)
        pl.when(step == 0)(get_o.wait)
        x = x_in[...] + mm(mixed[...], wo[...])
        x_out[...] = x
    else:
        x = x_in[...]
    hat, _ = norm_parts(x)
    h = (hat * gain[...]).astype(BF16)
    pl.when(step == 0)(get_q.wait)
    pack_rows(mm(h, wq[...]).astype(BF16), qkv_out, 0, seq)
    begin = step == 0
    scores(qkv_out, 0, qkv_out, HEADS, score_out, 0, seq, begin)
    if has_top:
        pl.when(step == 0)(get_t.wait)
        pack_rows(mm_nt(top[...], wt[...]).astype(BF16), dmix_out, 0, seq)
        scores(dmix_out, 0, qkv_out, 2 * HEADS, score_out, seq, seq, begin)


def add_gain(gain_out, d_h, hat, step):
    part = jnp.sum(d_h * hat, axis=0, keepdims=True)

    @pl.when(step == 0)
    def _():
        gain_out[...] = part

    @pl.when(step > 0)
    def _():
        gain_out[...] += part


def add_product(a, b, total, column, step, steps, staged):
    at = slice(column, column + b.shape[1])
    part = lax.dot_general(a, b, TN, preferred_element_type=F32)

    @pl.when(step == 0)
    def _():
        total[:, at] = part

    @pl.when((step > 0) & (step < steps - 1))
    def _():
        total[:, at] += part

    @pl.when(step == steps - 1)
    def _():
        staged[:, at] = ((total[:, at] if steps > 1 else 0.0) + part).astype(BF16)


def logit_grads(probs, sa, sb, first, seq, dl, dlt):
    for h in range(HEADS):
        at = slice(h * seq, (h + 1) * seq)
        prob = probs[:, at].astype(F32)
        d_prob = sa[first : first + seq, at] + sb[first : first + seq, at]
        d_logit = prob * (d_prob - jnp.sum(d_prob * prob, axis=-1, keepdims=True))
        dl[:, at] = d_logit.astype(BF16)
        dlt[:, at] = jnp.transpose(d_logit).astype(BF16)


def turn_probs(probs, seq, pt):
    for h in range(HEADS):
        at = slice(h * seq, (h + 1) * seq)
        pt[:, at] = jnp.transpose(probs[:, at].astype(F32)).astype(BF16)


def backward_kernel(is_top, info, *refs, layout, scale, seq, width, steps):
    it = iter(refs)
    sa, sb = next(it), next(it)
    if not is_top:
        probs = next(it)
    qkv, dmix, x_in, gain, dy, v_prev = [next(it) for _ in range(6)]
    if not is_top:
        next(it), next(it)
    own_q, own_o = next(it), next(it)
    stages = take_stages(it, layout)
    gain_out, dy_out, dmix_out, score_out = [next(it) for _ in range(4)]
    grad_a, grad_b = next(it), next(it)
    dl, dlt, pt, dqkv, mixed = [next(it) for _ in range(5)]
    total_a, total_b, staged_a, staged_b, sem_g = [next(it) for _ in range(5)]
    wq, sem_q, wo, sem_o = [next(it) for _ in range(4)]
    if is_top:
        probs = next(it)
    step = pl.program_id(0)
    get_q = Weights(info, 0, own_q, stages, slice(0, 3 * width), wq, sem_q)
    get_o = Weights(info, 2, own_o, stages, slice(3 * width, 4 * width), wo, sem_o)
    own = info[0] == 0

    @pl.when(step == 0)
    def _():
        get_q.start()
        get_o.start()
        if is_top:

            def keep(h, value):
                probs[:, h * seq : (h + 1) * seq] = value.astype(BF16)

            softmax_heads(sa.at[0:seq], sb.at[0:seq], scale, keep)
        logit_grads(probs, sa, sb, seq if is_top else 0, seq, dl, dlt)
        turn_probs(probs, seq, pt)

    mix(dl, qkv, HEADS, dqkv, 0, scale, seq)
    mix(dlt, qkv, 0, dqkv, width, scale, seq)
    mix(pt, dmix, 0, dqkv, 2 * width, None, seq)
    pl.when(step == 0)(get_q.wait)
    d_h = mm_nt(dqkv[...], wq[...]).astype(BF16).astype(F32)
    hat, rstd = norm_parts(x_in[...])
    add_gain(gain_out, d_h, hat, step)
    d_hat = d_h * gain[...]
    mean_d = jnp.mean(d_hat, axis=-1, keepdims=True)
    mean_dh = jnp.mean(d_hat * hat, axis=-1, keepdims=True)
    d_x = dy[...].astype(F32) + rstd * (d_hat - mean_d - hat * mean_dh)
    dy_out[...] = d_x
    pl.when(step == 0)(get_o.wait)
    pack_rows(mm_nt(d_x.astype(BF16), wo[...]).astype(BF16), dmix_out, 0, seq)
    scores(dmix_out, 0, v_prev, 0, score_out, 0, seq, step == 0)

    @pl.when(own)
    def _():
        mix(probs, qkv, 2 * HEADS, mixed, 0, None, seq)
        h = (norm_parts(x_in[...])[0] * gain[...]).astype(BF16)
        add_product(mixed[...], dy[...].astype(BF16), total_a, 0, step, steps, staged_a)
        add_product(h, dqkv[:, 2 * width :], total_a, width, step, steps, staged_a)
        add_product(h, dqkv[:, : 2 * width], total_b, 0, step, steps, staged_b)

    @pl.when(own & (step == steps - 1))
    def _():
        copies = [
            pltpu.make_async_copy(staged_a, grad_a, sem_g.at[0]),
            pltpu.make_async_copy(staged_b, grad_b, sem_g.at[1]),
        ]
        for copy in copies:
            copy.start()
        for copy in copies:
            copy.wait()


def early_kernel(info, *refs, layout, seq, width, steps):
    probs, v, dmix, x_in, gain, dy, _, dv_out, grad_a, pt, mixed, total, staged, sem = refs
    step = pl.program_id(0)
    own = info[0] == 0

    @pl.when(own)
    def _():
        @pl.when(step == 0)
        def _():
            turn_probs(probs, seq, pt)

        mix(probs, v, 0, mixed, 0, None, seq)
        mix(pt, dmix, 0, dv_out, 0, None, seq)
        h = (norm_parts(x_in[...])[0] * gain[...]).astype(BF16)
        add_product(mixed[...], dy[...].astype(BF16), total, 0, step, steps, staged)
        add_product(h, dv_out[...], total, width, step, steps, staged)

    @pl.when(own & (step == steps - 1))
    def _():
        copy = pltpu.make_async_copy(staged, grad_a, sem.at[0])
        copy.start()
        copy.wait()


def late_kernel(info, *refs, layout, scale, seq, width, steps):
    sa, sb, probs, qk, x_in, gain, _, dqk_out, grad_b, dl, dlt, total, staged, sem = refs
    step = pl.program_id(0)
    own = info[0] == 0

    @pl.when(own)
    def _():
        @pl.when(step == 0)
        def _():
            logit_grads(probs, sa, sb, 0, seq, dl, dlt)

        h = (norm_parts(x_in[...])[0] * gain[...]).astype(BF16)
        mix(dl, qk, HEADS, dqk_out, 0, scale, seq)
        mix(dlt, qk, 0, dqk_out, width, scale, seq)
        add_product(h, dqk_out[...], total, 0, step, steps, staged)

    @pl.when(own & (step == steps - 1))
    def _():
        copy = pltpu.make_async_copy(staged, grad_b, sem.at[0])
        copy.start()
        copy.wait()


def gain_kernel(info, *refs, layout, width):
    dqk, dv, x_in, own_q, gain_out, wq, sem = refs
    step = pl.program_id(0)

    @pl.when(info[0] == 0)
    def _():
        @pl.when(step == 0)
        def _():
            copy = pltpu.make_async_copy(own_q.at[0], wq, sem.at[0])
            copy.start()
            copy.wait()

        hat, _ = norm_parts(x_in[...])
        d_h = mm_nt(dqk[...], wq[:, : 2 * width]) + mm_nt(dv[...], wq[:, 2 * width :])
        add_gain(gain_out, d_h.astype(BF16).astype(F32), hat, step)


class Chain:
    def __init__(self, fetched, member, n_group, own, seq, width, rows, scale):
        self.fetched, self.member, self.n_group = fetched, member, n_group
        self.own, self.seq, self.width, self.rows = own, seq, width, rows
        self.scale = scale
        per_step = 4 if rows % 4 == 0 else 2
        self.chunk = per_step * seq
        self.steps = rows // per_step

    def info(self, now, other):
        picks = self.fetched.choices(now) + self.fetched.choices(other)
        return jnp.stack(picks + [self.member, self.fetched.half]).astype(jnp.int32)

    def whole(self, rows, lanes):
        return pl.BlockSpec((rows, lanes), lambda i, s: (0, 0))

    def tile(self, lanes, column=0, part=1):
        return pl.BlockSpec((self.chunk // part, lanes), lambda i, s: (i, column))

    def packed(self, heads, column=0):
        return self.tile(heads * PACK * HEAD_DIM, column, PACK)

    def call(self, body, name, info, stages, ins, outs, scratch, flops, carried=(), own=None):
        any_spec = pl.BlockSpec(memory_space=pl.ANY)
        groups = self.fetched.stages[:stages]
        weights = list(self.own if own is None else own)
        weights += [a for group in groups for _, arrays in group for a in arrays]
        arrays = [a for a, _ in ins] + list(carried)
        shapes = [o for o, _ in outs]
        size = sum(math.prod(a.shape) * a.dtype.itemsize for a in arrays + shapes)
        aliases = {
            1 + len(ins) + n: len(outs) - len(carried) + n for n in range(len(carried))
        }
        layout = tuple(tuple((kind, len(arrays)) for kind, arrays in group) for group in groups)
        return pl.pallas_call(
            functools.partial(body, layout=layout),
            name=name,
            out_shape=shapes,
            grid_spec=pltpu.PrefetchScalarGridSpec(
                num_scalar_prefetch=1,
                grid=(self.steps,),
                in_specs=[spec for _, spec in ins] + [any_spec] * (len(carried) + len(weights)),
                out_specs=[spec for _, spec in outs],
                scratch_shapes=scratch,
            ),
            input_output_aliases=aliases,
            compiler_params=pltpu.CompilerParams(
                dimension_semantics=("arbitrary",), vmem_limit_bytes=VMEM_LIMIT
            ),
            cost_estimate=pl.CostEstimate(flops=flops, bytes_accessed=size, transcendentals=0),
        )(info, *arrays, *weights)

    def weight_scratch(self, columns):
        return [
            pltpu.VMEM((self.width, columns * self.width), BF16),
            pltpu.SemaphoreType.DMA((self.n_group * BLOCKS,)),
        ]

    def shape(self, rows, lanes, dtype):
        return jax.ShapeDtypeStruct((rows, lanes), dtype)

    def grad_out(self):
        any_spec = pl.BlockSpec(memory_space=pl.ANY)
        return (self.shape(self.width, 2 * self.width, BF16), any_spec)

    def grad_scratch(self, copies):
        shape = (self.width, 2 * self.width)
        scratch = [pltpu.VMEM(shape, F32)] * copies + [pltpu.VMEM(shape, BF16)] * copies
        return scratch + [pltpu.SemaphoreType.DMA((copies,))]

    def forward(self, layer, x, gain, prev, top):
        seq, width = self.seq, self.width
        n = self.rows * seq
        hw = HEADS * seq
        score_rows = seq if top is None else 2 * seq
        ins = [(x, self.tile(width)), (gain, self.whole(1, width))]
        outs = [
            (self.shape(n // PACK, 3 * PACK * width, BF16), self.packed(3 * HEADS)),
            (self.shape(score_rows, hw, F32), self.whole(score_rows, hw)),
        ]
        scratch = self.weight_scratch(3)
        if prev is not None:
            ins = [
                (prev[0], self.whole(seq, hw)),
                (prev[1], self.whole(seq, hw)),
                (prev[2], self.packed(HEADS, 2)),
            ] + ins
            outs = [
                (self.shape(seq, hw, BF16), self.whole(seq, hw)),
                (self.shape(n, width, F32), self.tile(width)),
            ] + outs
            scratch += self.weight_scratch(1) + [pltpu.VMEM((self.chunk, width), BF16)]
        if top is not None:
            ins.append((top, self.tile(width)))
            outs.append((self.shape(n // PACK, PACK * width, BF16), self.packed(HEADS)))
            scratch += self.weight_scratch(1)
        body = functools.partial(
            forward_kernel, prev is not None, top is not None, scale=self.scale, seq=seq, width=width
        )
        return self.call(
            body,
            f"layer_in_{layer}",
            self.info(layer, max(layer - 1, 0)),
            self.fetched.first_stages if layer == 0 else None,
            ins,
            outs,
            scratch,
            2 * n * width * width * 5,
        )

    def backward(self, layer, scores, probs, qkv, dmix, x, gain, dy, v_prev, grads):
        seq, width = self.seq, self.width
        n = self.rows * seq
        hw = HEADS * seq
        is_top = probs is None
        score_rows = scores[0].shape[0]
        square = pltpu.VMEM((seq, hw), BF16)
        ins = [(s, self.whole(score_rows, hw)) for s in scores]
        if not is_top:
            ins.append((probs, self.whole(seq, hw)))
        ins += [
            (qkv, self.packed(3 * HEADS)),
            (dmix, self.packed(HEADS)),
            (x, self.tile(width)),
            (gain, self.whole(1, width)),
            (dy, self.tile(width)),
            (v_prev, self.packed(HEADS, 2)),
        ]
        outs = [
            (self.shape(1, width, F32), self.whole(1, width)),
            (self.shape(n, width, F32), self.tile(width)),
            (self.shape(n // PACK, PACK * width, BF16), self.packed(HEADS)),
            (self.shape(seq, hw, F32), self.whole(seq, hw)),
            self.grad_out(),
            self.grad_out(),
        ]
        scratch = [square] * 3
        scratch += [pltpu.VMEM((self.chunk, lanes * width), BF16) for lanes in (3, 1)]
        scratch += self.grad_scratch(2) + self.weight_scratch(3) + self.weight_scratch(1)
        if is_top:
            scratch.append(square)
        body = functools.partial(
            backward_kernel, is_top, scale=self.scale, seq=seq, width=width, steps=self.steps
        )
        return self.call(
            body,
            f"layer_back_{layer}",
            self.info(layer, layer - 1),
            None,
            ins,
            outs,
            scratch,
            2 * n * width * width * 5,
            carried=grads,
        )

    def early(self, probs, qkv, dmix, x, gain, dy, grad):
        seq, width = self.seq, self.width
        n, hw = self.rows * seq, HEADS * seq
        ins = [
            (probs, self.whole(seq, hw)),
            (qkv, self.packed(HEADS, 2)),
            (dmix, self.packed(HEADS)),
            (x, self.tile(width)),
            (gain, self.whole(1, width)),
            (dy, self.tile(width)),
        ]
        outs = [(self.shape(n, width, BF16), self.tile(width)), self.grad_out()]
        scratch = [pltpu.VMEM((seq, hw), BF16), pltpu.VMEM((self.chunk, width), BF16)]
        return self.call(
            functools.partial(early_kernel, seq=seq, width=width, steps=self.steps),
            "early_back_0",
            self.info(0, 0),
            0,
            ins,
            outs,
            scratch + self.grad_scratch(1),
            2 * n * width * width * 3,
            carried=(grad,),
            own=(),
        )

    def late(self, scores, probs, qkv, x, gain, grad):
        seq, width = self.seq, self.width
        n, hw = self.rows * seq, HEADS * seq
        ins = [
            (scores[0], self.whole(seq, hw)),
            (scores[1], self.whole(seq, hw)),
            (probs, self.whole(seq, hw)),
            (qkv, self.packed(2 * HEADS)),
            (x, self.tile(width)),
            (gain, self.whole(1, width)),
        ]
        outs = [(self.shape(n, 2 * width, BF16), self.tile(2 * width)), self.grad_out()]
        return self.call(
            functools.partial(
                late_kernel, scale=self.scale, seq=seq, width=width, steps=self.steps
            ),
            "late_back_0",
            self.info(0, 0),
            0,
            ins,
            outs,
            [pltpu.VMEM((seq, hw), BF16)] * 2 + self.grad_scratch(1),
            2 * n * width * width * 3,
            carried=(grad,),
            own=(),
        )

    def gain_grad(self, dqk, dv, x):
        width = self.width
        n = self.rows * self.seq
        return self.call(
            functools.partial(gain_kernel, width=width),
            "gain_back_0",
            self.info(0, 0),
            0,
            [(dqk, self.tile(2 * width)), (dv, self.tile(width)), (x, self.tile(width))],
            [(self.shape(1, width, F32), self.whole(1, width))],
            self.weight_scratch(3),
            2 * n * width * width * 3,
            own=self.own[:1],
        )[0]


def group_swap(value, n_row, n_group):
    other = jnp.zeros_like(value)
    bit = 1
    while bit < n_group:
        if bit > 1:
            value = value + other
        other = lax.ppermute(value, "row", [(r, r ^ bit) for r in range(n_row)])
        bit *= 2
    return value, other


class Fetched:
    first_stages = 2

    def __init__(self, wqkv, wout, section, place, n_section, n_row, n_group):
        assert n_section == 4 and n_group % 2 == 0
        self.section, self.n_row, self.n_group = section, n_row, n_group
        self.member, self.half = place % n_group, place // n_group % 2
        self.last = n_section - 1
        self.block = wqkv.shape[0] // n_group // BLOCKS
        self.own = (wqkv, wout)
        self.to_last = section == (self.last ^ jnp.where(self.member % 2 == 0, 2, 1))
        self.mine = jnp.concatenate([self.own_block(self.half), self.own_block(2)], axis=0)
        self.got = self.hop(self.mine, 1)
        self.across = self.cross(self.got)
        self.stages = [self.halves(self.got, self.across)]

    def own_block(self, place, count=1):
        start = (self.member * BLOCKS + place) * self.block
        rows = [lax.dynamic_slice_in_dim(w, start, count * self.block, 0) for w in self.own]
        return jnp.concatenate(rows, axis=1)

    def hop(self, value, even_bit):
        perm = [
            (s * self.n_row + r, (s ^ (even_bit if r % 2 == 0 else 3 - even_bit)) * self.n_row + r)
            for s in range(self.last + 1)
            for r in range(self.n_row)
        ]
        return lax.ppermute(value, ("section", "row"), perm)

    def cross(self, value):
        perm = [(r, r ^ self.n_group) for r in range(self.n_row)]
        return lax.ppermute(value[: self.block], "row", perm)

    def halves(self, got, across):
        return [(DIRECT, self.share(got)), (ACROSS, self.share(across))]

    def second(self, *ready):
        second, *ready = lax.optimization_barrier(
            (jnp.where(self.to_last, self.got, self.mine), *ready)
        )
        second = self.hop(second, 2)
        self.stages.append(self.halves(second, self.cross(second)))
        low = jnp.where(self.half == 0, self.got[: self.block], self.across)
        high = jnp.where(self.half == 0, self.across, self.got[: self.block])
        relayed = jnp.concatenate([low, high, self.got[self.block :]], axis=0)
        third, _ = lax.optimization_barrier(
            (jnp.where(self.to_last, self.own_block(0, BLOCKS), relayed), second)
        )
        self.third = self.hop(third, 2)
        return ready

    def finish(self, ready):
        third, ready = lax.optimization_barrier((self.third, ready))
        self.stages.append([(FULL, self.share(third))])
        return ready

    def share(self, value):
        have = [value[None]]
        bit = 1
        while bit < self.n_group:
            send = have[0] if len(have) == 1 else jnp.concatenate(have, axis=0)
            have.append(lax.ppermute(send, "row", [(r, r ^ bit) for r in range(self.n_row)]))
            bit *= 2
        return have

    def choices(self, layer):
        offset = self.section ^ layer
        at_last = self.section == self.last
        picks = []
        for parity in (self.member % 2, 1 - self.member % 2):
            first = jnp.where(parity == 0, 1, 2)
            second = jnp.where(at_last, 3, 3 - first)
            pick = jnp.where(offset == first, 1, jnp.where(offset == second, 2, 3))
            picks.append(jnp.where(offset == 0, 0, pick))
        return picks


def local(tokens, embed, ln_gain, w_qkv, w_out, out_grad):
    n_section = lax.axis_size("section")
    n_row = lax.axis_size("row")
    section = lax.axis_index("section")
    place = lax.axis_index("row")
    micro, rows_here, seq = tokens.shape
    width = embed.shape[1]
    n_group = n_row // micro
    member = place % n_group
    rows = rows_here * micro
    scale = HEAD_DIM ** (-0.5) / math.sqrt(rows_here * n_row)
    fetched = Fetched(w_qkv[0], w_out[0], section, place, n_section, n_row, n_group)
    same = [[m * n_group + g for m in range(micro)] for g in range(n_group)]
    exchange = functools.partial(
        lax.all_to_all,
        axis_name="row",
        split_axis=0,
        concat_axis=0,
        axis_index_groups=same,
        tiled=True,
    )
    tok = exchange(tokens).reshape(-1)
    top_grad = exchange(out_grad).reshape(rows * seq, width)
    gains = lax.all_gather(ln_gain[0], "section", axis=0, tiled=False)
    table = (jnp.arange(embed.shape[0], dtype=jnp.int32)[:, None] == tok[None, :]).astype(BF16)
    x = lax.dot_general(table, embed, TN, preferred_element_type=F32)

    x, gains = fetched.second(x, gains)
    chain = Chain(fetched, member, n_group, (w_qkv, w_out), seq, width, rows, scale)
    xs, qkvs, probs = [], [], []
    scores = None
    dmix = None
    for layer in range(n_section):
        prev = None if layer == 0 else (*scores, qkvs[-1])
        top = top_grad if layer == n_section - 1 else None
        outs = list(chain.forward(layer, x, gains[layer][None], prev, top))
        if prev is not None:
            probs.append(outs.pop(0))
            x = outs.pop(0)
        xs.append(x)
        qkvs.append(outs[0])
        if top is not None:
            dmix = outs[2]
        scores = group_swap(outs[1], n_row, n_group)
        if layer == 0:
            scores = (scores[0], fetched.finish(scores[1]))
    probs.append(None)

    dy = top_grad
    gain_parts = [None] * n_section
    grads = ()
    for layer in range(n_section - 1, 0, -1):
        gain_parts[layer], dy, dmix, part, *grads = chain.backward(
            layer,
            scores,
            probs[layer],
            qkvs[layer],
            dmix,
            xs[layer],
            gains[layer][None],
            dy,
            qkvs[layer - 1],
            grads,
        )
        scores = group_swap(part, n_row, n_group)
    sum_rows = functools.partial(
        lax.psum_scatter, axis_name="row", scatter_dimension=0, tiled=True
    )
    gain = gains[0][None]
    d_v, grad_a = chain.early(probs[0], qkvs[0], dmix, xs[0], gain, dy, grads[0])
    grad_a = sum_rows(grad_a).astype(F32)
    d_qk, grad_b = chain.late(scores, probs[0], qkvs[0], xs[0], gain, grads[1])
    grad_b = sum_rows(grad_b).astype(F32)
    gain_parts[0] = chain.gain_grad(d_qk, d_v, xs[0])
    g_gain = lax.select_n(section, *gain_parts)
    bit = 1
    while bit < n_row:
        g_gain = g_gain + lax.ppermute(g_gain, "row", [(r, r ^ bit) for r in range(n_row)])
        bit *= 2
    g_gain = lax.dynamic_slice_in_dim(g_gain, place * (width // n_row), width // n_row, 1)
    g_qkv = jnp.concatenate([grad_b, grad_a[:, width:]], axis=1)
    return (g_qkv[None], grad_a[None, :, :width], g_gain)


def solution(mesh):
    in_specs = (
        P(None, "row", None),
        P(),
        P("section", None),
        P("section", None, None),
        P("section", None, None),
        P(None, "row", None, None),
    )
    out_specs = (P("section", "row", None), P("section", "row", None), P("section", "row"))
    return jax.shard_map(local, mesh=mesh, in_specs=in_specs, out_specs=out_specs, check_vma=False)
```

```python
import functools
import math

import jax
import jax.numpy as jnp
from jax import lax
from jax.experimental import pallas as pl
from jax.experimental.pallas import tpu as pltpu
from jax.sharding import PartitionSpec as P

HEADS = 12
HEAD_DIM = 64
PACK = 2
BLOCKS = 3
TILE = 256
DIRECT, ACROSS, FULL = range(3)
F32 = jnp.float32
BF16 = jnp.bfloat16
VMEM_LIMIT = 60 * 1024 * 1024
NT = (((1,), (1,)), ((), ()))
TN = (((0,), (0,)), ((), ()))


def mm(a, b):
    return jnp.dot(a, b, preferred_element_type=F32)


def column_loop(columns, body):
    @pl.loop(0, columns // TILE)
    def _(n):
        body(pl.multiple_of(n * TILE, TILE))


def mm_nt(a, b):
    return lax.dot_general(a, b, NT, preferred_element_type=F32)


def head_lanes(ref, seq, head):
    width = PACK * HEAD_DIM
    first = head * width
    return jnp.concatenate(
        [ref[r * seq : (r + 1) * seq, first : first + width] for r in range(ref.shape[0] // seq)],
        axis=1,
    )


def regroup(blocks):
    return [
        jnp.concatenate([block[:, n * HEAD_DIM : (n + 1) * HEAD_DIM] for block in blocks], axis=1)
        for n in range(PACK)
    ]


def pack_rows(value, out, first, seq):
    width = PACK * HEAD_DIM
    for pair in range(value.shape[0] // seq // PACK):
        for p in range(value.shape[1] // width):
            blocks = [
                value[(pair * PACK + r) * seq : (pair * PACK + r + 1) * seq, p * width : (p + 1) * width]
                for r in range(PACK)
            ]
            for n, block in enumerate(regroup(blocks)):
                at = pl.multiple_of(first + (p * PACK + n) * width, width)
                out[pair * seq : (pair + 1) * seq, pl.ds(at, width)] = block


class Weights:
    def __init__(self, info, first, own, stages, columns, dst, sems):
        self.choices = (info[first], info[first + 1])
        self.member, self.half = info[4], info[5]
        self.own, self.stages = own, stages
        self.columns, self.dst, self.sems = columns, dst, sems

    def each(self, act):
        @pl.when(self.choices[0] == 0)
        def _():
            act(pltpu.make_async_copy(self.own.at[0], self.dst, self.sems.at[0]))

        for stage, group in enumerate(self.stages):
            for parity in range(2):

                @pl.when(self.choices[parity] == stage + 1)
                def _(group=group, parity=parity):
                    for kind, refs in group:
                        self.shares(kind, refs, parity, act)

    def shares(self, kind, refs, parity, act):
        group = self.sems.shape[0] // BLOCKS
        block = self.dst.shape[0] // group // BLOCKS
        places = {DIRECT: (self.half, 2), ACROSS: (1 - self.half,), FULL: (0, 1, 2)}[kind]
        sems = {DIRECT: (0, 1), ACROSS: (2,), FULL: (0, 1, 2)}[kind]
        seen = 0
        for ref in refs:
            for n in range(ref.shape[0]):
                if seen % 2 == parity:
                    base = (self.member ^ seen) * BLOCKS
                    for j, place in enumerate(places):
                        start = pl.multiple_of((base + place) * block, block)
                        act(
                            pltpu.make_async_copy(
                                ref.at[n, j * block : (j + 1) * block, self.columns],
                                self.dst.at[pl.ds(start, block)],
                                self.sems.at[seen * BLOCKS + sems[j]],
                            )
                        )
                seen += 1

    def start(self):
        self.each(lambda copy: copy.start())

    def wait(self):
        self.each(lambda copy: copy.wait())


def take_stages(it, layout):
    return [[(kind, [next(it) for _ in range(count)]) for kind, count in group] for group in layout]


def softmax_heads(la, lb, scale, keep):
    seq = la.shape[0]
    for h in range(HEADS):
        at = slice(h * seq, (h + 1) * seq)
        logits = (la[:, at] + lb[:, at]) * scale
        e = jnp.exp(logits - jnp.max(logits, axis=-1, keepdims=True))
        keep(h, e / jnp.sum(e, axis=-1, keepdims=True))


def norm_parts(x):
    centred = x - jnp.mean(x, axis=-1, keepdims=True)
    spread = jnp.mean(centred * centred, axis=-1, keepdims=True)
    rstd = lax.rsqrt(spread + 1e-05)
    return centred * rstd, rstd


def scores(ref_a, first_a, ref_b, first_b, out, out_row, seq, begin):
    parts = [
        mm_nt(head_lanes(ref_a, seq, first_a + h), head_lanes(ref_b, seq, first_b + h))
        for h in range(HEADS)
    ]
    rows = slice(out_row, out_row + seq)

    @pl.when(begin)
    def _():
        for h, part in enumerate(parts):
            out[rows, h * seq : (h + 1) * seq] = part

    @pl.when(jnp.logical_not(begin))
    def _():
        for h, part in enumerate(parts):
            out[rows, h * seq : (h + 1) * seq] += part


def mix(weights, ref_b, first_b, out, first_out, scale, seq):
    width = PACK * HEAD_DIM
    for p in range(HEADS // PACK):
        values = []
        for h in range(p * PACK, (p + 1) * PACK):
            value = mm(weights[:, h * seq : (h + 1) * seq], head_lanes(ref_b, seq, first_b + h))
            values.append((value if scale is None else value * scale).astype(BF16))
        at = first_out + p * width
        for pair in range(ref_b.shape[0] // seq):
            blocks = [value[:, pair * width : (pair + 1) * width] for value in values]
            for n, block in enumerate(regroup(blocks)):
                row = (pair * PACK + n) * seq
                out[row : row + seq, at : at + width] = block


def forward_kernel(has_prev, has_top, info, *refs, layout, scale, seq, width):
    it = iter(refs)
    if has_prev:
        la, lb, v_prev = next(it), next(it), next(it)
    x_in, gain = next(it), next(it)
    top = next(it) if has_top else None
    own_q, own_o = next(it), next(it)
    stages = take_stages(it, layout)
    if has_prev:
        probs_out, x_out = next(it), next(it)
    qkv_out, score_out = next(it), next(it)
    if has_top:
        dmix_out = next(it)
    wq, sem_q, h = next(it), next(it), next(it)
    if has_prev:
        wo, sem_o, mixed = next(it), next(it), next(it)
    if has_top:
        wt, sem_t = next(it), next(it)
    step = pl.program_id(0)
    qcols, ocols = slice(0, 3 * width), slice(3 * width, 4 * width)
    get_q = Weights(info, 0, own_q, stages, qcols, wq, sem_q)
    if has_prev:
        get_o = Weights(info, 2, own_o, stages, ocols, wo, sem_o)
    if has_top:
        get_t = Weights(info, 0, own_o, stages, ocols, wt, sem_t)

    @pl.when(step == 0)
    def _():
        if has_prev:
            get_o.start()
        get_q.start()
        if has_top:
            get_t.start()
        if has_prev:

            def keep(h, value):
                probs_out[:, h * seq : (h + 1) * seq] = value.astype(BF16)

            softmax_heads(la, lb, scale, keep)

    if has_prev:
        mix(probs_out, v_prev, 0, mixed, 0, None, seq)
        pl.when(step == 0)(get_o.wait)

        @functools.partial(column_loop, width)
        def _(at):
            cols = pl.ds(at, TILE)
            x_out[:, cols] = x_in[:, cols] + mm(mixed[...], wo[:, cols])

    hat, _ = norm_parts(x_out[...] if has_prev else x_in[...])
    h[...] = (hat * gain[...]).astype(BF16)
    pl.when(step == 0)(get_q.wait)

    @functools.partial(column_loop, 3 * width)
    def _(at):
        part = mm(h[...], wq[:, pl.ds(at, TILE)]).astype(BF16)
        pack_rows(part, qkv_out, PACK * at, seq)

    begin = step == 0
    scores(qkv_out, 0, qkv_out, HEADS, score_out, 0, seq, begin)
    if has_top:
        pl.when(step == 0)(get_t.wait)

        @functools.partial(column_loop, width)
        def _(at):
            part = mm_nt(top[...], wt[pl.ds(at, TILE), :]).astype(BF16)
            pack_rows(part, dmix_out, PACK * at, seq)

        scores(dmix_out, 0, qkv_out, 2 * HEADS, score_out, seq, seq, begin)


def add_gain(gain_out, d_h, hat, step):
    part = jnp.sum(d_h * hat, axis=0, keepdims=True)

    @pl.when(step == 0)
    def _():
        gain_out[...] = part

    @pl.when(step > 0)
    def _():
        gain_out[...] += part


def add_product(a, b, first, columns, total, place, step, steps, staged):
    @functools.partial(column_loop, columns)
    def _(at):
        there = pl.ds(pl.multiple_of(place + at, TILE), TILE)
        right = b[:, pl.ds(pl.multiple_of(first + at, TILE), TILE)].astype(BF16)
        part = lax.dot_general(a[...], right, TN, preferred_element_type=F32)

        @pl.when(step == 0)
        def _():
            total[:, there] = part

        @pl.when((step > 0) & (step < steps - 1))
        def _():
            total[:, there] += part

        @pl.when(step == steps - 1)
        def _():
            staged[:, there] = ((total[:, there] if steps > 1 else 0.0) + part).astype(BF16)


def logit_grads(probs, sa, sb, first, seq, dl, dlt):
    for h in range(HEADS):
        at = slice(h * seq, (h + 1) * seq)
        prob = probs[:, at].astype(F32)
        d_prob = sa[first : first + seq, at] + sb[first : first + seq, at]
        d_logit = prob * (d_prob - jnp.sum(d_prob * prob, axis=-1, keepdims=True))
        dl[:, at] = d_logit.astype(BF16)
        dlt[:, at] = jnp.transpose(d_logit).astype(BF16)


def turn_probs(probs, seq, pt):
    for h in range(HEADS):
        at = slice(h * seq, (h + 1) * seq)
        pt[:, at] = jnp.transpose(probs[:, at].astype(F32)).astype(BF16)


def backward_kernel(is_top, info, *refs, layout, scale, seq, width, steps):
    it = iter(refs)
    sa, sb = next(it), next(it)
    if not is_top:
        probs = next(it)
    qkv, dmix, x_in, gain, dy, v_prev = [next(it) for _ in range(6)]
    if not is_top:
        next(it), next(it)
    own_q, own_o = next(it), next(it)
    stages = take_stages(it, layout)
    gain_out, dy_out, dmix_out, score_out = [next(it) for _ in range(4)]
    grad_a, grad_b = next(it), next(it)
    dl, dlt, pt, dqkv, d_hs, mixed = [next(it) for _ in range(6)]
    total_a, total_b, staged_a, staged_b, sem_g = [next(it) for _ in range(5)]
    wq, sem_q, wo, sem_o = [next(it) for _ in range(4)]
    if is_top:
        probs = next(it)
    step = pl.program_id(0)
    get_q = Weights(info, 0, own_q, stages, slice(0, 3 * width), wq, sem_q)
    get_o = Weights(info, 2, own_o, stages, slice(3 * width, 4 * width), wo, sem_o)
    own = info[0] == 0

    @pl.when(step == 0)
    def _():
        get_q.start()
        get_o.start()
        if is_top:

            def keep(h, value):
                probs[:, h * seq : (h + 1) * seq] = value.astype(BF16)

            softmax_heads(sa.at[0:seq], sb.at[0:seq], scale, keep)
        logit_grads(probs, sa, sb, seq if is_top else 0, seq, dl, dlt)
        turn_probs(probs, seq, pt)

    mix(dl, qkv, HEADS, dqkv, 0, scale, seq)
    mix(dlt, qkv, 0, dqkv, width, scale, seq)
    mix(pt, dmix, 0, dqkv, 2 * width, None, seq)
    pl.when(step == 0)(get_q.wait)

    @functools.partial(column_loop, width)
    def _(at):
        d_hs[:, pl.ds(at, TILE)] = mm_nt(dqkv[...], wq[pl.ds(at, TILE), :]).astype(BF16)

    d_h = d_hs[...].astype(F32)
    hat, rstd = norm_parts(x_in[...])
    add_gain(gain_out, d_h, hat, step)
    d_hat = d_h * gain[...]
    mean_d = jnp.mean(d_hat, axis=-1, keepdims=True)
    mean_dh = jnp.mean(d_hat * hat, axis=-1, keepdims=True)
    d_x = dy[...].astype(F32) + rstd * (d_hat - mean_d - hat * mean_dh)
    dy_out[...] = d_x
    d_hs[...] = d_x.astype(BF16)
    pl.when(step == 0)(get_o.wait)

    @functools.partial(column_loop, width)
    def _(at):
        part = mm_nt(d_hs[...], wo[pl.ds(at, TILE), :]).astype(BF16)
        pack_rows(part, dmix_out, PACK * at, seq)

    scores(dmix_out, 0, v_prev, 0, score_out, 0, seq, step == 0)

    @pl.when(own)
    def _():
        mix(probs, qkv, 2 * HEADS, mixed, 0, None, seq)
        add_product(mixed, dy, 0, width, total_a, 0, step, steps, staged_a)
        mixed[...] = (norm_parts(x_in[...])[0] * gain[...]).astype(BF16)
        add_product(mixed, dqkv, 2 * width, width, total_a, width, step, steps, staged_a)
        add_product(mixed, dqkv, 0, 2 * width, total_b, 0, step, steps, staged_b)

    @pl.when(own & (step == steps - 1))
    def _():
        copies = [
            pltpu.make_async_copy(staged_a, grad_a, sem_g.at[0]),
            pltpu.make_async_copy(staged_b, grad_b, sem_g.at[1]),
        ]
        for copy in copies:
            copy.start()
        for copy in copies:
            copy.wait()


def early_kernel(info, *refs, layout, seq, width, steps):
    probs, v, dmix, x_in, gain, dy, _, dv_out, grad_a, pt, mixed, total, staged, sem = refs
    step = pl.program_id(0)
    own = info[0] == 0

    @pl.when(own)
    def _():
        @pl.when(step == 0)
        def _():
            turn_probs(probs, seq, pt)

        mix(probs, v, 0, mixed, 0, None, seq)
        mix(pt, dmix, 0, dv_out, 0, None, seq)
        add_product(mixed, dy, 0, width, total, 0, step, steps, staged)
        mixed[...] = (norm_parts(x_in[...])[0] * gain[...]).astype(BF16)
        add_product(mixed, dv_out, 0, width, total, width, step, steps, staged)

    @pl.when(own & (step == steps - 1))
    def _():
        copy = pltpu.make_async_copy(staged, grad_a, sem.at[0])
        copy.start()
        copy.wait()


def late_kernel(info, *refs, layout, scale, seq, width, steps):
    sa, sb, probs, qk, x_in, gain, _, dqk_out, grad_b, dl, dlt, h, total, staged, sem = refs
    step = pl.program_id(0)
    own = info[0] == 0

    @pl.when(own)
    def _():
        @pl.when(step == 0)
        def _():
            logit_grads(probs, sa, sb, 0, seq, dl, dlt)

        h[...] = (norm_parts(x_in[...])[0] * gain[...]).astype(BF16)
        mix(dl, qk, HEADS, dqk_out, 0, scale, seq)
        mix(dlt, qk, 0, dqk_out, width, scale, seq)
        add_product(h, dqk_out, 0, 2 * width, total, 0, step, steps, staged)

    @pl.when(own & (step == steps - 1))
    def _():
        copy = pltpu.make_async_copy(staged, grad_b, sem.at[0])
        copy.start()
        copy.wait()


def gain_kernel(info, *refs, layout, width):
    dqk, dv, x_in, own_q, gain_out, d_h, wq, sem = refs
    step = pl.program_id(0)

    @pl.when(info[0] == 0)
    def _():
        @pl.when(step == 0)
        def _():
            copy = pltpu.make_async_copy(own_q.at[0], wq, sem.at[0])
            copy.start()
            copy.wait()

        hat, _ = norm_parts(x_in[...])

        @functools.partial(column_loop, width)
        def _(at):
            rows = pl.ds(at, TILE)
            part = mm_nt(dqk[...], wq[rows, : 2 * width]) + mm_nt(dv[...], wq[rows, 2 * width :])
            d_h[:, rows] = part.astype(BF16)

        add_gain(gain_out, d_h[...].astype(F32), hat, step)


class Chain:
    def __init__(self, fetched, member, n_group, own, seq, width, rows, scale):
        self.fetched, self.member, self.n_group = fetched, member, n_group
        self.own, self.seq, self.width, self.rows = own, seq, width, rows
        self.scale = scale
        per_step = 4 if rows % 4 == 0 else 2
        self.chunk = per_step * seq
        self.steps = rows // per_step

    def info(self, now, other):
        picks = self.fetched.choices(now) + self.fetched.choices(other)
        return jnp.stack(picks + [self.member, self.fetched.half]).astype(jnp.int32)

    def whole(self, rows, lanes):
        return pl.BlockSpec((rows, lanes), lambda i, s: (0, 0))

    def tile(self, lanes, column=0, part=1):
        return pl.BlockSpec((self.chunk // part, lanes), lambda i, s: (i, column))

    def packed(self, heads, column=0):
        return self.tile(heads * PACK * HEAD_DIM, column, PACK)

    def call(self, body, name, info, stages, ins, outs, scratch, flops, carried=(), own=None):
        any_spec = pl.BlockSpec(memory_space=pl.ANY)
        groups = self.fetched.stages[:stages]
        weights = list(self.own if own is None else own)
        weights += [a for group in groups for _, arrays in group for a in arrays]
        arrays = [a for a, _ in ins] + list(carried)
        shapes = [o for o, _ in outs]
        size = sum(math.prod(a.shape) * a.dtype.itemsize for a in arrays + shapes)
        aliases = {
            1 + len(ins) + n: len(outs) - len(carried) + n for n in range(len(carried))
        }
        layout = tuple(tuple((kind, len(arrays)) for kind, arrays in group) for group in groups)
        return pl.pallas_call(
            functools.partial(body, layout=layout),
            name=name,
            out_shape=shapes,
            grid_spec=pltpu.PrefetchScalarGridSpec(
                num_scalar_prefetch=1,
                grid=(self.steps,),
                in_specs=[spec for _, spec in ins] + [any_spec] * (len(carried) + len(weights)),
                out_specs=[spec for _, spec in outs],
                scratch_shapes=scratch,
            ),
            input_output_aliases=aliases,
            compiler_params=pltpu.CompilerParams(
                dimension_semantics=("arbitrary",), vmem_limit_bytes=VMEM_LIMIT
            ),
            cost_estimate=pl.CostEstimate(flops=flops, bytes_accessed=size, transcendentals=0),
        )(info, *arrays, *weights)

    def weight_scratch(self, columns):
        return [
            pltpu.VMEM((self.width, columns * self.width), BF16),
            pltpu.SemaphoreType.DMA((self.n_group * BLOCKS,)),
        ]

    def shape(self, rows, lanes, dtype):
        return jax.ShapeDtypeStruct((rows, lanes), dtype)

    def grad_out(self):
        any_spec = pl.BlockSpec(memory_space=pl.ANY)
        return (self.shape(self.width, 2 * self.width, BF16), any_spec)

    def grad_scratch(self, copies):
        shape = (self.width, 2 * self.width)
        scratch = [pltpu.VMEM(shape, F32)] * copies + [pltpu.VMEM(shape, BF16)] * copies
        return scratch + [pltpu.SemaphoreType.DMA((copies,))]

    def forward(self, layer, x, gain, prev, top):
        seq, width = self.seq, self.width
        n = self.rows * seq
        hw = HEADS * seq
        score_rows = seq if top is None else 2 * seq
        ins = [(x, self.tile(width)), (gain, self.whole(1, width))]
        outs = [
            (self.shape(n // PACK, 3 * PACK * width, BF16), self.packed(3 * HEADS)),
            (self.shape(score_rows, hw, F32), self.whole(score_rows, hw)),
        ]
        scratch = self.weight_scratch(3) + [pltpu.VMEM((self.chunk, width), BF16)]
        if prev is not None:
            ins = [
                (prev[0], self.whole(seq, hw)),
                (prev[1], self.whole(seq, hw)),
                (prev[2], self.packed(HEADS, 2)),
            ] + ins
            outs = [
                (self.shape(seq, hw, BF16), self.whole(seq, hw)),
                (self.shape(n, width, F32), self.tile(width)),
            ] + outs
            scratch += self.weight_scratch(1) + [pltpu.VMEM((self.chunk, width), BF16)]
        if top is not None:
            ins.append((top, self.tile(width)))
            outs.append((self.shape(n // PACK, PACK * width, BF16), self.packed(HEADS)))
            scratch += self.weight_scratch(1)
        body = functools.partial(
            forward_kernel, prev is not None, top is not None, scale=self.scale, seq=seq, width=width
        )
        return self.call(
            body,
            f"layer_in_{layer}",
            self.info(layer, max(layer - 1, 0)),
            self.fetched.first_stages if layer == 0 else None,
            ins,
            outs,
            scratch,
            2 * n * width * width * 5,
        )

    def backward(self, layer, scores, probs, qkv, dmix, x, gain, dy, v_prev, grads):
        seq, width = self.seq, self.width
        n = self.rows * seq
        hw = HEADS * seq
        is_top = probs is None
        score_rows = scores[0].shape[0]
        square = pltpu.VMEM((seq, hw), BF16)
        ins = [(s, self.whole(score_rows, hw)) for s in scores]
        if not is_top:
            ins.append((probs, self.whole(seq, hw)))
        ins += [
            (qkv, self.packed(3 * HEADS)),
            (dmix, self.packed(HEADS)),
            (x, self.tile(width)),
            (gain, self.whole(1, width)),
            (dy, self.tile(width)),
            (v_prev, self.packed(HEADS, 2)),
        ]
        outs = [
            (self.shape(1, width, F32), self.whole(1, width)),
            (self.shape(n, width, F32), self.tile(width)),
            (self.shape(n // PACK, PACK * width, BF16), self.packed(HEADS)),
            (self.shape(seq, hw, F32), self.whole(seq, hw)),
            self.grad_out(),
            self.grad_out(),
        ]
        scratch = [square] * 3
        scratch += [pltpu.VMEM((self.chunk, lanes * width), BF16) for lanes in (3, 1, 1)]
        scratch += self.grad_scratch(2) + self.weight_scratch(3) + self.weight_scratch(1)
        if is_top:
            scratch.append(square)
        body = functools.partial(
            backward_kernel, is_top, scale=self.scale, seq=seq, width=width, steps=self.steps
        )
        return self.call(
            body,
            f"layer_back_{layer}",
            self.info(layer, layer - 1),
            None,
            ins,
            outs,
            scratch,
            2 * n * width * width * 5,
            carried=grads,
        )

    def early(self, probs, qkv, dmix, x, gain, dy, grad):
        seq, width = self.seq, self.width
        n, hw = self.rows * seq, HEADS * seq
        ins = [
            (probs, self.whole(seq, hw)),
            (qkv, self.packed(HEADS, 2)),
            (dmix, self.packed(HEADS)),
            (x, self.tile(width)),
            (gain, self.whole(1, width)),
            (dy, self.tile(width)),
        ]
        outs = [(self.shape(n, width, BF16), self.tile(width)), self.grad_out()]
        scratch = [pltpu.VMEM((seq, hw), BF16), pltpu.VMEM((self.chunk, width), BF16)]
        return self.call(
            functools.partial(early_kernel, seq=seq, width=width, steps=self.steps),
            "early_back_0",
            self.info(0, 0),
            0,
            ins,
            outs,
            scratch + self.grad_scratch(1),
            2 * n * width * width * 3,
            carried=(grad,),
            own=(),
        )

    def late(self, scores, probs, qkv, x, gain, grad):
        seq, width = self.seq, self.width
        n, hw = self.rows * seq, HEADS * seq
        ins = [
            (scores[0], self.whole(seq, hw)),
            (scores[1], self.whole(seq, hw)),
            (probs, self.whole(seq, hw)),
            (qkv, self.packed(2 * HEADS)),
            (x, self.tile(width)),
            (gain, self.whole(1, width)),
        ]
        outs = [(self.shape(n, 2 * width, BF16), self.tile(2 * width)), self.grad_out()]
        return self.call(
            functools.partial(
                late_kernel, scale=self.scale, seq=seq, width=width, steps=self.steps
            ),
            "late_back_0",
            self.info(0, 0),
            0,
            ins,
            outs,
            [pltpu.VMEM((seq, hw), BF16)] * 2
            + [pltpu.VMEM((self.chunk, width), BF16)]
            + self.grad_scratch(1),
            2 * n * width * width * 3,
            carried=(grad,),
            own=(),
        )

    def gain_grad(self, dqk, dv, x):
        width = self.width
        n = self.rows * self.seq
        return self.call(
            functools.partial(gain_kernel, width=width),
            "gain_back_0",
            self.info(0, 0),
            0,
            [(dqk, self.tile(2 * width)), (dv, self.tile(width)), (x, self.tile(width))],
            [(self.shape(1, width, F32), self.whole(1, width))],
            [pltpu.VMEM((self.chunk, width), BF16)] + self.weight_scratch(3),
            2 * n * width * width * 3,
            own=self.own[:1],
        )[0]


def group_swap(value, n_row, n_group):
    other = jnp.zeros_like(value)
    bit = 1
    while bit < n_group:
        if bit > 1:
            value = value + other
        other = lax.ppermute(value, "row", [(r, r ^ bit) for r in range(n_row)])
        bit *= 2
    return value, other


def sum_rows(grad, place, n_row, n_group):
    rows = grad.shape[0] // n_row
    spans = [1 << n for n in range(n_row.bit_length() - 1)]
    value = grad.reshape(n_row, rows, grad.shape[1])
    for bit in spans:
        mine = (place // bit) % 2
        pair = value.reshape(value.shape[0] // 2, 2, *value.shape[1:])
        keep = lax.dynamic_index_in_dim(pair, mine, 1, keepdims=False)
        send = lax.dynamic_index_in_dim(pair, 1 - mine, 1, keepdims=False)
        other = lax.ppermute(
            send.astype(BF16), "row", [(r, r ^ bit) for r in range(n_row)]
        )
        value = keep.astype(F32) + other.astype(F32)
    return value[0]


class Fetched:
    first_stages = 2

    def __init__(self, wqkv, wout, section, place, n_section, n_row, n_group):
        assert n_section == 4 and n_group % 2 == 0
        self.section, self.n_row, self.n_group = section, n_row, n_group
        self.member, self.half = place % n_group, place // n_group % 2
        self.last = n_section - 1
        self.block = wqkv.shape[0] // n_group // BLOCKS
        self.own = (wqkv, wout)
        self.to_last = section == (self.last ^ jnp.where(self.member % 2 == 0, 2, 1))
        self.mine = jnp.concatenate([self.own_block(self.half), self.own_block(2)], axis=0)
        self.got = self.hop(self.mine, 1)
        self.across = self.cross(self.got)
        self.stages = [self.halves(self.got, self.across)]

    def own_block(self, place, count=1):
        start = (self.member * BLOCKS + place) * self.block
        rows = [lax.dynamic_slice_in_dim(w, start, count * self.block, 0) for w in self.own]
        return jnp.concatenate(rows, axis=1)

    def hop(self, value, even_bit):
        perm = [
            (s * self.n_row + r, (s ^ (even_bit if r % 2 == 0 else 3 - even_bit)) * self.n_row + r)
            for s in range(self.last + 1)
            for r in range(self.n_row)
        ]
        return lax.ppermute(value, ("section", "row"), perm)

    def cross(self, value):
        perm = [(r, r ^ self.n_group) for r in range(self.n_row)]
        return lax.ppermute(value[: self.block], "row", perm)

    def halves(self, got, across):
        return [(DIRECT, self.share(got)), (ACROSS, self.share(across))]

    def second(self, x, gains):
        second, x = lax.optimization_barrier((jnp.where(self.to_last, self.got, self.mine), x))
        second = self.hop(second, 2)
        self.stages.append(self.halves(second, self.cross(second)))
        low = jnp.where(self.half == 0, self.got[: self.block], self.across)
        high = jnp.where(self.half == 0, self.across, self.got[: self.block])
        relayed = jnp.concatenate([low, high, self.got[self.block :]], axis=0)
        third = jnp.where(self.to_last, self.own_block(0, BLOCKS), relayed)
        third, gains, _ = lax.optimization_barrier((third, gains, second))
        self.third = self.hop(third, 2)
        return x, gains

    def finish(self, ready):
        third, ready = lax.optimization_barrier((self.third, ready))
        self.stages.append([(FULL, self.share(third))])
        return ready

    def share(self, value):
        have = [value[None]]
        bit = 1
        while bit < self.n_group:
            send = have[0] if len(have) == 1 else jnp.concatenate(have, axis=0)
            have.append(lax.ppermute(send, "row", [(r, r ^ bit) for r in range(self.n_row)]))
            bit *= 2
        return have

    def choices(self, layer):
        offset = self.section ^ layer
        at_last = self.section == self.last
        picks = []
        for parity in (self.member % 2, 1 - self.member % 2):
            first = jnp.where(parity == 0, 1, 2)
            second = jnp.where(at_last, 3, 3 - first)
            pick = jnp.where(offset == first, 1, jnp.where(offset == second, 2, 3))
            picks.append(jnp.where(offset == 0, 0, pick))
        return picks


def local(tokens, embed, ln_gain, w_qkv, w_out, out_grad):
    n_section = lax.axis_size("section")
    n_row = lax.axis_size("row")
    section = lax.axis_index("section")
    place = lax.axis_index("row")
    micro, rows_here, seq = tokens.shape
    width = embed.shape[1]
    n_group = n_row // micro
    member = place % n_group
    rows = rows_here * micro
    scale = HEAD_DIM ** (-0.5) / math.sqrt(rows_here * n_row)
    fetched = Fetched(w_qkv[0], w_out[0], section, place, n_section, n_row, n_group)
    same = [[m * n_group + g for m in range(micro)] for g in range(n_group)]
    exchange = functools.partial(
        lax.all_to_all,
        axis_name="row",
        split_axis=0,
        concat_axis=0,
        axis_index_groups=same,
        tiled=True,
    )
    tok = exchange(tokens).reshape(-1)
    top_grad = exchange(out_grad).reshape(rows * seq, width)
    gains = lax.all_gather(ln_gain[0], "section", axis=0, tiled=False)
    table = (jnp.arange(embed.shape[0], dtype=jnp.int32)[:, None] == tok[None, :]).astype(BF16)
    x = lax.dot_general(table, embed, TN, preferred_element_type=F32)

    x, gains = fetched.second(x, gains)
    chain = Chain(fetched, member, n_group, (w_qkv, w_out), seq, width, rows, scale)
    xs, qkvs, probs = [], [], []
    scores = None
    dmix = None
    for layer in range(n_section):
        prev = None if layer == 0 else (*scores, qkvs[-1])
        top = top_grad if layer == n_section - 1 else None
        outs = list(chain.forward(layer, x, gains[layer][None], prev, top))
        if prev is not None:
            probs.append(outs.pop(0))
            x = outs.pop(0)
        xs.append(x)
        qkvs.append(outs[0])
        if top is not None:
            dmix = outs[2]
        scores = group_swap(outs[1], n_row, n_group)
        if layer == 0:
            scores = (scores[0], fetched.finish(scores[1]))
    probs.append(None)

    dy = top_grad
    gain_parts = [None] * n_section
    grads = ()
    for layer in range(n_section - 1, 0, -1):
        gain_parts[layer], dy, dmix, part, *grads = chain.backward(
            layer,
            scores,
            probs[layer],
            qkvs[layer],
            dmix,
            xs[layer],
            gains[layer][None],
            dy,
            qkvs[layer - 1],
            grads,
        )
        scores = group_swap(part, n_row, n_group)
    gain = gains[0][None]
    d_v, grad_a = chain.early(probs[0], qkvs[0], dmix, xs[0], gain, dy, grads[0])
    grad_a = sum_rows(grad_a, place, n_row, n_group)
    d_qk, grad_b = chain.late(scores, probs[0], qkvs[0], xs[0], gain, grads[1])
    grad_b = sum_rows(grad_b, place, n_row, n_group)
    gain_parts[0] = chain.gain_grad(d_qk, d_v, xs[0])
    g_gain = lax.select_n(section, *gain_parts)
    bit = 1
    while bit < n_row:
        g_gain = g_gain + lax.ppermute(g_gain, "row", [(r, r ^ bit) for r in range(n_row)])
        bit *= 2
    g_gain = lax.dynamic_slice_in_dim(g_gain, place * (width // n_row), width // n_row, 1)
    g_qkv = jnp.concatenate([grad_b, grad_a[:, width:]], axis=1)
    return (g_qkv[None], grad_a[None, :, :width], g_gain)


def solution(mesh):
    in_specs = (
        P(None, "row", None),
        P(),
        P("section", None),
        P("section", None, None),
        P("section", None, None),
        P(None, "row", None, None),
    )
    out_specs = (P("section", "row", None), P("section", "row", None), P("section", "row"))
    return jax.shard_map(local, mesh=mesh, in_specs=in_specs, out_specs=out_specs, check_vma=False)
```

```python
import functools
import math

import jax
import jax.numpy as jnp
from jax import lax
from jax.experimental import pallas as pl
from jax.experimental.pallas import tpu as pltpu
from jax.sharding import PartitionSpec as P

HEADS = 12
HEAD_DIM = 64
PACK = 2
BLOCKS = 3
DIRECT, ACROSS, FULL = range(3)
F32 = jnp.float32
BF16 = jnp.bfloat16
VMEM_LIMIT = 60 * 1024 * 1024
NT = (((1,), (1,)), ((), ()))
TN = (((0,), (0,)), ((), ()))


def mm(a, b):
    return jnp.dot(a, b, preferred_element_type=F32)


def mm_nt(a, b):
    return lax.dot_general(a, b, NT, preferred_element_type=F32)


def head_lanes(ref, seq, head):
    width = PACK * HEAD_DIM
    first = head * width
    return jnp.concatenate(
        [ref[r * seq : (r + 1) * seq, first : first + width] for r in range(ref.shape[0] // seq)],
        axis=1,
    )


def regroup(blocks):
    return [
        jnp.concatenate([block[:, n * HEAD_DIM : (n + 1) * HEAD_DIM] for block in blocks], axis=1)
        for n in range(PACK)
    ]


def pack_rows(value, out, first, seq):
    width = PACK * HEAD_DIM
    for pair in range(value.shape[0] // seq // PACK):
        for p in range(value.shape[1] // width):
            blocks = [
                value[(pair * PACK + r) * seq : (pair * PACK + r + 1) * seq, p * width : (p + 1) * width]
                for r in range(PACK)
            ]
            for n, block in enumerate(regroup(blocks)):
                at = (first + p * PACK + n) * width
                out[pair * seq : (pair + 1) * seq, at : at + width] = block


class Weights:
    def __init__(self, info, first, own, stages, columns, dst, sems):
        self.choices = (info[first], info[first + 1])
        self.member, self.half = info[4], info[5]
        self.own, self.stages = own, stages
        self.columns, self.dst, self.sems = columns, dst, sems

    def each(self, act):
        @pl.when(self.choices[0] == 0)
        def _():
            act(pltpu.make_async_copy(self.own.at[0], self.dst, self.sems.at[0]))

        for stage, group in enumerate(self.stages):
            for parity in range(2):

                @pl.when(self.choices[parity] == stage + 1)
                def _(group=group, parity=parity):
                    for kind, refs in group:
                        self.shares(kind, refs, parity, act)

    def shares(self, kind, refs, parity, act):
        group = self.sems.shape[0] // BLOCKS
        block = self.dst.shape[0] // group // BLOCKS
        places = {DIRECT: (self.half, 2), ACROSS: (1 - self.half,), FULL: (0, 1, 2)}[kind]
        sems = {DIRECT: (0, 1), ACROSS: (2,), FULL: (0, 1, 2)}[kind]
        seen = 0
        for ref in refs:
            for n in range(ref.shape[0]):
                if seen % 2 == parity:
                    base = (self.member ^ seen) * BLOCKS
                    for j, place in enumerate(places):
                        start = pl.multiple_of((base + place) * block, block)
                        act(
                            pltpu.make_async_copy(
                                ref.at[n, j * block : (j + 1) * block, self.columns],
                                self.dst.at[pl.ds(start, block)],
                                self.sems.at[seen * BLOCKS + sems[j]],
                            )
                        )
                seen += 1

    def start(self):
        self.each(lambda copy: copy.start())

    def wait(self):
        self.each(lambda copy: copy.wait())


def take_stages(it, layout):
    return [[(kind, [next(it) for _ in range(count)]) for kind, count in group] for group in layout]


def softmax_heads(la, lb, scale, keep):
    seq = la.shape[0]
    for h in range(HEADS):
        at = slice(h * seq, (h + 1) * seq)
        logits = (la[:, at] + lb[:, at]) * scale
        e = jnp.exp(logits - jnp.max(logits, axis=-1, keepdims=True))
        keep(h, e / jnp.sum(e, axis=-1, keepdims=True))


def norm_parts(x):
    centred = x - jnp.mean(x, axis=-1, keepdims=True)
    spread = jnp.mean(centred * centred, axis=-1, keepdims=True)
    rstd = lax.rsqrt(spread + 1e-05)
    return centred * rstd, rstd


def scores(ref_a, first_a, ref_b, first_b, out, out_row, seq, begin):
    parts = [
        mm_nt(head_lanes(ref_a, seq, first_a + h), head_lanes(ref_b, seq, first_b + h))
        for h in range(HEADS)
    ]
    rows = slice(out_row, out_row + seq)

    @pl.when(begin)
    def _():
        for h, part in enumerate(parts):
            out[rows, h * seq : (h + 1) * seq] = part

    @pl.when(jnp.logical_not(begin))
    def _():
        for h, part in enumerate(parts):
            out[rows, h * seq : (h + 1) * seq] += part


def mix(weights, ref_b, first_b, out, first_out, scale, seq):
    width = PACK * HEAD_DIM
    for p in range(HEADS // PACK):
        values = []
        for h in range(p * PACK, (p + 1) * PACK):
            value = mm(weights[:, h * seq : (h + 1) * seq], head_lanes(ref_b, seq, first_b + h))
            values.append((value if scale is None else value * scale).astype(BF16))
        at = first_out + p * width
        for pair in range(ref_b.shape[0] // seq):
            blocks = [value[:, pair * width : (pair + 1) * width] for value in values]
            for n, block in enumerate(regroup(blocks)):
                row = (pair * PACK + n) * seq
                out[row : row + seq, at : at + width] = block


def forward_kernel(has_prev, has_top, info, *refs, layout, scale, seq, width):
    it = iter(refs)
    if has_prev:
        la, lb, v_prev = next(it), next(it), next(it)
    x_in, gain = next(it), next(it)
    top = next(it) if has_top else None
    own_q, own_o = next(it), next(it)
    stages = take_stages(it, layout)
    if has_prev:
        probs_out, x_out = next(it), next(it)
    qkv_out, score_out = next(it), next(it)
    if has_top:
        dmix_out = next(it)
    wq, sem_q = next(it), next(it)
    if has_prev:
        wo, sem_o, mixed = next(it), next(it), next(it)
    if has_top:
        wt, sem_t = next(it), next(it)
    step = pl.program_id(0)
    qcols, ocols = slice(0, 3 * width), slice(3 * width, 4 * width)
    get_q = Weights(info, 0, own_q, stages, qcols, wq, sem_q)
    if has_prev:
        get_o = Weights(info, 2, own_o, stages, ocols, wo, sem_o)
    if has_top:
        get_t = Weights(info, 0, own_o, stages, ocols, wt, sem_t)

    @pl.when(step == 0)
    def _():
        if has_prev:
            get_o.start()
        get_q.start()
        if has_top:
            get_t.start()
        if has_prev:

            def keep(h, value):
                probs_out[:, h * seq : (h + 1) * seq] = value.astype(BF16)

            softmax_heads(la, lb, scale, keep)

    if has_prev:
        mix(probs_out, v_prev, 0, mixed, 0, None, seq)
        pl.when(step == 0)(get_o.wait)
        x = x_in[...] + mm(mixed[...], wo[...])
        x_out[...] = x
    else:
        x = x_in[...]
    hat, _ = norm_parts(x)
    h = (hat * gain[pl.ds(info[6], 1), :]).astype(BF16)
    pl.when(step == 0)(get_q.wait)
    pack_rows(mm(h, wq[...]).astype(BF16), qkv_out, 0, seq)
    begin = step == 0
    scores(qkv_out, 0, qkv_out, HEADS, score_out, 0, seq, begin)
    if has_top:
        pl.when(step == 0)(get_t.wait)
        pack_rows(mm_nt(top[...], wt[...]).astype(BF16), dmix_out, 0, seq)
        scores(dmix_out, 0, qkv_out, 2 * HEADS, score_out, seq, seq, begin)


def add_product(a, b, total, column, step, steps, staged):
    at = slice(column, column + b.shape[1])
    part = lax.dot_general(a, b, TN, preferred_element_type=F32)

    @pl.when(step == 0)
    def _():
        total[:, at] = part

    @pl.when((step > 0) & (step < steps - 1))
    def _():
        total[:, at] += part

    @pl.when(step == steps - 1)
    def _():
        staged[:, at] = ((total[:, at] if steps > 1 else 0.0) + part).astype(staged.dtype)


def logit_grads(probs, sa, sb, first, seq, dl, dlt):
    for h in range(HEADS):
        at = slice(h * seq, (h + 1) * seq)
        prob = probs[:, at].astype(F32)
        d_prob = sa[first : first + seq, at] + sb[first : first + seq, at]
        d_logit = prob * (d_prob - jnp.sum(d_prob * prob, axis=-1, keepdims=True))
        dl[:, at] = d_logit.astype(BF16)
        dlt[:, at] = jnp.transpose(d_logit).astype(BF16)


def turn_probs(probs, seq, pt):
    for h in range(HEADS):
        at = slice(h * seq, (h + 1) * seq)
        pt[:, at] = jnp.transpose(probs[:, at].astype(F32)).astype(BF16)


def ship(staged, keep, send, member, sems):
    count, rows = keep.shape[0], keep.shape[1]
    copies = []
    for n in range(count):
        for k, dst in enumerate((keep, send)):
            start = pl.multiple_of((2 * n + (member + k) % 2) * rows, rows)
            copies.append(
                pltpu.make_async_copy(staged.at[pl.ds(start, rows)], dst.at[n], sems.at[2 * n + k])
            )
    return copies


def run_copies(copies):
    for copy in copies:
        copy.start()
    for copy in copies:
        copy.wait()


def backward_kernel(is_top, info, *refs, layout, scale, seq, width, steps):
    it = iter(refs)
    sa, sb = next(it), next(it)
    if not is_top:
        probs = next(it)
    qkv, dmix, x_in, gains, dy, v_prev = [next(it) for _ in range(6)]
    if not is_top:
        for _ in range(4):
            next(it)
    own_q, own_o = next(it), next(it)
    stages = take_stages(it, layout)
    dy_out, dmix_out, score_out, send_out = [next(it) for _ in range(4)]
    keep_a, send_a, keep_b, send_b = [next(it) for _ in range(4)]
    dl, dlt, pt, dqkv, mixed = [next(it) for _ in range(5)]
    total_a, staged_a, sem_a, total_b, staged_b, sem_b = [next(it) for _ in range(6)]
    wq, sem_q, wo, sem_o = [next(it) for _ in range(4)]
    if is_top:
        probs = next(it)
    step = pl.program_id(0)
    get_q = Weights(info, 0, own_q, stages, slice(0, 3 * width), wq, sem_q)
    get_o = Weights(info, 2, own_o, stages, slice(3 * width, 4 * width), wo, sem_o)
    own = info[0] == 0
    gain = gains[pl.ds(info[6], 1), :]

    @pl.when(step == 0)
    def _():
        get_q.start()
        get_o.start()
        if is_top:

            def keep(h, value):
                probs[:, h * seq : (h + 1) * seq] = value.astype(BF16)

            softmax_heads(sa.at[0:seq], sb.at[0:seq], scale, keep)
        logit_grads(probs, sa, sb, seq if is_top else 0, seq, dl, dlt)
        turn_probs(probs, seq, pt)

    mix(dl, qkv, HEADS, dqkv, 0, scale, seq)
    mix(dlt, qkv, 0, dqkv, width, scale, seq)
    mix(pt, dmix, 0, dqkv, 2 * width, None, seq)
    pl.when(step == 0)(get_q.wait)
    d_hat = mm_nt(dqkv[...], wq[...]).astype(BF16).astype(F32) * gain
    hat, rstd = norm_parts(x_in[...])
    mean_d = jnp.mean(d_hat, axis=-1, keepdims=True)
    mean_dh = jnp.mean(d_hat * hat, axis=-1, keepdims=True)
    d_x = dy[...].astype(F32) + rstd * (d_hat - mean_d - hat * mean_dh)
    dy_out[...] = d_x
    pl.when(step == 0)(get_o.wait)
    pack_rows(mm_nt(d_x.astype(BF16), wo[...]).astype(BF16), dmix_out, 0, seq)
    scores(dmix_out, 0, v_prev, 0, score_out, 0, seq, step == 0)

    @pl.when(step == steps - 1)
    def _():
        send_out[...] = score_out[...].astype(BF16)

    @pl.when(own)
    def _():
        mix(probs, qkv, 2 * HEADS, mixed, 0, None, seq)
        h = (norm_parts(x_in[...])[0] * gain).astype(BF16)
        add_product(mixed[...], dy[...].astype(BF16), total_a, 0, step, steps, staged_a)
        add_product(h, dqkv[:, 2 * width :], total_a, width, step, steps, staged_a)
        add_product(h, dqkv[:, : 2 * width], total_b, 0, step, steps, staged_b)

    @pl.when(own & (step == steps - 1))
    def _():
        copies = ship(staged_a, keep_a, send_a, info[4], sem_a)
        run_copies(copies + ship(staged_b, keep_b, send_b, info[4], sem_b))


def early_kernel(info, *refs, layout, seq, width, steps):
    probs, v, dmix, x_in, gains, dy, _, _, keep, send, pt, mixed, dv, total, staged, sem = refs
    step = pl.program_id(0)
    own = info[0] == 0

    @pl.when(own)
    def _():
        @pl.when(step == 0)
        def _():
            turn_probs(probs, seq, pt)

        mix(probs, v, 0, mixed, 0, None, seq)
        mix(pt, dmix, 0, dv, 0, None, seq)
        h = (norm_parts(x_in[...])[0] * gains[pl.ds(info[6], 1), :]).astype(BF16)
        add_product(mixed[...], dy[...].astype(BF16), total, 0, step, steps, staged)
        add_product(h, dv[...], total, width, step, steps, staged)

    @pl.when(own & (step == steps - 1))
    def _():
        run_copies(ship(staged, keep, send, info[4], sem))


def late_kernel(info, *refs, layout, scale, seq, width, steps):
    sa, sb, probs, qk, x_in, gains, _, _, keep, send, dl, dlt, dqk, total, staged, sem = refs
    step = pl.program_id(0)
    own = info[0] == 0

    @pl.when(own)
    def _():
        @pl.when(step == 0)
        def _():
            logit_grads(probs, sa, sb, 0, seq, dl, dlt)

        mix(dl, qk, HEADS, dqk, 0, scale, seq)
        mix(dlt, qk, 0, dqk, width, scale, seq)
        h = (norm_parts(x_in[...])[0] * gains[pl.ds(info[6], 1), :]).astype(BF16)
        add_product(h, dqk[...], total, 0, step, steps, staged)

    @pl.when(own & (step == steps - 1))
    def _():
        run_copies(ship(staged, keep, send, info[4], sem))


class Chain:
    def __init__(self, fetched, member, n_row, n_group, own, gains, seq, width, rows, scale):
        self.fetched, self.member, self.n_row, self.n_group = fetched, member, n_row, n_group
        self.gains = (gains, self.whole(*gains.shape))
        self.own, self.seq, self.width, self.rows = own, seq, width, rows
        self.scale = scale
        per_step = 4 if rows % 4 == 0 else 2
        self.chunk = per_step * seq
        self.steps = rows // per_step

    def info(self, now, other):
        picks = self.fetched.choices(now) + self.fetched.choices(other)
        picks += [self.member, self.fetched.half, self.fetched.section ^ now]
        return jnp.stack(picks).astype(jnp.int32)

    def whole(self, rows, lanes):
        return pl.BlockSpec((rows, lanes), lambda i, s: (0, 0))

    def tile(self, lanes, column=0, part=1):
        return pl.BlockSpec((self.chunk // part, lanes), lambda i, s: (i, column))

    def packed(self, heads, column=0):
        return self.tile(heads * PACK * HEAD_DIM, column, PACK)

    def call(self, body, name, info, stages, ins, outs, scratch, flops, carried=(), own=None):
        any_spec = pl.BlockSpec(memory_space=pl.ANY)
        groups = self.fetched.stages[:stages]
        weights = list(self.own if own is None else own)
        weights += [a for group in groups for _, arrays in group for a in arrays]
        arrays = [a for a, _ in ins] + list(carried)
        shapes = [o for o, _ in outs]
        size = sum(math.prod(a.shape) * a.dtype.itemsize for a in arrays + shapes)
        aliases = {
            1 + len(ins) + n: len(outs) - len(carried) + n for n in range(len(carried))
        }
        layout = tuple(tuple((kind, len(arrays)) for kind, arrays in group) for group in groups)
        return pl.pallas_call(
            functools.partial(body, layout=layout),
            name=name,
            out_shape=shapes,
            grid_spec=pltpu.PrefetchScalarGridSpec(
                num_scalar_prefetch=1,
                grid=(self.steps,),
                in_specs=[spec for _, spec in ins] + [any_spec] * (len(carried) + len(weights)),
                out_specs=[spec for _, spec in outs],
                scratch_shapes=scratch,
            ),
            input_output_aliases=aliases,
            compiler_params=pltpu.CompilerParams(
                dimension_semantics=("arbitrary",), vmem_limit_bytes=VMEM_LIMIT
            ),
            cost_estimate=pl.CostEstimate(flops=flops, bytes_accessed=size, transcendentals=0),
        )(info, *arrays, *weights)

    def weight_scratch(self, columns):
        return [
            pltpu.VMEM((self.width, columns * self.width), BF16),
            pltpu.SemaphoreType.DMA((self.n_group * BLOCKS,)),
        ]

    def shape(self, rows, lanes, dtype):
        return jax.ShapeDtypeStruct((rows, lanes), dtype)

    def grad_outs(self):
        any_spec = pl.BlockSpec(memory_space=pl.ANY)
        rows = self.width // self.n_row
        shape = (self.n_row // 2, rows, 2 * self.width)
        return [(jax.ShapeDtypeStruct(shape, self.grad_type()), any_spec)] * 2

    def grad_type(self):
        return BF16 if self.width // self.n_row % 16 == 0 else F32

    def grad_scratch(self):
        shape = (self.width, 2 * self.width)
        scratch = [pltpu.VMEM(shape, F32), pltpu.VMEM(shape, self.grad_type())]
        return scratch + [pltpu.SemaphoreType.DMA((self.n_row,))]

    def forward(self, layer, x, prev, top):
        seq, width = self.seq, self.width
        n = self.rows * seq
        hw = HEADS * seq
        score_rows = seq if top is None else 2 * seq
        ins = [(x, self.tile(width)), self.gains]
        outs = [
            (self.shape(n // PACK, 3 * PACK * width, BF16), self.packed(3 * HEADS)),
            (self.shape(score_rows, hw, F32), self.whole(score_rows, hw)),
        ]
        scratch = self.weight_scratch(3)
        if prev is not None:
            ins = [
                (prev[0], self.whole(seq, hw)),
                (prev[1], self.whole(seq, hw)),
                (prev[2], self.packed(HEADS, 2)),
            ] + ins
            outs = [
                (self.shape(seq, hw, BF16), self.whole(seq, hw)),
                (self.shape(n, width, F32), self.tile(width)),
            ] + outs
            scratch += self.weight_scratch(1) + [pltpu.VMEM((self.chunk, width), BF16)]
        if top is not None:
            ins.append((top, self.tile(width)))
            outs.append((self.shape(n // PACK, PACK * width, BF16), self.packed(HEADS)))
            scratch += self.weight_scratch(1)
        body = functools.partial(
            forward_kernel, prev is not None, top is not None, scale=self.scale, seq=seq, width=width
        )
        return self.call(
            body,
            f"layer_in_{layer}",
            self.info(layer, max(layer - 1, 0)),
            self.fetched.first_stages if layer == 0 else None,
            ins,
            outs,
            scratch,
            2 * n * width * width * 5,
        )

    def backward(self, layer, scores, probs, qkv, dmix, x, dy, v_prev, grads):
        seq, width = self.seq, self.width
        n = self.rows * seq
        hw = HEADS * seq
        is_top = probs is None
        score_rows = scores[0].shape[0]
        square = pltpu.VMEM((seq, hw), BF16)
        ins = [(s, self.whole(score_rows, hw)) for s in scores]
        if not is_top:
            ins.append((probs, self.whole(seq, hw)))
        ins += [
            (qkv, self.packed(3 * HEADS)),
            (dmix, self.packed(HEADS)),
            (x, self.tile(width)),
            self.gains,
            (dy, self.tile(width)),
            (v_prev, self.packed(HEADS, 2)),
        ]
        outs = [
            (self.shape(n, width, F32), self.tile(width)),
            (self.shape(n // PACK, PACK * width, BF16), self.packed(HEADS)),
            (self.shape(seq, hw, F32), self.whole(seq, hw)),
            (self.shape(seq, hw, BF16), self.whole(seq, hw)),
            *self.grad_outs(),
            *self.grad_outs(),
        ]
        scratch = [square] * 3
        scratch += [pltpu.VMEM((self.chunk, lanes * width), BF16) for lanes in (3, 1)]
        scratch += self.grad_scratch() * 2 + self.weight_scratch(3) + self.weight_scratch(1)
        if is_top:
            scratch.append(square)
        body = functools.partial(
            backward_kernel, is_top, scale=self.scale, seq=seq, width=width, steps=self.steps
        )
        return self.call(
            body,
            f"layer_back_{layer}",
            self.info(layer, layer - 1),
            None,
            ins,
            outs,
            scratch,
            2 * n * width * width * 5,
            carried=grads,
        )

    def early(self, probs, qkv, dmix, x, dy, grads):
        seq, width = self.seq, self.width
        n, hw = self.rows * seq, HEADS * seq
        ins = [
            (probs, self.whole(seq, hw)),
            (qkv, self.packed(HEADS, 2)),
            (dmix, self.packed(HEADS)),
            (x, self.tile(width)),
            self.gains,
            (dy, self.tile(width)),
        ]
        scratch = [pltpu.VMEM((seq, hw), BF16)] + [pltpu.VMEM((self.chunk, width), BF16)] * 2
        return self.call(
            functools.partial(early_kernel, seq=seq, width=width, steps=self.steps),
            "early_back_0",
            self.info(0, 0),
            0,
            ins,
            self.grad_outs(),
            scratch + self.grad_scratch(),
            2 * n * width * width * 3,
            carried=grads,
            own=(),
        )

    def late(self, scores, probs, qkv, x, grads):
        seq, width = self.seq, self.width
        n, hw = self.rows * seq, HEADS * seq
        ins = [
            (scores[0], self.whole(seq, hw)),
            (scores[1], self.whole(seq, hw)),
            (probs, self.whole(seq, hw)),
            (qkv, self.packed(2 * HEADS)),
            (x, self.tile(width)),
            self.gains,
        ]
        scratch = [pltpu.VMEM((seq, hw), BF16)] * 2 + [pltpu.VMEM((self.chunk, 2 * width), BF16)]
        return self.call(
            functools.partial(
                late_kernel, scale=self.scale, seq=seq, width=width, steps=self.steps
            ),
            "late_back_0",
            self.info(0, 0),
            0,
            ins,
            self.grad_outs(),
            scratch + self.grad_scratch(),
            2 * n * width * width * 3,
            carried=grads,
            own=(),
        )


def group_swap(value, send, n_row, n_group):
    other = jnp.zeros_like(send)
    bit = 1
    while bit < n_group:
        if bit > 1:
            value = value + other
            send = value.astype(send.dtype)
        other = lax.ppermute(send, "row", [(r, r ^ bit) for r in range(n_row)])
        bit *= 2
    return value, other


class RowSum:
    def __init__(self, keep, send, place, n_row):
        self.keep, self.send, self.place, self.n_row, self.bit = keep, send, place, n_row, 1

    def step(self):
        perm = [(r, r ^ self.bit) for r in range(self.n_row)]
        other = lax.ppermute(self.send.astype(BF16), "row", perm)
        value = self.keep.astype(F32) + other.astype(F32)
        self.bit *= 2
        if self.bit == self.n_row:
            return value[0]
        mine = self.place // self.bit % 2
        pair = value.reshape(value.shape[0] // 2, 2, *value.shape[1:])
        self.keep = lax.dynamic_index_in_dim(pair, mine, 1, keepdims=False)
        self.send = lax.dynamic_index_in_dim(pair, 1 - mine, 1, keepdims=False).astype(BF16)
        return None

    def finish(self):
        value = None
        while value is None:
            value = self.step()
        return value


class Fetched:
    first_stages = 2

    def __init__(self, wqkv, wout, section, place, n_section, n_row, n_group):
        assert n_section == 4 and n_group % 2 == 0
        self.section, self.n_row, self.n_group = section, n_row, n_group
        self.member, self.half = place % n_group, place // n_group % 2
        self.last = n_section - 1
        self.block = wqkv.shape[0] // n_group // BLOCKS
        self.own = (wqkv, wout)
        self.to_last = section == (self.last ^ jnp.where(self.member % 2 == 0, 2, 1))
        self.mine = jnp.concatenate([self.own_block(self.half), self.own_block(2)], axis=0)
        self.got = self.hop(self.mine, 1)
        self.across = self.cross(self.got)
        self.stages = [self.halves(self.got, self.across)]

    def own_block(self, place, count=1):
        start = (self.member * BLOCKS + place) * self.block
        rows = [lax.dynamic_slice_in_dim(w, start, count * self.block, 0) for w in self.own]
        return jnp.concatenate(rows, axis=1)

    def hop(self, value, even_bit):
        perm = [
            (s * self.n_row + r, (s ^ (even_bit if r % 2 == 0 else 3 - even_bit)) * self.n_row + r)
            for s in range(self.last + 1)
            for r in range(self.n_row)
        ]
        return lax.ppermute(value, ("section", "row"), perm)

    def cross(self, value):
        perm = [(r, r ^ self.n_group) for r in range(self.n_row)]
        return lax.ppermute(value[: self.block], "row", perm)

    def halves(self, got, across):
        return [(DIRECT, self.share(got)), (ACROSS, self.share(across))]

    def second(self, x):
        second, x = lax.optimization_barrier((jnp.where(self.to_last, self.got, self.mine), x))
        second = self.hop(second, 2)
        self.stages.append(self.halves(second, self.cross(second)))
        low = jnp.where(self.half == 0, self.got[: self.block], self.across)
        high = jnp.where(self.half == 0, self.across, self.got[: self.block])
        relayed = jnp.concatenate([low, high, self.got[self.block :]], axis=0)
        third = jnp.where(self.to_last, self.own_block(0, BLOCKS), relayed)
        self.third = self.hop(third, 2)
        return x

    def finish(self, ready):
        third, ready = lax.optimization_barrier((self.third, ready))
        self.stages.append([(FULL, self.share(third))])
        return ready

    def share(self, value):
        have = [value[None]]
        bit = 1
        while bit < self.n_group:
            send = have[0] if len(have) == 1 else jnp.concatenate(have, axis=0)
            have.append(lax.ppermute(send, "row", [(r, r ^ bit) for r in range(self.n_row)]))
            bit *= 2
        return have

    def choices(self, layer):
        offset = self.section ^ layer
        at_last = self.section == self.last
        picks = []
        for parity in (self.member % 2, 1 - self.member % 2):
            first = jnp.where(parity == 0, 1, 2)
            second = jnp.where(at_last, 3, 3 - first)
            pick = jnp.where(offset == first, 1, jnp.where(offset == second, 2, 3))
            picks.append(jnp.where(offset == 0, 0, pick))
        return picks


def local(tokens, embed, ln_gain, w_qkv, w_out, out_grad):
    n_section = lax.axis_size("section")
    n_row = lax.axis_size("row")
    section = lax.axis_index("section")
    place = lax.axis_index("row")
    micro, rows_here, seq = tokens.shape
    width = embed.shape[1]
    n_group = n_row // micro
    member = place % n_group
    rows = rows_here * micro
    scale = HEAD_DIM ** (-0.5) / math.sqrt(rows_here * n_row)
    fetched = Fetched(w_qkv[0], w_out[0], section, place, n_section, n_row, n_group)
    same = [[m * n_group + g for m in range(micro)] for g in range(n_group)]
    exchange = functools.partial(
        lax.all_to_all,
        axis_name="row",
        split_axis=0,
        concat_axis=0,
        axis_index_groups=same,
        tiled=True,
    )
    tok = exchange(tokens).reshape(-1)
    top_grad = exchange(out_grad).reshape(rows * seq, width)
    gains = jnp.concatenate(
        [ln_gain]
        + [
            lax.ppermute(ln_gain, "section", [(s, s ^ offset) for s in range(n_section)])
            for offset in range(1, n_section)
        ],
        axis=0,
    )
    table = (jnp.arange(embed.shape[0], dtype=jnp.int32)[:, None] == tok[None, :]).astype(BF16)
    x = lax.dot_general(table, embed, TN, preferred_element_type=F32)

    x, gains = fetched.second((x, gains))
    chain = Chain(
        fetched, member, n_row, n_group, (w_qkv, w_out), gains, seq, width, rows, scale
    )
    xs, qkvs, probs = [], [], []
    scores = None
    dmix = None
    for layer in range(n_section):
        prev = None if layer == 0 else (*scores, qkvs[-1])
        top = top_grad if layer == n_section - 1 else None
        outs = list(chain.forward(layer, x, prev, top))
        if prev is not None:
            probs.append(outs.pop(0))
            x = outs.pop(0)
        xs.append(x)
        qkvs.append(outs[0])
        if top is not None:
            dmix = outs[2]
        scores = group_swap(outs[1], outs[1], n_row, n_group)
        if layer == 0:
            scores = (scores[0], fetched.finish(scores[1]))
    probs.append(None)

    dy = top_grad
    grads = ()
    for layer in range(n_section - 1, 0, -1):
        dy, dmix, part, send, *grads = chain.backward(
            layer,
            scores,
            probs[layer],
            qkvs[layer],
            dmix,
            xs[layer],
            dy,
            qkvs[layer - 1],
            grads,
        )
        scores = group_swap(part, send, n_row, n_group)
    early = RowSum(*chain.early(probs[0], qkvs[0], dmix, xs[0], dy, grads[:2]), place, n_row)
    early.step()
    early.send, other = lax.optimization_barrier((early.send, scores[1]))
    late = chain.late((scores[0], other), probs[0], qkvs[0], xs[0], grads[2:])
    g_early = early.finish()
    g_late = RowSum(*late, place, n_row).finish()
    g_qkv = jnp.concatenate([g_late, g_early[:, width:]], axis=1)
    block = width // n_row
    w_here = lax.dynamic_slice_in_dim(w_qkv[0], place * block, block, 0).astype(F32)
    gain_here = lax.dynamic_slice_in_dim(ln_gain, place * block, block, 1)
    g_gain = jnp.sum(g_qkv * w_here, axis=1)[None] / gain_here
    return (g_qkv[None], g_early[None, :, :width], g_gain)


def solution(mesh):
    in_specs = (
        P(None, "row", None),
        P(),
        P("section", None),
        P("section", None, None),
        P("section", None, None),
        P(None, "row", None, None),
    )
    out_specs = (P("section", "row", None), P("section", "row", None), P("section", "row"))
    return jax.shard_map(local, mesh=mesh, in_specs=in_specs, out_specs=out_specs, check_vma=False)
```

```python
import functools
import math

import jax
import jax.numpy as jnp
from jax import lax
from jax.experimental import pallas as pl
from jax.experimental.pallas import tpu as pltpu
from jax.sharding import PartitionSpec as P

HEADS = 12
HEAD_DIM = 64
PACK = 2
BLOCKS = 3
DIRECT, ACROSS, FULL = range(3)
F32 = jnp.float32
BF16 = jnp.bfloat16
VMEM_LIMIT = 60 * 1024 * 1024
NT = (((1,), (1,)), ((), ()))
TN = (((0,), (0,)), ((), ()))


def mm(a, b):
    return jnp.dot(a, b, preferred_element_type=F32)


def mm_nt(a, b):
    return lax.dot_general(a, b, NT, preferred_element_type=F32)


def head_lanes(ref, seq, head):
    width = PACK * HEAD_DIM
    first = head * width
    return jnp.concatenate(
        [ref[r * seq : (r + 1) * seq, first : first + width] for r in range(ref.shape[0] // seq)],
        axis=1,
    )


def regroup(blocks):
    return [
        jnp.concatenate([block[:, n * HEAD_DIM : (n + 1) * HEAD_DIM] for block in blocks], axis=1)
        for n in range(PACK)
    ]


def pack_rows(value, out, first, seq):
    width = PACK * HEAD_DIM
    for pair in range(value.shape[0] // seq // PACK):
        for p in range(value.shape[1] // width):
            blocks = [
                value[(pair * PACK + r) * seq : (pair * PACK + r + 1) * seq, p * width : (p + 1) * width]
                for r in range(PACK)
            ]
            for n, block in enumerate(regroup(blocks)):
                at = (first + p * PACK + n) * width
                out[pair * seq : (pair + 1) * seq, at : at + width] = block


class Weights:
    def __init__(self, info, first, own, stages, columns, dst, sems):
        self.choices = (info[first], info[first + 1])
        self.member, self.half = info[4], info[5]
        self.own, self.stages = own, stages
        self.columns, self.dst, self.sems = columns, dst, sems

    def each(self, act):
        @pl.when(self.choices[0] == 0)
        def _():
            act(pltpu.make_async_copy(self.own.at[0], self.dst, self.sems.at[0]))

        for stage, group in enumerate(self.stages):
            for parity in range(2):

                @pl.when(self.choices[parity] == stage + 1)
                def _(group=group, parity=parity):
                    for kind, refs in group:
                        self.shares(kind, refs, parity, act)

    def shares(self, kind, refs, parity, act):
        group = self.sems.shape[0] // BLOCKS
        block = self.dst.shape[0] // group // BLOCKS
        places = {DIRECT: (self.half, 2), ACROSS: (1 - self.half,), FULL: (0, 1, 2)}[kind]
        sems = {DIRECT: (0, 1), ACROSS: (2,), FULL: (0, 1, 2)}[kind]
        seen = 0
        for ref in refs:
            for n in range(ref.shape[0]):
                if seen % 2 == parity:
                    base = (self.member ^ seen) * BLOCKS
                    for j, place in enumerate(places):
                        start = pl.multiple_of((base + place) * block, block)
                        act(
                            pltpu.make_async_copy(
                                ref.at[n, j * block : (j + 1) * block, self.columns],
                                self.dst.at[pl.ds(start, block)],
                                self.sems.at[seen * BLOCKS + sems[j]],
                            )
                        )
                seen += 1

    def start(self):
        self.each(lambda copy: copy.start())

    def wait(self):
        self.each(lambda copy: copy.wait())


def take_stages(it, layout):
    return [[(kind, [next(it) for _ in range(count)]) for kind, count in group] for group in layout]


def softmax_heads(la, lb, scale, keep):
    seq = la.shape[0]
    for h in range(HEADS):
        at = slice(h * seq, (h + 1) * seq)
        logits = (la[:, at] + lb[:, at]) * scale
        e = jnp.exp(logits - jnp.max(logits, axis=-1, keepdims=True))
        keep(h, e / jnp.sum(e, axis=-1, keepdims=True))


def norm_parts(x):
    centred = x - jnp.mean(x, axis=-1, keepdims=True)
    spread = jnp.mean(centred * centred, axis=-1, keepdims=True)
    rstd = lax.rsqrt(spread + 1e-05)
    return centred * rstd, rstd


def scores(ref_a, first_a, ref_b, first_b, out, out_row, seq, begin):
    parts = [
        mm_nt(head_lanes(ref_a, seq, first_a + h), head_lanes(ref_b, seq, first_b + h))
        for h in range(HEADS)
    ]
    rows = slice(out_row, out_row + seq)

    @pl.when(begin)
    def _():
        for h, part in enumerate(parts):
            out[rows, h * seq : (h + 1) * seq] = part

    @pl.when(jnp.logical_not(begin))
    def _():
        for h, part in enumerate(parts):
            out[rows, h * seq : (h + 1) * seq] += part


def mix(weights, ref_b, first_b, out, first_out, scale, seq):
    width = PACK * HEAD_DIM
    for p in range(HEADS // PACK):
        values = []
        for h in range(p * PACK, (p + 1) * PACK):
            value = mm(weights[:, h * seq : (h + 1) * seq], head_lanes(ref_b, seq, first_b + h))
            values.append((value if scale is None else value * scale).astype(BF16))
        at = first_out + p * width
        for pair in range(ref_b.shape[0] // seq):
            blocks = [value[:, pair * width : (pair + 1) * width] for value in values]
            for n, block in enumerate(regroup(blocks)):
                row = (pair * PACK + n) * seq
                out[row : row + seq, at : at + width] = block


def forward_kernel(has_prev, has_top, info, *refs, layout, scale, seq, width):
    it = iter(refs)
    if has_prev:
        la, lb, v_prev = next(it), next(it), next(it)
    x_in, gain = next(it), next(it)
    top = next(it) if has_top else None
    own_q, own_o = next(it), next(it)
    stages = take_stages(it, layout)
    if has_prev:
        probs_out, x_out = next(it), next(it)
    qkv_out, score_out = next(it), next(it)
    if has_top:
        dmix_out = next(it)
    wq, sem_q = next(it), next(it)
    if has_prev:
        wo, sem_o, mixed = next(it), next(it), next(it)
    if has_top:
        wt, sem_t = next(it), next(it)
    step = pl.program_id(0)
    qcols, ocols = slice(0, 3 * width), slice(3 * width, 4 * width)
    get_q = Weights(info, 0, own_q, stages, qcols, wq, sem_q)
    if has_prev:
        get_o = Weights(info, 2, own_o, stages, ocols, wo, sem_o)
    if has_top:
        get_t = Weights(info, 0, own_o, stages, ocols, wt, sem_t)

    @pl.when(step == 0)
    def _():
        if has_prev:
            get_o.start()
        get_q.start()
        if has_top:
            get_t.start()
        if has_prev:

            def keep(h, value):
                probs_out[:, h * seq : (h + 1) * seq] = value.astype(BF16)

            softmax_heads(la, lb, scale, keep)

    if has_prev:
        mix(probs_out, v_prev, 0, mixed, 0, None, seq)
        pl.when(step == 0)(get_o.wait)
        x = x_in[...] + mm(mixed[...], wo[...])
        x_out[...] = x
    else:
        x = x_in[...]
    hat, _ = norm_parts(x)
    h = (hat * gain[pl.ds(info[6], 1), :]).astype(BF16)
    pl.when(step == 0)(get_q.wait)
    pack_rows(mm(h, wq[...]).astype(BF16), qkv_out, 0, seq)
    begin = step == 0
    scores(qkv_out, 0, qkv_out, HEADS, score_out, 0, seq, begin)
    if has_top:
        pl.when(step == 0)(get_t.wait)
        pack_rows(mm_nt(top[...], wt[...]).astype(BF16), dmix_out, 0, seq)
        scores(dmix_out, 0, qkv_out, 2 * HEADS, score_out, seq, seq, begin)


def add_product(a, b, total, column, step, steps, staged):
    at = slice(column, column + b.shape[1])
    part = lax.dot_general(a, b, TN, preferred_element_type=F32)

    @pl.when(step == 0)
    def _():
        total[:, at] = part

    @pl.when((step > 0) & (step < steps - 1))
    def _():
        total[:, at] += part

    @pl.when(step == steps - 1)
    def _():
        staged[:, at] = ((total[:, at] if steps > 1 else 0.0) + part).astype(staged.dtype)


def logit_grads(probs, sa, sb, first, seq, dl, dlt):
    for h in range(HEADS):
        at = slice(h * seq, (h + 1) * seq)
        prob = probs[:, at].astype(F32)
        d_prob = sa[first : first + seq, at] + sb[first : first + seq, at]
        d_logit = prob * (d_prob - jnp.sum(d_prob * prob, axis=-1, keepdims=True))
        dl[:, at] = d_logit.astype(BF16)
        dlt[:, at] = jnp.transpose(d_logit).astype(BF16)


def turn_probs(probs, seq, pt):
    for h in range(HEADS):
        at = slice(h * seq, (h + 1) * seq)
        pt[:, at] = jnp.transpose(probs[:, at].astype(F32)).astype(BF16)


def ship(staged, keep, send, member, sems):
    count, rows = keep.shape[0], keep.shape[1]
    copies = []
    for n in range(count):
        for k, dst in enumerate((keep, send)):
            start = pl.multiple_of((2 * n + (member + k) % 2) * rows, rows)
            copies.append(
                pltpu.make_async_copy(staged.at[pl.ds(start, rows)], dst.at[n], sems.at[2 * n + k])
            )
    return copies


def run_copies(copies):
    for copy in copies:
        copy.start()
    for copy in copies:
        copy.wait()


def backward_kernel(is_top, info, *refs, layout, scale, seq, width, steps):
    it = iter(refs)
    sa, sb = next(it), next(it)
    if not is_top:
        probs = next(it)
    qkv, dmix, x_in, gains, dy, v_prev = [next(it) for _ in range(6)]
    if not is_top:
        for _ in range(4):
            next(it)
    own_q, own_o = next(it), next(it)
    stages = take_stages(it, layout)
    dy_out, dmix_out, score_out, send_out = [next(it) for _ in range(4)]
    keep_a, send_a, keep_b, send_b = [next(it) for _ in range(4)]
    dl, dlt, pt, dqkv, mixed = [next(it) for _ in range(5)]
    total_a, staged_a, sem_a, total_b, staged_b, sem_b = [next(it) for _ in range(6)]
    wq, sem_q, wo, sem_o = [next(it) for _ in range(4)]
    if is_top:
        probs = next(it)
    step = pl.program_id(0)
    get_q = Weights(info, 0, own_q, stages, slice(0, 3 * width), wq, sem_q)
    get_o = Weights(info, 2, own_o, stages, slice(3 * width, 4 * width), wo, sem_o)
    own = info[0] == 0
    gain = gains[pl.ds(info[6], 1), :]

    @pl.when(step == 0)
    def _():
        get_q.start()
        get_o.start()
        if is_top:

            def keep(h, value):
                probs[:, h * seq : (h + 1) * seq] = value.astype(BF16)

            softmax_heads(sa.at[0:seq], sb.at[0:seq], scale, keep)
        logit_grads(probs, sa, sb, seq if is_top else 0, seq, dl, dlt)
        turn_probs(probs, seq, pt)

    mix(dl, qkv, HEADS, dqkv, 0, scale, seq)
    mix(dlt, qkv, 0, dqkv, width, scale, seq)
    mix(pt, dmix, 0, dqkv, 2 * width, None, seq)
    pl.when(step == 0)(get_q.wait)
    d_hat = mm_nt(dqkv[...], wq[...]).astype(BF16).astype(F32) * gain
    hat, rstd = norm_parts(x_in[...])
    mean_d = jnp.mean(d_hat, axis=-1, keepdims=True)
    mean_dh = jnp.mean(d_hat * hat, axis=-1, keepdims=True)
    d_x = dy[...].astype(F32) + rstd * (d_hat - mean_d - hat * mean_dh)
    dy_out[...] = d_x
    pl.when(step == 0)(get_o.wait)
    pack_rows(mm_nt(d_x.astype(BF16), wo[...]).astype(BF16), dmix_out, 0, seq)
    scores(dmix_out, 0, v_prev, 0, score_out, 0, seq, step == 0)

    @pl.when(step == steps - 1)
    def _():
        send_out[...] = score_out[...].astype(BF16)

    @pl.when(own)
    def _():
        mix(probs, qkv, 2 * HEADS, mixed, 0, None, seq)
        h = (norm_parts(x_in[...])[0] * gain).astype(BF16)
        add_product(mixed[...], dy[...].astype(BF16), total_a, 0, step, steps, staged_a)
        add_product(h, dqkv[:, 2 * width :], total_a, width, step, steps, staged_a)
        add_product(h, dqkv[:, : 2 * width], total_b, 0, step, steps, staged_b)

    @pl.when(own & (step == steps - 1))
    def _():
        copies = ship(staged_a, keep_a, send_a, info[4], sem_a)
        run_copies(copies + ship(staged_b, keep_b, send_b, info[4], sem_b))


def early_kernel(info, *refs, layout, seq, width, steps):
    probs, v, dmix, x_in, gains, dy, _, _, keep, send, pt, mixed, dv, total, staged, sem = refs
    step = pl.program_id(0)
    own = info[0] == 0

    @pl.when(own)
    def _():
        @pl.when(step == 0)
        def _():
            turn_probs(probs, seq, pt)

        mix(probs, v, 0, mixed, 0, None, seq)
        mix(pt, dmix, 0, dv, 0, None, seq)
        h = (norm_parts(x_in[...])[0] * gains[pl.ds(info[6], 1), :]).astype(BF16)
        add_product(mixed[...], dy[...].astype(BF16), total, 0, step, steps, staged)
        add_product(h, dv[...], total, width, step, steps, staged)

    @pl.when(own & (step == steps - 1))
    def _():
        run_copies(ship(staged, keep, send, info[4], sem))


def late_kernel(info, *refs, layout, scale, seq, width, steps):
    sa, sb, probs, qk, x_in, gains, _, _, keep, send, dl, dlt, dqk, total, staged, sem = refs
    step = pl.program_id(0)
    own = info[0] == 0

    @pl.when(own)
    def _():
        @pl.when(step == 0)
        def _():
            logit_grads(probs, sa, sb, 0, seq, dl, dlt)

        mix(dl, qk, HEADS, dqk, 0, scale, seq)
        mix(dlt, qk, 0, dqk, width, scale, seq)
        h = (norm_parts(x_in[...])[0] * gains[pl.ds(info[6], 1), :]).astype(BF16)
        add_product(h, dqk[...], total, 0, step, steps, staged)

    @pl.when(own & (step == steps - 1))
    def _():
        run_copies(ship(staged, keep, send, info[4], sem))


class Chain:
    def __init__(self, fetched, member, n_row, n_group, own, gains, seq, width, rows, scale):
        self.fetched, self.member, self.n_row, self.n_group = fetched, member, n_row, n_group
        self.gains = (gains, self.whole(*gains.shape))
        self.own, self.seq, self.width, self.rows = own, seq, width, rows
        self.scale = scale
        per_step = 4 if rows % 4 == 0 else 2
        self.chunk = per_step * seq
        self.steps = rows // per_step

    def info(self, now, other):
        picks = self.fetched.choices(now) + self.fetched.choices(other)
        picks += [self.member, self.fetched.half, self.fetched.section ^ now]
        return jnp.stack(picks).astype(jnp.int32)

    def whole(self, rows, lanes):
        return pl.BlockSpec((rows, lanes), lambda i, s: (0, 0))

    def tile(self, lanes, column=0, part=1):
        return pl.BlockSpec((self.chunk // part, lanes), lambda i, s: (i, column))

    def packed(self, heads, column=0):
        return self.tile(heads * PACK * HEAD_DIM, column, PACK)

    def call(self, body, name, info, stages, ins, outs, scratch, flops, carried=(), own=None):
        any_spec = pl.BlockSpec(memory_space=pl.ANY)
        groups = self.fetched.stages[:stages]
        weights = list(self.own if own is None else own)
        weights += [a for group in groups for _, arrays in group for a in arrays]
        arrays = [a for a, _ in ins] + list(carried)
        shapes = [o for o, _ in outs]
        size = sum(math.prod(a.shape) * a.dtype.itemsize for a in arrays + shapes)
        aliases = {
            1 + len(ins) + n: len(outs) - len(carried) + n for n in range(len(carried))
        }
        layout = tuple(tuple((kind, len(arrays)) for kind, arrays in group) for group in groups)
        return pl.pallas_call(
            functools.partial(body, layout=layout),
            name=name,
            out_shape=shapes,
            grid_spec=pltpu.PrefetchScalarGridSpec(
                num_scalar_prefetch=1,
                grid=(self.steps,),
                in_specs=[spec for _, spec in ins] + [any_spec] * (len(carried) + len(weights)),
                out_specs=[spec for _, spec in outs],
                scratch_shapes=scratch,
            ),
            input_output_aliases=aliases,
            compiler_params=pltpu.CompilerParams(
                dimension_semantics=("arbitrary",), vmem_limit_bytes=VMEM_LIMIT
            ),
            cost_estimate=pl.CostEstimate(flops=flops, bytes_accessed=size, transcendentals=0),
        )(info, *arrays, *weights)

    def weight_scratch(self, columns):
        return [
            pltpu.VMEM((self.width, columns * self.width), BF16),
            pltpu.SemaphoreType.DMA((self.n_group * BLOCKS,)),
        ]

    def shape(self, rows, lanes, dtype):
        return jax.ShapeDtypeStruct((rows, lanes), dtype)

    def grad_outs(self):
        any_spec = pl.BlockSpec(memory_space=pl.ANY)
        rows = self.width // self.n_row
        shape = (self.n_row // 2, rows, 2 * self.width)
        return [(jax.ShapeDtypeStruct(shape, self.grad_type()), any_spec)] * 2

    def grad_type(self):
        return BF16 if self.width // self.n_row % 16 == 0 else F32

    def grad_scratch(self):
        shape = (self.width, 2 * self.width)
        scratch = [pltpu.VMEM(shape, F32), pltpu.VMEM(shape, self.grad_type())]
        return scratch + [pltpu.SemaphoreType.DMA((self.n_row,))]

    def forward(self, layer, x, prev, top):
        seq, width = self.seq, self.width
        n = self.rows * seq
        hw = HEADS * seq
        score_rows = seq if top is None else 2 * seq
        ins = [(x, self.tile(width)), self.gains]
        outs = [
            (self.shape(n // PACK, 3 * PACK * width, BF16), self.packed(3 * HEADS)),
            (self.shape(score_rows, hw, F32), self.whole(score_rows, hw)),
        ]
        scratch = self.weight_scratch(3)
        if prev is not None:
            ins = [
                (prev[0], self.whole(seq, hw)),
                (prev[1], self.whole(seq, hw)),
                (prev[2], self.packed(HEADS, 2)),
            ] + ins
            outs = [
                (self.shape(seq, hw, BF16), self.whole(seq, hw)),
                (self.shape(n, width, F32), self.tile(width)),
            ] + outs
            scratch += self.weight_scratch(1) + [pltpu.VMEM((self.chunk, width), BF16)]
        if top is not None:
            ins.append((top, self.tile(width)))
            outs.append((self.shape(n // PACK, PACK * width, BF16), self.packed(HEADS)))
            scratch += self.weight_scratch(1)
        body = functools.partial(
            forward_kernel, prev is not None, top is not None, scale=self.scale, seq=seq, width=width
        )
        return self.call(
            body,
            f"layer_in_{layer}",
            self.info(layer, max(layer - 1, 0)),
            self.fetched.first_stages if layer == 0 else None,
            ins,
            outs,
            scratch,
            2 * n * width * width * 5,
        )

    def backward(self, layer, scores, probs, qkv, dmix, x, dy, v_prev, grads):
        seq, width = self.seq, self.width
        n = self.rows * seq
        hw = HEADS * seq
        is_top = probs is None
        score_rows = scores[0].shape[0]
        square = pltpu.VMEM((seq, hw), BF16)
        ins = [(s, self.whole(score_rows, hw)) for s in scores]
        if not is_top:
            ins.append((probs, self.whole(seq, hw)))
        ins += [
            (qkv, self.packed(3 * HEADS)),
            (dmix, self.packed(HEADS)),
            (x, self.tile(width)),
            self.gains,
            (dy, self.tile(width)),
            (v_prev, self.packed(HEADS, 2)),
        ]
        outs = [
            (self.shape(n, width, F32), self.tile(width)),
            (self.shape(n // PACK, PACK * width, BF16), self.packed(HEADS)),
            (self.shape(seq, hw, F32), self.whole(seq, hw)),
            (self.shape(seq, hw, BF16), self.whole(seq, hw)),
            *self.grad_outs(),
            *self.grad_outs(),
        ]
        scratch = [square] * 3
        scratch += [pltpu.VMEM((self.chunk, lanes * width), BF16) for lanes in (3, 1)]
        scratch += self.grad_scratch() * 2 + self.weight_scratch(3) + self.weight_scratch(1)
        if is_top:
            scratch.append(square)
        body = functools.partial(
            backward_kernel, is_top, scale=self.scale, seq=seq, width=width, steps=self.steps
        )
        return self.call(
            body,
            f"layer_back_{layer}",
            self.info(layer, layer - 1),
            None,
            ins,
            outs,
            scratch,
            2 * n * width * width * 5,
            carried=grads,
        )

    def early(self, probs, qkv, dmix, x, dy, grads):
        seq, width = self.seq, self.width
        n, hw = self.rows * seq, HEADS * seq
        ins = [
            (probs, self.whole(seq, hw)),
            (qkv, self.packed(HEADS, 2)),
            (dmix, self.packed(HEADS)),
            (x, self.tile(width)),
            self.gains,
            (dy, self.tile(width)),
        ]
        scratch = [pltpu.VMEM((seq, hw), BF16)] + [pltpu.VMEM((self.chunk, width), BF16)] * 2
        return self.call(
            functools.partial(early_kernel, seq=seq, width=width, steps=self.steps),
            "early_back_0",
            self.info(0, 0),
            0,
            ins,
            self.grad_outs(),
            scratch + self.grad_scratch(),
            2 * n * width * width * 3,
            carried=grads,
            own=(),
        )

    def late(self, scores, probs, qkv, x, grads):
        seq, width = self.seq, self.width
        n, hw = self.rows * seq, HEADS * seq
        ins = [
            (scores[0], self.whole(seq, hw)),
            (scores[1], self.whole(seq, hw)),
            (probs, self.whole(seq, hw)),
            (qkv, self.packed(2 * HEADS)),
            (x, self.tile(width)),
            self.gains,
        ]
        scratch = [pltpu.VMEM((seq, hw), BF16)] * 2 + [pltpu.VMEM((self.chunk, 2 * width), BF16)]
        return self.call(
            functools.partial(
                late_kernel, scale=self.scale, seq=seq, width=width, steps=self.steps
            ),
            "late_back_0",
            self.info(0, 0),
            0,
            ins,
            self.grad_outs(),
            scratch + self.grad_scratch(),
            2 * n * width * width * 3,
            carried=grads,
            own=(),
        )


def group_swap(value, send, n_row, n_group):
    other = jnp.zeros_like(send)
    bit = 1
    while bit < n_group:
        if bit > 1:
            value = value + other
            send = value.astype(send.dtype)
        other = lax.ppermute(send, "row", [(r, r ^ bit) for r in range(n_row)])
        bit *= 2
    return value, other


class RowSum:
    def __init__(self, keep, send, place, n_row):
        self.keep, self.send, self.place, self.n_row, self.bit = keep, send, place, n_row, 1

    def exchange(self):
        perm = [(r, r ^ self.bit) for r in range(self.n_row)]
        return lax.ppermute(self.send.astype(BF16), "row", perm)

    def add(self, other):
        value = self.keep.astype(F32) + other.astype(F32)
        self.bit *= 2
        if self.bit == self.n_row:
            return value[0]
        mine = self.place // self.bit % 2
        pair = value.reshape(value.shape[0] // 2, 2, *value.shape[1:])
        self.keep = lax.dynamic_index_in_dim(pair, mine, 1, keepdims=False)
        self.send = lax.dynamic_index_in_dim(pair, 1 - mine, 1, keepdims=False).astype(BF16)
        return None

    def finish(self):
        value = None
        while value is None:
            value = self.add(self.exchange())
        return value


def copy_call(body, name, scalars, outs, arrays):
    any_spec = pl.BlockSpec(memory_space=pl.ANY)
    return pl.pallas_call(
        body,
        name=name,
        out_shape=outs,
        grid_spec=pltpu.PrefetchScalarGridSpec(
            num_scalar_prefetch=1,
            grid=(1,),
            in_specs=[any_spec] * len(arrays),
            out_specs=[any_spec] * len(outs),
            scratch_shapes=[pltpu.SemaphoreType.DMA((2 * BLOCKS + 1,))],
        ),
        compiler_params=pltpu.CompilerParams(vmem_limit_bytes=VMEM_LIMIT),
        cost_estimate=pl.CostEstimate(flops=0, bytes_accessed=0, transcendentals=0),
    )(jnp.stack(scalars).astype(jnp.int32), *arrays)


def own_blocks(own, places, block, out, sems):
    copies, column = [], 0
    for k, ref in enumerate(own):
        columns = ref.shape[2]
        for n, place in enumerate(places):
            start = pl.multiple_of(place * block, block)
            copies.append(
                pltpu.make_async_copy(
                    ref.at[0, pl.ds(start, block)],
                    out.at[n * block : (n + 1) * block, column : column + columns],
                    sems.at[2 * n + k],
                )
            )
        column += columns
    return copies


def first_kernel(block, info, own_q, own_o, out, sems):
    base = info[0] * BLOCKS
    run_copies(own_blocks((own_q, own_o), (base + info[1], base + 2), block, out, sems))


def second_kernel(block, info, got, mine, *refs):
    out, cross, sems = refs[-3:]
    copy = pltpu.make_async_copy(got.at[:block], cross, sems.at[1])
    copy.start()
    for flag, source in ((1, got), (0, mine)):

        @pl.when(info[2] == flag)
        def _(source=source):
            run_copies([pltpu.make_async_copy(source, out, sems.at[0])])

    copy.wait()


def third_kernel(block, info, got, across, own_q, own_o, second, out, cross, sems):
    copy = pltpu.make_async_copy(second.at[:block], cross, sems.at[2 * BLOCKS])
    copy.start()

    @pl.when(info[2] == 1)
    def _():
        base = info[0] * BLOCKS
        places = [base + n for n in range(BLOCKS)]
        run_copies(own_blocks((own_q, own_o), places, block, out, sems))

    @pl.when(info[2] == 0)
    def _():
        copies = []
        for n, (source, place) in enumerate(
            ((got.at[:block], info[1]), (across, 1 - info[1]), (got.at[block:], 2))
        ):
            start = pl.multiple_of(place * block, block)
            copies.append(pltpu.make_async_copy(source, out.at[pl.ds(start, block)], sems.at[n]))
        run_copies(copies)

    copy.wait()


class Fetched:
    first_stages = 2

    def __init__(self, own, section, place, n_section, n_row, n_group):
        assert n_section == 4 and n_group % 2 == 0
        self.section, self.n_row, self.n_group = section, n_row, n_group
        self.member, self.half = place % n_group, place // n_group % 2
        self.last = n_section - 1
        self.block = own[0].shape[1] // n_group // BLOCKS
        self.own = own
        to_last = section == (self.last ^ jnp.where(self.member % 2 == 0, 2, 1))
        self.scalars = [self.member, self.half, to_last]
        (self.mine,) = self.copies(first_kernel, "share_first", [2], own)
        self.got = self.hop(self.mine, 1)

    def copies(self, body, name, blocks, arrays):
        columns = sum(w.shape[2] for w in self.own)
        outs = [jax.ShapeDtypeStruct((n * self.block, columns), BF16) for n in blocks]
        body = functools.partial(body, self.block)
        return copy_call(body, name, self.scalars, outs, arrays)

    def hop(self, value, even_bit):
        perm = [
            (s * self.n_row + r, (s ^ (even_bit if r % 2 == 0 else 3 - even_bit)) * self.n_row + r)
            for s in range(self.last + 1)
            for r in range(self.n_row)
        ]
        return lax.ppermute(value, ("section", "row"), perm)

    def cross(self, value):
        perm = [(r, r ^ self.n_group) for r in range(self.n_row)]
        return lax.ppermute(value, "row", perm)

    def halves(self, got, across):
        return [(DIRECT, self.share(got)), (ACROSS, self.share(across))]

    def second(self, *ready):
        arrays = [self.got, self.mine, *ready]
        second, cross = self.copies(second_kernel, "share_second", [2, 1], arrays)
        second = self.hop(second, 2)
        across = self.cross(cross)
        self.stages = [self.halves(self.got, across)]
        arrays = [self.got, across, *self.own, second]
        third, cross = self.copies(third_kernel, "share_third", [BLOCKS, 1], arrays)
        self.third = self.hop(third, 2)
        self.stages.append(self.halves(second, self.cross(cross)))

    def finish(self, ready):
        third, ready = lax.optimization_barrier((self.third, ready))
        self.stages.append([(FULL, self.share(third))])
        return ready

    def share(self, value):
        have = [value[None]]
        bit = 1
        while bit < self.n_group:
            send = have[0] if len(have) == 1 else jnp.concatenate(have, axis=0)
            have.append(lax.ppermute(send, "row", [(r, r ^ bit) for r in range(self.n_row)]))
            bit *= 2
        return have

    def choices(self, layer):
        offset = self.section ^ layer
        at_last = self.section == self.last
        picks = []
        for parity in (self.member % 2, 1 - self.member % 2):
            first = jnp.where(parity == 0, 1, 2)
            second = jnp.where(at_last, 3, 3 - first)
            pick = jnp.where(offset == first, 1, jnp.where(offset == second, 2, 3))
            picks.append(jnp.where(offset == 0, 0, pick))
        return picks


def local(tokens, embed, ln_gain, w_qkv, w_out, out_grad):
    n_section = lax.axis_size("section")
    n_row = lax.axis_size("row")
    section = lax.axis_index("section")
    place = lax.axis_index("row")
    micro, rows_here, seq = tokens.shape
    width = embed.shape[1]
    n_group = n_row // micro
    member = place % n_group
    rows = rows_here * micro
    scale = HEAD_DIM ** (-0.5) / math.sqrt(rows_here * n_row)
    fetched = Fetched((w_qkv, w_out), section, place, n_section, n_row, n_group)
    same = [[m * n_group + g for m in range(micro)] for g in range(n_group)]
    exchange = functools.partial(
        lax.all_to_all,
        axis_name="row",
        split_axis=0,
        concat_axis=0,
        axis_index_groups=same,
        tiled=True,
    )
    tok = exchange(tokens).reshape(-1)
    top_grad = exchange(out_grad).reshape(rows * seq, width)
    gain_parts = [ln_gain] + [
        lax.ppermute(ln_gain, "section", [(s, s ^ offset) for s in range(n_section)])
        for offset in range(1, n_section)
    ]
    gains = jnp.concatenate(gain_parts, axis=0)
    table = (jnp.arange(embed.shape[0], dtype=jnp.int32)[:, None] == tok[None, :]).astype(BF16)
    x = lax.dot_general(table, embed, TN, preferred_element_type=F32)

    fetched.second(x, *gain_parts[1:])
    chain = Chain(
        fetched, member, n_row, n_group, (w_qkv, w_out), gains, seq, width, rows, scale
    )
    xs, qkvs, probs = [], [], []
    scores = None
    dmix = None
    for layer in range(n_section):
        prev = None if layer == 0 else (*scores, qkvs[-1])
        top = top_grad if layer == n_section - 1 else None
        outs = list(chain.forward(layer, x, prev, top))
        if prev is not None:
            probs.append(outs.pop(0))
            x = outs.pop(0)
        xs.append(x)
        qkvs.append(outs[0])
        if top is not None:
            dmix = outs[2]
        scores = group_swap(outs[1], outs[1], n_row, n_group)
        if layer == 0:
            scores = (scores[0], fetched.finish(scores[1]))
    probs.append(None)

    dy = top_grad
    grads = ()
    for layer in range(n_section - 1, 0, -1):
        dy, dmix, part, send, *grads = chain.backward(
            layer,
            scores,
            probs[layer],
            qkvs[layer],
            dmix,
            xs[layer],
            dy,
            qkvs[layer - 1],
            grads,
        )
        scores = group_swap(part, send, n_row, n_group)
    early = RowSum(*chain.early(probs[0], qkvs[0], dmix, xs[0], dy, grads[:2]), place, n_row)
    early.add(early.exchange())
    early.send, other = lax.optimization_barrier((early.send, scores[1]))
    moved = early.exchange()
    late = RowSum(*chain.late((scores[0], other), probs[0], qkvs[0], xs[0], grads[2:]), place, n_row)
    late.send, moved = lax.optimization_barrier((late.send, moved))
    early.add(moved)
    g_early = early.finish()
    g_late = late.finish()
    g_qkv = jnp.concatenate([g_late, g_early[:, width:]], axis=1)
    block = width // n_row
    w_here = lax.dynamic_slice_in_dim(w_qkv[0], place * block, block, 0).astype(F32)
    gain_here = lax.dynamic_slice_in_dim(ln_gain, place * block, block, 1)
    g_gain = jnp.sum(g_qkv * w_here, axis=1)[None] / gain_here
    return (g_qkv[None], g_early[None, :, :width], g_gain)


def solution(mesh):
    in_specs = (
        P(None, "row", None),
        P(),
        P("section", None),
        P("section", None, None),
        P("section", None, None),
        P(None, "row", None, None),
    )
    out_specs = (P("section", "row", None), P("section", "row", None), P("section", "row"))
    return jax.shard_map(local, mesh=mesh, in_specs=in_specs, out_specs=out_specs, check_vma=False)
```

```python
import functools
import math

import jax
import jax.numpy as jnp
from jax import lax
from jax.experimental import pallas as pl
from jax.experimental.pallas import tpu as pltpu
from jax.sharding import PartitionSpec as P

HEADS = 12
HEAD_DIM = 64
PACK = 2
BLOCKS = 3
DIRECT, ACROSS, FULL = range(3)
F32 = jnp.float32
BF16 = jnp.bfloat16
VMEM_LIMIT = 60 * 1024 * 1024
NT = (((1,), (1,)), ((), ()))
TN = (((0,), (0,)), ((), ()))


def mm(a, b):
    return jnp.dot(a, b, preferred_element_type=F32)


def mm_nt(a, b):
    return lax.dot_general(a, b, NT, preferred_element_type=F32)


def head_lanes(ref, seq, head):
    width = PACK * HEAD_DIM
    first = head * width
    return jnp.concatenate(
        [ref[r * seq : (r + 1) * seq, first : first + width] for r in range(ref.shape[0] // seq)],
        axis=1,
    )


def regroup(blocks):
    return [
        jnp.concatenate([block[:, n * HEAD_DIM : (n + 1) * HEAD_DIM] for block in blocks], axis=1)
        for n in range(PACK)
    ]


def pack_rows(value, out, first, seq):
    width = PACK * HEAD_DIM
    for pair in range(value.shape[0] // seq // PACK):
        for p in range(value.shape[1] // width):
            blocks = [
                value[(pair * PACK + r) * seq : (pair * PACK + r + 1) * seq, p * width : (p + 1) * width]
                for r in range(PACK)
            ]
            for n, block in enumerate(regroup(blocks)):
                at = (first + p * PACK + n) * width
                out[pair * seq : (pair + 1) * seq, at : at + width] = block


class Weights:
    def __init__(self, info, first, own, stages, columns, dst, sems):
        self.choices = (info[first], info[first + 1])
        self.member, self.half = info[4], info[5]
        self.own, self.stages = own, stages
        self.columns, self.dst, self.sems = columns, dst, sems

    def each(self, act):
        @pl.when(self.choices[0] == 0)
        def _():
            act(pltpu.make_async_copy(self.own.at[0], self.dst, self.sems.at[0]))

        for stage, group in enumerate(self.stages):
            for parity in range(2):

                @pl.when(self.choices[parity] == stage + 1)
                def _(group=group, parity=parity):
                    for kind, refs in group:
                        self.shares(kind, refs, parity, act)

    def shares(self, kind, refs, parity, act):
        group = self.sems.shape[0] // BLOCKS
        block = self.dst.shape[0] // group // BLOCKS
        places = {DIRECT: (self.half, 2), ACROSS: (1 - self.half,), FULL: (0, 1, 2)}[kind]
        sems = {DIRECT: (0, 1), ACROSS: (2,), FULL: (0, 1, 2)}[kind]
        seen = 0
        for ref in refs:
            for n in range(ref.shape[0]):
                if seen % 2 == parity:
                    base = (self.member ^ seen) * BLOCKS
                    for j, place in enumerate(places):
                        start = pl.multiple_of((base + place) * block, block)
                        act(
                            pltpu.make_async_copy(
                                ref.at[n, j * block : (j + 1) * block, self.columns],
                                self.dst.at[pl.ds(start, block)],
                                self.sems.at[seen * BLOCKS + sems[j]],
                            )
                        )
                seen += 1

    def start(self):
        self.each(lambda copy: copy.start())

    def wait(self):
        self.each(lambda copy: copy.wait())


def take_stages(it, layout):
    return [[(kind, [next(it) for _ in range(count)]) for kind, count in group] for group in layout]


def softmax_heads(la, lb, scale, keep):
    seq = la.shape[0]
    for h in range(HEADS):
        at = slice(h * seq, (h + 1) * seq)
        logits = (la[:, at] + lb[:, at]) * scale
        e = jnp.exp(logits - jnp.max(logits, axis=-1, keepdims=True))
        keep(h, e / jnp.sum(e, axis=-1, keepdims=True))


def norm_parts(x):
    centred = x - jnp.mean(x, axis=-1, keepdims=True)
    spread = jnp.mean(centred * centred, axis=-1, keepdims=True)
    rstd = lax.rsqrt(spread + 1e-05)
    return centred * rstd, rstd


def scores(ref_a, first_a, ref_b, first_b, out, out_row, seq, begin):
    parts = [
        mm_nt(head_lanes(ref_a, seq, first_a + h), head_lanes(ref_b, seq, first_b + h))
        for h in range(HEADS)
    ]
    rows = slice(out_row, out_row + seq)

    @pl.when(begin)
    def _():
        for h, part in enumerate(parts):
            out[rows, h * seq : (h + 1) * seq] = part

    @pl.when(jnp.logical_not(begin))
    def _():
        for h, part in enumerate(parts):
            out[rows, h * seq : (h + 1) * seq] += part


def mix(weights, ref_b, first_b, out, first_out, scale, seq):
    width = PACK * HEAD_DIM
    for p in range(HEADS // PACK):
        values = []
        for h in range(p * PACK, (p + 1) * PACK):
            value = mm(weights[:, h * seq : (h + 1) * seq], head_lanes(ref_b, seq, first_b + h))
            values.append((value if scale is None else value * scale).astype(BF16))
        at = first_out + p * width
        for pair in range(ref_b.shape[0] // seq):
            blocks = [value[:, pair * width : (pair + 1) * width] for value in values]
            for n, block in enumerate(regroup(blocks)):
                row = (pair * PACK + n) * seq
                out[row : row + seq, at : at + width] = block


def forward_kernel(has_prev, has_top, info, *refs, layout, scale, seq, width):
    it = iter(refs)
    if has_prev:
        la, lb, v_prev = next(it), next(it), next(it)
    x_in, gain = next(it), next(it)
    top = next(it) if has_top else None
    own_q, own_o = next(it), next(it)
    stages = take_stages(it, layout)
    if has_prev:
        probs_out, x_out = next(it), next(it)
    qkv_out, score_out = next(it), next(it)
    if has_top:
        dmix_out = next(it)
    wq, sem_q = next(it), next(it)
    if has_prev:
        wo, sem_o, mixed = next(it), next(it), next(it)
    if has_top:
        wt, sem_t = next(it), next(it)
    step = pl.program_id(0)
    qcols, ocols = slice(0, 3 * width), slice(3 * width, 4 * width)
    get_q = Weights(info, 0, own_q, stages, qcols, wq, sem_q)
    if has_prev:
        get_o = Weights(info, 2, own_o, stages, ocols, wo, sem_o)
    if has_top:
        get_t = Weights(info, 0, own_o, stages, ocols, wt, sem_t)

    @pl.when(step == 0)
    def _():
        if has_prev:
            get_o.start()
        get_q.start()
        if has_top:
            get_t.start()
        if has_prev:

            def keep(h, value):
                probs_out[:, h * seq : (h + 1) * seq] = value.astype(BF16)

            softmax_heads(la, lb, scale, keep)

    if has_prev:
        mix(probs_out, v_prev, 0, mixed, 0, None, seq)
        pl.when(step == 0)(get_o.wait)
        x = x_in[...] + mm(mixed[...], wo[...])
        x_out[...] = x
    else:
        x = x_in[...]
    hat, _ = norm_parts(x)
    h = (hat * gain[pl.ds(info[6], 1), :]).astype(BF16)
    pl.when(step == 0)(get_q.wait)
    pack_rows(mm(h, wq[...]).astype(BF16), qkv_out, 0, seq)
    begin = step == 0
    scores(qkv_out, 0, qkv_out, HEADS, score_out, 0, seq, begin)
    if has_top:
        pl.when(step == 0)(get_t.wait)
        pack_rows(mm_nt(top[...], wt[...]).astype(BF16), dmix_out, 0, seq)
        scores(dmix_out, 0, qkv_out, 2 * HEADS, score_out, seq, seq, begin)


def add_product(a, b, total, column, step, steps, staged):
    at = slice(column, column + b.shape[1])
    part = lax.dot_general(a, b, TN, preferred_element_type=F32)

    @pl.when(step == 0)
    def _():
        total[:, at] = part

    @pl.when((step > 0) & (step < steps - 1))
    def _():
        total[:, at] += part

    @pl.when(step == steps - 1)
    def _():
        staged[:, at] = ((total[:, at] if steps > 1 else 0.0) + part).astype(staged.dtype)


def logit_grads(probs, sa, sb, first, seq, dl, dlt):
    for h in range(HEADS):
        at = slice(h * seq, (h + 1) * seq)
        prob = probs[:, at].astype(F32)
        d_prob = sa[first : first + seq, at] + sb[first : first + seq, at]
        d_logit = prob * (d_prob - jnp.sum(d_prob * prob, axis=-1, keepdims=True))
        dl[:, at] = d_logit.astype(BF16)
        dlt[:, at] = jnp.transpose(d_logit).astype(BF16)


def turn_probs(probs, seq, pt):
    for h in range(HEADS):
        at = slice(h * seq, (h + 1) * seq)
        pt[:, at] = jnp.transpose(probs[:, at].astype(F32)).astype(BF16)


def ship(staged, keep, send, member, sems):
    count, rows = keep.shape[0], keep.shape[1]
    copies = []
    for n in range(count):
        for k, dst in enumerate((keep, send)):
            start = pl.multiple_of((2 * n + (member + k) % 2) * rows, rows)
            copies.append(
                pltpu.make_async_copy(staged.at[pl.ds(start, rows)], dst.at[n], sems.at[2 * n + k])
            )
    return copies


def run_copies(copies):
    for copy in copies:
        copy.start()
    for copy in copies:
        copy.wait()


def backward_kernel(is_top, info, *refs, layout, scale, seq, width, steps):
    it = iter(refs)
    sa, sb = next(it), next(it)
    if not is_top:
        probs = next(it)
    qkv, dmix, x_in, gains, dy, v_prev = [next(it) for _ in range(6)]
    if not is_top:
        for _ in range(4):
            next(it)
    own_q, own_o = next(it), next(it)
    stages = take_stages(it, layout)
    dy_out, dmix_out, score_out, send_out = [next(it) for _ in range(4)]
    keep_a, send_a, keep_b, send_b = [next(it) for _ in range(4)]
    dl, dlt, pt, dqkv, mixed = [next(it) for _ in range(5)]
    total_a, staged_a, sem_a, total_b, staged_b, sem_b = [next(it) for _ in range(6)]
    wq, sem_q, wo, sem_o = [next(it) for _ in range(4)]
    if is_top:
        probs = next(it)
    step = pl.program_id(0)
    get_q = Weights(info, 0, own_q, stages, slice(0, 3 * width), wq, sem_q)
    get_o = Weights(info, 2, own_o, stages, slice(3 * width, 4 * width), wo, sem_o)
    own = info[0] == 0
    gain = gains[pl.ds(info[6], 1), :]

    @pl.when(step == 0)
    def _():
        get_q.start()
        get_o.start()
        if is_top:

            def keep(h, value):
                probs[:, h * seq : (h + 1) * seq] = value.astype(BF16)

            softmax_heads(sa.at[0:seq], sb.at[0:seq], scale, keep)
        logit_grads(probs, sa, sb, seq if is_top else 0, seq, dl, dlt)
        turn_probs(probs, seq, pt)

    mix(dl, qkv, HEADS, dqkv, 0, scale, seq)
    mix(dlt, qkv, 0, dqkv, width, scale, seq)
    mix(pt, dmix, 0, dqkv, 2 * width, None, seq)
    pl.when(step == 0)(get_q.wait)
    d_hat = mm_nt(dqkv[...], wq[...]).astype(BF16).astype(F32) * gain
    hat, rstd = norm_parts(x_in[...])
    mean_d = jnp.mean(d_hat, axis=-1, keepdims=True)
    mean_dh = jnp.mean(d_hat * hat, axis=-1, keepdims=True)
    d_x = dy[...].astype(F32) + rstd * (d_hat - mean_d - hat * mean_dh)
    dy_out[...] = d_x
    pl.when(step == 0)(get_o.wait)
    pack_rows(mm_nt(d_x.astype(BF16), wo[...]).astype(BF16), dmix_out, 0, seq)
    scores(dmix_out, 0, v_prev, 0, score_out, 0, seq, step == 0)

    @pl.when(step == steps - 1)
    def _():
        send_out[...] = score_out[...].astype(BF16)

    @pl.when(own)
    def _():
        mix(probs, qkv, 2 * HEADS, mixed, 0, None, seq)
        h = (norm_parts(x_in[...])[0] * gain).astype(BF16)
        add_product(mixed[...], dy[...].astype(BF16), total_a, 0, step, steps, staged_a)
        add_product(h, dqkv[:, 2 * width :], total_a, width, step, steps, staged_a)
        add_product(h, dqkv[:, : 2 * width], total_b, 0, step, steps, staged_b)

    @pl.when(own & (step == steps - 1))
    def _():
        copies = ship(staged_a, keep_a, send_a, info[4], sem_a)
        run_copies(copies + ship(staged_b, keep_b, send_b, info[4], sem_b))


def early_kernel(info, *refs, layout, seq, width, steps):
    probs, v, dmix, x_in, gains, dy, _, _, keep, send, pt, mixed, dv, total, staged, sem = refs
    step = pl.program_id(0)
    own = info[0] == 0

    @pl.when(own)
    def _():
        @pl.when(step == 0)
        def _():
            turn_probs(probs, seq, pt)

        mix(probs, v, 0, mixed, 0, None, seq)
        mix(pt, dmix, 0, dv, 0, None, seq)
        h = (norm_parts(x_in[...])[0] * gains[pl.ds(info[6], 1), :]).astype(BF16)
        add_product(mixed[...], dy[...].astype(BF16), total, 0, step, steps, staged)
        add_product(h, dv[...], total, width, step, steps, staged)

    @pl.when(own & (step == steps - 1))
    def _():
        run_copies(ship(staged, keep, send, info[4], sem))


def late_kernel(info, *refs, layout, scale, seq, width, steps):
    sa, sb, probs, qk, x_in, gains, _, _, keep, send, dl, dlt, dqk, total, staged, sem = refs
    step = pl.program_id(0)
    own = info[0] == 0

    @pl.when(own)
    def _():
        @pl.when(step == 0)
        def _():
            logit_grads(probs, sa, sb, 0, seq, dl, dlt)

        mix(dl, qk, HEADS, dqk, 0, scale, seq)
        mix(dlt, qk, 0, dqk, width, scale, seq)
        h = (norm_parts(x_in[...])[0] * gains[pl.ds(info[6], 1), :]).astype(BF16)
        add_product(h, dqk[...], total, 0, step, steps, staged)

    @pl.when(own & (step == steps - 1))
    def _():
        run_copies(ship(staged, keep, send, info[4], sem))


class Chain:
    def __init__(self, fetched, member, n_row, n_group, own, gains, seq, width, rows, scale):
        self.fetched, self.member, self.n_row, self.n_group = fetched, member, n_row, n_group
        self.gains = (gains, self.whole(*gains.shape))
        self.own, self.seq, self.width, self.rows = own, seq, width, rows
        self.scale = scale
        per_step = 4 if rows % 4 == 0 else 2
        self.chunk = per_step * seq
        self.steps = rows // per_step

    def info(self, now, other):
        picks = self.fetched.choices(now) + self.fetched.choices(other)
        picks += [self.member, self.fetched.half, self.fetched.section ^ now]
        return jnp.stack(picks).astype(jnp.int32)

    def whole(self, rows, lanes):
        return pl.BlockSpec((rows, lanes), lambda i, s: (0, 0))

    def tile(self, lanes, column=0, part=1):
        return pl.BlockSpec((self.chunk // part, lanes), lambda i, s: (i, column))

    def packed(self, heads, column=0):
        return self.tile(heads * PACK * HEAD_DIM, column, PACK)

    def call(self, body, name, info, stages, ins, outs, scratch, flops, carried=(), own=None):
        any_spec = pl.BlockSpec(memory_space=pl.ANY)
        groups = self.fetched.stages[:stages]
        weights = list(self.own if own is None else own)
        weights += [a for group in groups for _, arrays in group for a in arrays]
        arrays = [a for a, _ in ins] + list(carried)
        shapes = [o for o, _ in outs]
        size = sum(math.prod(a.shape) * a.dtype.itemsize for a in arrays + shapes)
        aliases = {
            1 + len(ins) + n: len(outs) - len(carried) + n for n in range(len(carried))
        }
        layout = tuple(tuple((kind, len(arrays)) for kind, arrays in group) for group in groups)
        return pl.pallas_call(
            functools.partial(body, layout=layout),
            name=name,
            out_shape=shapes,
            grid_spec=pltpu.PrefetchScalarGridSpec(
                num_scalar_prefetch=1,
                grid=(self.steps,),
                in_specs=[spec for _, spec in ins] + [any_spec] * (len(carried) + len(weights)),
                out_specs=[spec for _, spec in outs],
                scratch_shapes=scratch,
            ),
            input_output_aliases=aliases,
            compiler_params=pltpu.CompilerParams(
                dimension_semantics=("arbitrary",), vmem_limit_bytes=VMEM_LIMIT
            ),
            cost_estimate=pl.CostEstimate(flops=flops, bytes_accessed=size, transcendentals=0),
        )(info, *arrays, *weights)

    def weight_scratch(self, columns):
        return [
            pltpu.VMEM((self.width, columns * self.width), BF16),
            pltpu.SemaphoreType.DMA((self.n_group * BLOCKS,)),
        ]

    def shape(self, rows, lanes, dtype):
        return jax.ShapeDtypeStruct((rows, lanes), dtype)

    def grad_outs(self):
        any_spec = pl.BlockSpec(memory_space=pl.ANY)
        rows = self.width // self.n_row
        shape = (self.n_row // 2, rows, 2 * self.width)
        return [(jax.ShapeDtypeStruct(shape, self.grad_type()), any_spec)] * 2

    def grad_type(self):
        return BF16 if self.width // self.n_row % 16 == 0 else F32

    def grad_scratch(self):
        shape = (self.width, 2 * self.width)
        scratch = [pltpu.VMEM(shape, F32), pltpu.VMEM(shape, self.grad_type())]
        return scratch + [pltpu.SemaphoreType.DMA((self.n_row,))]

    def forward(self, layer, x, prev, top):
        seq, width = self.seq, self.width
        n = self.rows * seq
        hw = HEADS * seq
        score_rows = seq if top is None else 2 * seq
        ins = [(x, self.tile(width)), self.gains]
        outs = [
            (self.shape(n // PACK, 3 * PACK * width, BF16), self.packed(3 * HEADS)),
            (self.shape(score_rows, hw, F32), self.whole(score_rows, hw)),
        ]
        scratch = self.weight_scratch(3)
        if prev is not None:
            ins = [
                (prev[0], self.whole(seq, hw)),
                (prev[1], self.whole(seq, hw)),
                (prev[2], self.packed(HEADS, 2)),
            ] + ins
            outs = [
                (self.shape(seq, hw, BF16), self.whole(seq, hw)),
                (self.shape(n, width, F32), self.tile(width)),
            ] + outs
            scratch += self.weight_scratch(1) + [pltpu.VMEM((self.chunk, width), BF16)]
        if top is not None:
            ins.append((top, self.tile(width)))
            outs.append((self.shape(n // PACK, PACK * width, BF16), self.packed(HEADS)))
            scratch += self.weight_scratch(1)
        body = functools.partial(
            forward_kernel, prev is not None, top is not None, scale=self.scale, seq=seq, width=width
        )
        return self.call(
            body,
            f"layer_in_{layer}",
            self.info(layer, max(layer - 1, 0)),
            self.fetched.first_stages if layer == 0 else None,
            ins,
            outs,
            scratch,
            2 * n * width * width * 5,
        )

    def backward(self, layer, scores, probs, qkv, dmix, x, dy, v_prev, grads):
        seq, width = self.seq, self.width
        n = self.rows * seq
        hw = HEADS * seq
        is_top = probs is None
        score_rows = scores[0].shape[0]
        square = pltpu.VMEM((seq, hw), BF16)
        ins = [(s, self.whole(score_rows, hw)) for s in scores]
        if not is_top:
            ins.append((probs, self.whole(seq, hw)))
        ins += [
            (qkv, self.packed(3 * HEADS)),
            (dmix, self.packed(HEADS)),
            (x, self.tile(width)),
            self.gains,
            (dy, self.tile(width)),
            (v_prev, self.packed(HEADS, 2)),
        ]
        outs = [
            (self.shape(n, width, F32), self.tile(width)),
            (self.shape(n // PACK, PACK * width, BF16), self.packed(HEADS)),
            (self.shape(seq, hw, F32), self.whole(seq, hw)),
            (self.shape(seq, hw, BF16), self.whole(seq, hw)),
            *self.grad_outs(),
            *self.grad_outs(),
        ]
        scratch = [square] * 3
        scratch += [pltpu.VMEM((self.chunk, lanes * width), BF16) for lanes in (3, 1)]
        scratch += self.grad_scratch() * 2 + self.weight_scratch(3) + self.weight_scratch(1)
        if is_top:
            scratch.append(square)
        body = functools.partial(
            backward_kernel, is_top, scale=self.scale, seq=seq, width=width, steps=self.steps
        )
        return self.call(
            body,
            f"layer_back_{layer}",
            self.info(layer, layer - 1),
            None,
            ins,
            outs,
            scratch,
            2 * n * width * width * 5,
            carried=grads,
        )

    def early(self, probs, qkv, dmix, x, dy, grads):
        seq, width = self.seq, self.width
        n, hw = self.rows * seq, HEADS * seq
        ins = [
            (probs, self.whole(seq, hw)),
            (qkv, self.packed(HEADS, 2)),
            (dmix, self.packed(HEADS)),
            (x, self.tile(width)),
            self.gains,
            (dy, self.tile(width)),
        ]
        scratch = [pltpu.VMEM((seq, hw), BF16)] + [pltpu.VMEM((self.chunk, width), BF16)] * 2
        return self.call(
            functools.partial(early_kernel, seq=seq, width=width, steps=self.steps),
            "early_back_0",
            self.info(0, 0),
            0,
            ins,
            self.grad_outs(),
            scratch + self.grad_scratch(),
            2 * n * width * width * 3,
            carried=grads,
            own=(),
        )

    def late(self, scores, probs, qkv, x, grads):
        seq, width = self.seq, self.width
        n, hw = self.rows * seq, HEADS * seq
        ins = [
            (scores[0], self.whole(seq, hw)),
            (scores[1], self.whole(seq, hw)),
            (probs, self.whole(seq, hw)),
            (qkv, self.packed(2 * HEADS)),
            (x, self.tile(width)),
            self.gains,
        ]
        scratch = [pltpu.VMEM((seq, hw), BF16)] * 2 + [pltpu.VMEM((self.chunk, 2 * width), BF16)]
        return self.call(
            functools.partial(
                late_kernel, scale=self.scale, seq=seq, width=width, steps=self.steps
            ),
            "late_back_0",
            self.info(0, 0),
            0,
            ins,
            self.grad_outs(),
            scratch + self.grad_scratch(),
            2 * n * width * width * 3,
            carried=grads,
            own=(),
        )


def group_swap(value, send, n_row, n_group):
    other = jnp.zeros_like(send)
    bit = 1
    while bit < n_group:
        if bit > 1:
            value = value + other
            send = value.astype(send.dtype)
        other = lax.ppermute(send, "row", [(r, r ^ bit) for r in range(n_row)])
        bit *= 2
    return value, other


class RowSum:
    def __init__(self, keep, send, place, n_row):
        self.keep, self.send, self.place, self.n_row, self.bit = keep, send, place, n_row, 1

    def exchange(self):
        perm = [(r, r ^ self.bit) for r in range(self.n_row)]
        return lax.ppermute(self.send.astype(BF16), "row", perm)

    def add(self, other):
        value = self.keep.astype(F32) + other.astype(F32)
        self.bit *= 2
        if self.bit == self.n_row:
            return value[0]
        mine = self.place // self.bit % 2
        pair = value.reshape(value.shape[0] // 2, 2, *value.shape[1:])
        self.keep = lax.dynamic_index_in_dim(pair, mine, 1, keepdims=False)
        self.send = lax.dynamic_index_in_dim(pair, 1 - mine, 1, keepdims=False).astype(BF16)
        return None

    def finish(self):
        value = None
        while value is None:
            value = self.add(self.exchange())
        return value


def copy_call(body, name, scalars, outs, arrays):
    any_spec = pl.BlockSpec(memory_space=pl.ANY)
    return pl.pallas_call(
        body,
        name=name,
        out_shape=outs,
        grid_spec=pltpu.PrefetchScalarGridSpec(
            num_scalar_prefetch=1,
            grid=(1,),
            in_specs=[any_spec] * len(arrays),
            out_specs=[pl.BlockSpec(o.shape, lambda i, s: (0, 0)) for o in outs],
            scratch_shapes=[pltpu.SemaphoreType.DMA((2 * BLOCKS + 1,))],
        ),
        compiler_params=pltpu.CompilerParams(vmem_limit_bytes=VMEM_LIMIT),
        cost_estimate=pl.CostEstimate(flops=0, bytes_accessed=0, transcendentals=0),
    )(jnp.stack(scalars).astype(jnp.int32), *arrays)


def own_blocks(own, places, block, out, sems):
    copies, column = [], 0
    for k, ref in enumerate(own):
        columns = ref.shape[2]
        for n, place in enumerate(places):
            start = pl.multiple_of(place * block, block)
            copies.append(
                pltpu.make_async_copy(
                    ref.at[0, pl.ds(start, block)],
                    out.at[n * block : (n + 1) * block, column : column + columns],
                    sems.at[2 * n + k],
                )
            )
        column += columns
    return copies


def first_kernel(block, info, own_q, own_o, out, sems):
    base = info[0] * BLOCKS
    run_copies(own_blocks((own_q, own_o), (base + info[1], base + 2), block, out, sems))


def second_kernel(block, info, got, mine, *refs):
    out, cross, sems = refs[-3:]
    copy = pltpu.make_async_copy(got.at[:block], cross, sems.at[1])
    copy.start()
    for flag, source in ((1, got), (0, mine)):

        @pl.when(info[2] == flag)
        def _(source=source):
            run_copies([pltpu.make_async_copy(source, out, sems.at[0])])

    copy.wait()


def third_kernel(block, info, got, across, own_q, own_o, second, out, cross, sems):
    copy = pltpu.make_async_copy(second.at[:block], cross, sems.at[2 * BLOCKS])
    copy.start()

    @pl.when(info[2] == 1)
    def _():
        base = info[0] * BLOCKS
        places = [base + n for n in range(BLOCKS)]
        run_copies(own_blocks((own_q, own_o), places, block, out, sems))

    @pl.when(info[2] == 0)
    def _():
        copies = []
        for n, (source, place) in enumerate(
            ((got.at[:block], info[1]), (across, 1 - info[1]), (got.at[block:], 2))
        ):
            start = pl.multiple_of(place * block, block)
            copies.append(pltpu.make_async_copy(source, out.at[pl.ds(start, block)], sems.at[n]))
        run_copies(copies)

    copy.wait()


class Fetched:
    first_stages = 2

    def __init__(self, own, section, place, n_section, n_row, n_group):
        assert n_section == 4 and n_group % 2 == 0
        self.section, self.n_row, self.n_group = section, n_row, n_group
        self.member, self.half = place % n_group, place // n_group % 2
        self.last = n_section - 1
        self.block = own[0].shape[1] // n_group // BLOCKS
        self.own = own
        to_last = section == (self.last ^ jnp.where(self.member % 2 == 0, 2, 1))
        self.scalars = [self.member, self.half, to_last]
        (self.mine,) = self.copies(first_kernel, "share_first", [2], own)
        self.got = self.hop(self.mine, 1)

    def copies(self, body, name, blocks, arrays):
        columns = sum(w.shape[2] for w in self.own)
        outs = [jax.ShapeDtypeStruct((n * self.block, columns), BF16) for n in blocks]
        body = functools.partial(body, self.block)
        return copy_call(body, name, self.scalars, outs, arrays)

    def hop(self, value, even_bit):
        perm = [
            (s * self.n_row + r, (s ^ (even_bit if r % 2 == 0 else 3 - even_bit)) * self.n_row + r)
            for s in range(self.last + 1)
            for r in range(self.n_row)
        ]
        return lax.ppermute(value, ("section", "row"), perm)

    def cross(self, value):
        perm = [(r, r ^ self.n_group) for r in range(self.n_row)]
        return lax.ppermute(value, "row", perm)

    def halves(self, got, across):
        return [(DIRECT, self.share(got)), (ACROSS, self.share(across))]

    def second(self, *ready):
        arrays = [self.got, self.mine, *ready]
        second, cross = self.copies(second_kernel, "share_second", [2, 1], arrays)
        second = self.hop(second, 2)
        across = self.cross(cross)
        self.stages = [self.halves(self.got, across)]
        arrays = [self.got, across, *self.own, second]
        third, cross = self.copies(third_kernel, "share_third", [BLOCKS, 1], arrays)
        self.third = self.hop(third, 2)
        self.stages.append(self.halves(second, self.cross(cross)))

    def finish(self, ready):
        third, ready = lax.optimization_barrier((self.third, ready))
        self.stages.append([(FULL, self.share(third))])
        return ready

    def share(self, value):
        have = [value[None]]
        bit = 1
        while bit < self.n_group:
            send = have[0] if len(have) == 1 else jnp.concatenate(have, axis=0)
            have.append(lax.ppermute(send, "row", [(r, r ^ bit) for r in range(self.n_row)]))
            bit *= 2
        return have

    def choices(self, layer):
        offset = self.section ^ layer
        at_last = self.section == self.last
        picks = []
        for parity in (self.member % 2, 1 - self.member % 2):
            first = jnp.where(parity == 0, 1, 2)
            second = jnp.where(at_last, 3, 3 - first)
            pick = jnp.where(offset == first, 1, jnp.where(offset == second, 2, 3))
            picks.append(jnp.where(offset == 0, 0, pick))
        return picks


def local(tokens, embed, ln_gain, w_qkv, w_out, out_grad):
    n_section = lax.axis_size("section")
    n_row = lax.axis_size("row")
    section = lax.axis_index("section")
    place = lax.axis_index("row")
    micro, rows_here, seq = tokens.shape
    width = embed.shape[1]
    n_group = n_row // micro
    member = place % n_group
    rows = rows_here * micro
    scale = HEAD_DIM ** (-0.5) / math.sqrt(rows_here * n_row)
    fetched = Fetched((w_qkv, w_out), section, place, n_section, n_row, n_group)
    same = [[m * n_group + g for m in range(micro)] for g in range(n_group)]
    exchange = functools.partial(
        lax.all_to_all,
        axis_name="row",
        split_axis=0,
        concat_axis=0,
        axis_index_groups=same,
        tiled=True,
    )
    tok = exchange(tokens).reshape(-1)
    top_grad = exchange(out_grad).reshape(rows * seq, width)
    gain_parts = [ln_gain] + [
        lax.ppermute(ln_gain, "section", [(s, s ^ offset) for s in range(n_section)])
        for offset in range(1, n_section)
    ]
    gains = jnp.concatenate(gain_parts, axis=0)
    table = (jnp.arange(embed.shape[0], dtype=jnp.int32)[:, None] == tok[None, :]).astype(BF16)
    x = lax.dot_general(table, embed, TN, preferred_element_type=F32)

    fetched.second(x, *gain_parts[1:])
    chain = Chain(
        fetched, member, n_row, n_group, (w_qkv, w_out), gains, seq, width, rows, scale
    )
    xs, qkvs, probs = [], [], []
    scores = None
    dmix = None
    for layer in range(n_section):
        prev = None if layer == 0 else (*scores, qkvs[-1])
        top = top_grad if layer == n_section - 1 else None
        outs = list(chain.forward(layer, x, prev, top))
        if prev is not None:
            probs.append(outs.pop(0))
            x = outs.pop(0)
        xs.append(x)
        qkvs.append(outs[0])
        if top is not None:
            dmix = outs[2]
        scores = group_swap(outs[1], outs[1], n_row, n_group)
        if layer == 0:
            scores = (scores[0], fetched.finish(scores[1]))
    probs.append(None)

    dy = top_grad
    grads = ()
    for layer in range(n_section - 1, 0, -1):
        dy, dmix, part, send, *grads = chain.backward(
            layer,
            scores,
            probs[layer],
            qkvs[layer],
            dmix,
            xs[layer],
            dy,
            qkvs[layer - 1],
            grads,
        )
        scores = group_swap(part, send, n_row, n_group)
    early = RowSum(*chain.early(probs[0], qkvs[0], dmix, xs[0], dy, grads[:2]), place, n_row)
    early.add(early.exchange())
    early.send, other = lax.optimization_barrier((early.send, scores[1]))
    moved = early.exchange()
    late = RowSum(*chain.late((scores[0], other), probs[0], qkvs[0], xs[0], grads[2:]), place, n_row)
    late.send, moved = lax.optimization_barrier((late.send, moved))
    early.add(moved)
    g_early = early.finish()
    g_late = late.finish()
    g_qkv = jnp.concatenate([g_late, g_early[:, width:]], axis=1)
    block = width // n_row
    w_here = lax.dynamic_slice_in_dim(w_qkv[0], place * block, block, 0).astype(F32)
    gain_here = lax.dynamic_slice_in_dim(ln_gain, place * block, block, 1)
    g_gain = jnp.sum(g_qkv * w_here, axis=1)[None] / gain_here
    return (g_qkv[None], g_early[None, :, :width], g_gain)


def solution(mesh):
    in_specs = (
        P(None, "row", None),
        P(),
        P("section", None),
        P("section", None, None),
        P("section", None, None),
        P(None, "row", None, None),
    )
    out_specs = (P("section", "row", None), P("section", "row", None), P("section", "row"))
    return jax.shard_map(local, mesh=mesh, in_specs=in_specs, out_specs=out_specs, check_vma=False)
```

```python
import functools
import math

import jax
import jax.numpy as jnp
from jax import lax
from jax.experimental import pallas as pl
from jax.experimental.pallas import tpu as pltpu
from jax.sharding import PartitionSpec as P

HEADS = 12
HEAD_DIM = 64
PACK = 2
BLOCKS = 3
DIRECT, ACROSS, FULL = range(3)
F32 = jnp.float32
BF16 = jnp.bfloat16
VMEM_LIMIT = 50 * 1024 * 1024
NT = (((1,), (1,)), ((), ()))
TN = (((0,), (0,)), ((), ()))


def mm(a, b):
    return jnp.dot(a, b, preferred_element_type=F32)


def mm_nt(a, b):
    return lax.dot_general(a, b, NT, preferred_element_type=F32)


def head_lanes(ref, seq, head):
    width = PACK * HEAD_DIM
    first = head * width
    return jnp.concatenate(
        [ref[r * seq : (r + 1) * seq, first : first + width] for r in range(ref.shape[0] // seq)],
        axis=1,
    )


def regroup(blocks):
    return [
        jnp.concatenate([block[:, n * HEAD_DIM : (n + 1) * HEAD_DIM] for block in blocks], axis=1)
        for n in range(PACK)
    ]


def pack_rows(value, out, first, seq):
    width = PACK * HEAD_DIM
    for pair in range(value.shape[0] // seq // PACK):
        for p in range(value.shape[1] // width):
            blocks = [
                value[(pair * PACK + r) * seq : (pair * PACK + r + 1) * seq, p * width : (p + 1) * width]
                for r in range(PACK)
            ]
            for n, block in enumerate(regroup(blocks)):
                at = (first + p * PACK + n) * width
                out[pair * seq : (pair + 1) * seq, at : at + width] = block


class Weights:
    def __init__(self, info, first, own, stages, columns, dst, sems):
        self.choices = (info[first], info[first + 1])
        self.member, self.half = info[4], info[5]
        self.own, self.stages = own, stages
        self.columns, self.dst, self.sems = columns, dst, sems

    def each(self, act):
        @pl.when(self.choices[0] == 0)
        def _():
            act(pltpu.make_async_copy(self.own.at[0], self.dst, self.sems.at[0]))

        for stage, group in enumerate(self.stages):
            for parity in range(2):

                @pl.when(self.choices[parity] == stage + 1)
                def _(group=group, parity=parity):
                    for kind, refs in group:
                        self.shares(kind, refs, parity, act)

    def shares(self, kind, refs, parity, act):
        group = self.sems.shape[0] // BLOCKS
        block = self.dst.shape[0] // group // BLOCKS
        places = {DIRECT: (self.half, 2), ACROSS: (1 - self.half,), FULL: (0, 1, 2)}[kind]
        sems = {DIRECT: (0, 1), ACROSS: (2,), FULL: (0, 1, 2)}[kind]
        seen = 0
        for ref in refs:
            for n in range(ref.shape[0]):
                if seen % 2 == parity:
                    base = (self.member ^ seen) * BLOCKS
                    for j, place in enumerate(places):
                        start = pl.multiple_of((base + place) * block, block)
                        act(
                            pltpu.make_async_copy(
                                ref.at[n, j * block : (j + 1) * block, self.columns],
                                self.dst.at[pl.ds(start, block)],
                                self.sems.at[seen * BLOCKS + sems[j]],
                            )
                        )
                seen += 1

    def start(self):
        self.each(lambda copy: copy.start())

    def wait(self):
        self.each(lambda copy: copy.wait())


def take_stages(it, layout):
    return [[(kind, [next(it) for _ in range(count)]) for kind, count in group] for group in layout]


def softmax_heads(la, lb, scale, keep):
    seq = la.shape[0]
    for h in range(HEADS):
        at = slice(h * seq, (h + 1) * seq)
        logits = (la[:, at] + lb[:, at]) * scale
        e = jnp.exp(logits - jnp.max(logits, axis=-1, keepdims=True))
        keep(h, e / jnp.sum(e, axis=-1, keepdims=True))


def norm_parts(x):
    centred = x - jnp.mean(x, axis=-1, keepdims=True)
    spread = jnp.mean(centred * centred, axis=-1, keepdims=True)
    rstd = lax.rsqrt(spread + 1e-05)
    return centred * rstd, rstd


def scores(ref_a, first_a, ref_b, first_b, out, out_row, seq, begin):
    parts = [
        mm_nt(head_lanes(ref_a, seq, first_a + h), head_lanes(ref_b, seq, first_b + h))
        for h in range(HEADS)
    ]
    rows = slice(out_row, out_row + seq)

    @pl.when(begin)
    def _():
        for h, part in enumerate(parts):
            out[rows, h * seq : (h + 1) * seq] = part

    @pl.when(jnp.logical_not(begin))
    def _():
        for h, part in enumerate(parts):
            out[rows, h * seq : (h + 1) * seq] += part


def mix(weights, ref_b, first_b, out, first_out, scale, seq):
    width = PACK * HEAD_DIM
    for p in range(HEADS // PACK):
        values = []
        for h in range(p * PACK, (p + 1) * PACK):
            value = mm(weights[:, h * seq : (h + 1) * seq], head_lanes(ref_b, seq, first_b + h))
            values.append((value if scale is None else value * scale).astype(BF16))
        at = first_out + p * width
        for pair in range(ref_b.shape[0] // seq):
            blocks = [value[:, pair * width : (pair + 1) * width] for value in values]
            for n, block in enumerate(regroup(blocks)):
                row = (pair * PACK + n) * seq
                out[row : row + seq, at : at + width] = block


def forward_kernel(has_prev, has_top, info, *refs, layout, scale, seq, width):
    it = iter(refs)
    if has_prev:
        la, lb, v_prev = next(it), next(it), next(it)
    x_in, gain = next(it), next(it)
    top = next(it) if has_top else None
    own_q, own_o = next(it), next(it)
    stages = take_stages(it, layout)
    if has_prev:
        probs_out, x_out = next(it), next(it)
    qkv_out, score_out = next(it), next(it)
    if has_top:
        dmix_out = next(it)
    wq, sem_q = next(it), next(it)
    if has_prev:
        wo, sem_o, mixed = next(it), next(it), next(it)
    if has_top:
        wt, sem_t = next(it), next(it)
    step = pl.program_id(0)
    qcols, ocols = slice(0, 3 * width), slice(3 * width, 4 * width)
    get_q = Weights(info, 0, own_q, stages, qcols, wq, sem_q)
    if has_prev:
        get_o = Weights(info, 2, own_o, stages, ocols, wo, sem_o)
    if has_top:
        get_t = Weights(info, 0, own_o, stages, ocols, wt, sem_t)

    @pl.when(step == 0)
    def _():
        if has_prev:
            get_o.start()
        get_q.start()
        if has_top:
            get_t.start()
        if has_prev:

            def keep(h, value):
                probs_out[:, h * seq : (h + 1) * seq] = value.astype(BF16)

            softmax_heads(la, lb, scale, keep)

    if has_prev:
        mix(probs_out, v_prev, 0, mixed, 0, None, seq)
        pl.when(step == 0)(get_o.wait)
        x = x_in[...] + mm(mixed[...], wo[...])
        x_out[...] = x
    else:
        x = x_in[...]
    hat, _ = norm_parts(x)
    h = (hat * gain[pl.ds(info[6], 1), :]).astype(BF16)
    pl.when(step == 0)(get_q.wait)
    pack_rows(mm(h, wq[...]).astype(BF16), qkv_out, 0, seq)
    begin = step == 0
    scores(qkv_out, 0, qkv_out, HEADS, score_out, 0, seq, begin)
    if has_top:
        pl.when(step == 0)(get_t.wait)
        pack_rows(mm_nt(top[...], wt[...]).astype(BF16), dmix_out, 0, seq)
        scores(dmix_out, 0, qkv_out, 2 * HEADS, score_out, seq, seq, begin)


def add_product(a, b, total, column, step, steps, staged):
    at = slice(column, column + b.shape[1])
    part = lax.dot_general(a, b, TN, preferred_element_type=F32)

    @pl.when(step == 0)
    def _():
        total[:, at] = part

    @pl.when((step > 0) & (step < steps - 1))
    def _():
        total[:, at] += part

    @pl.when(step == steps - 1)
    def _():
        staged[:, at] = ((total[:, at] if steps > 1 else 0.0) + part).astype(staged.dtype)


def logit_grads(probs, sa, sb, first, seq, dl, dlt):
    for h in range(HEADS):
        at = slice(h * seq, (h + 1) * seq)
        prob = probs[:, at].astype(F32)
        d_prob = sa[first : first + seq, at] + sb[first : first + seq, at]
        d_logit = prob * (d_prob - jnp.sum(d_prob * prob, axis=-1, keepdims=True))
        dl[:, at] = d_logit.astype(BF16)
        dlt[:, at] = jnp.transpose(d_logit).astype(BF16)


def turn_probs(probs, seq, pt):
    for h in range(HEADS):
        at = slice(h * seq, (h + 1) * seq)
        pt[:, at] = jnp.transpose(probs[:, at].astype(F32)).astype(BF16)


def ship(staged, keep, send, member, sems):
    count, rows = keep.shape[0], keep.shape[1]
    copies = []
    for n in range(count):
        for k, dst in enumerate((keep, send)):
            start = pl.multiple_of((2 * n + (member + k) % 2) * rows, rows)
            copies.append(
                pltpu.make_async_copy(staged.at[pl.ds(start, rows)], dst.at[n], sems.at[2 * n + k])
            )
    return copies


def run_copies(copies):
    for copy in copies:
        copy.start()
    for copy in copies:
        copy.wait()


def backward_kernel(is_top, info, *refs, **sizes):
    step = pl.program_id(0)

    @pl.when(info[7] == 1)
    def _():
        backward_body(is_top, step, info, *refs, **sizes)


def backward_body(is_top, step, info, *refs, layout, scale, seq, width, steps):
    it = iter(refs)
    sa, sb = next(it), next(it)
    if not is_top:
        probs = next(it)
    qkv, dmix, x_in, gains, dy, v_prev = [next(it) for _ in range(6)]
    if not is_top:
        for _ in range(4):
            next(it)
    own_q, own_o = next(it), next(it)
    stages = take_stages(it, layout)
    dy_out, dmix_out, score_out, send_out = [next(it) for _ in range(4)]
    keep_a, send_a, keep_b, send_b = [next(it) for _ in range(4)]
    dl, dlt, pt, dqkv, mixed = [next(it) for _ in range(5)]
    total_a, staged_a, sem_a, total_b, staged_b, sem_b = [next(it) for _ in range(6)]
    wq, sem_q, wo, sem_o = [next(it) for _ in range(4)]
    if is_top:
        probs = next(it)
    get_q = Weights(info, 0, own_q, stages, slice(0, 3 * width), wq, sem_q)
    get_o = Weights(info, 2, own_o, stages, slice(3 * width, 4 * width), wo, sem_o)
    own = info[0] == 0
    gain = gains[pl.ds(info[6], 1), :]

    @pl.when(step == 0)
    def _():
        get_q.start()
        get_o.start()
        if is_top:

            def keep(h, value):
                probs[:, h * seq : (h + 1) * seq] = value.astype(BF16)

            softmax_heads(sa.at[0:seq], sb.at[0:seq], scale, keep)
        logit_grads(probs, sa, sb, seq if is_top else 0, seq, dl, dlt)
        turn_probs(probs, seq, pt)

    mix(dl, qkv, HEADS, dqkv, 0, scale, seq)
    mix(dlt, qkv, 0, dqkv, width, scale, seq)
    mix(pt, dmix, 0, dqkv, 2 * width, None, seq)
    pl.when(step == 0)(get_q.wait)
    d_hat = mm_nt(dqkv[...], wq[...]).astype(BF16).astype(F32) * gain
    hat, rstd = norm_parts(x_in[...])
    mean_d = jnp.mean(d_hat, axis=-1, keepdims=True)
    mean_dh = jnp.mean(d_hat * hat, axis=-1, keepdims=True)
    d_x = dy[...].astype(F32) + rstd * (d_hat - mean_d - hat * mean_dh)
    dy_out[...] = d_x
    pl.when(step == 0)(get_o.wait)
    pack_rows(mm_nt(d_x.astype(BF16), wo[...]).astype(BF16), dmix_out, 0, seq)
    scores(dmix_out, 0, v_prev, 0, score_out, 0, seq, step == 0)

    @pl.when(step == steps - 1)
    def _():
        send_out[...] = score_out[...].astype(BF16)

    @pl.when(own)
    def _():
        mix(probs, qkv, 2 * HEADS, mixed, 0, None, seq)
        h = (norm_parts(x_in[...])[0] * gain).astype(BF16)
        add_product(mixed[...], dy[...].astype(BF16), total_a, 0, step, steps, staged_a)
        add_product(h, dqkv[:, 2 * width :], total_a, width, step, steps, staged_a)
        add_product(h, dqkv[:, : 2 * width], total_b, 0, step, steps, staged_b)

    @pl.when(own & (step == steps - 1))
    def _():
        copies = ship(staged_a, keep_a, send_a, info[4], sem_a)
        run_copies(copies + ship(staged_b, keep_b, send_b, info[4], sem_b))


def early_kernel(info, *refs, layout, seq, width, steps):
    probs, v, dmix, x_in, gains, dy, _, _, keep, send, pt, mixed, dv, total, staged, sem = refs
    step = pl.program_id(0)
    own = info[0] == 0

    @pl.when(own)
    def _():
        @pl.when(step == 0)
        def _():
            turn_probs(probs, seq, pt)

        mix(probs, v, 0, mixed, 0, None, seq)
        mix(pt, dmix, 0, dv, 0, None, seq)
        h = (norm_parts(x_in[...])[0] * gains[pl.ds(info[6], 1), :]).astype(BF16)
        add_product(mixed[...], dy[...].astype(BF16), total, 0, step, steps, staged)
        add_product(h, dv[...], total, width, step, steps, staged)

    @pl.when(own & (step == steps - 1))
    def _():
        run_copies(ship(staged, keep, send, info[4], sem))


def late_kernel(info, *refs, layout, scale, seq, width, steps):
    sa, sb, probs, qk, x_in, gains, _, _, keep, send, dl, dlt, dqk, total, staged, sem = refs
    step = pl.program_id(0)
    own = info[0] == 0

    @pl.when(own)
    def _():
        @pl.when(step == 0)
        def _():
            logit_grads(probs, sa, sb, 0, seq, dl, dlt)

        mix(dl, qk, HEADS, dqk, 0, scale, seq)
        mix(dlt, qk, 0, dqk, width, scale, seq)
        h = (norm_parts(x_in[...])[0] * gains[pl.ds(info[6], 1), :]).astype(BF16)
        add_product(h, dqk[...], total, 0, step, steps, staged)

    @pl.when(own & (step == steps - 1))
    def _():
        run_copies(ship(staged, keep, send, info[4], sem))


class Chain:
    def __init__(self, fetched, member, n_row, n_group, own, gains, seq, width, rows, scale):
        self.fetched, self.member, self.n_row, self.n_group = fetched, member, n_row, n_group
        self.gains = (gains, self.whole(*gains.shape))
        self.own, self.seq, self.width, self.rows = own, seq, width, rows
        self.scale = scale
        per_step = 4 if rows % 4 == 0 else 2
        self.chunk = per_step * seq
        self.steps = rows // per_step

    def info(self, now, other):
        picks = self.fetched.choices(now) + self.fetched.choices(other)
        picks += [self.member, self.fetched.half, self.fetched.section ^ now]
        picks.append(self.fetched.section <= now)
        return jnp.stack(picks).astype(jnp.int32)

    def whole(self, rows, lanes):
        return pl.BlockSpec((rows, lanes), lambda i, s: (0, 0))

    def tile(self, lanes, column=0, part=1):
        return pl.BlockSpec((self.chunk // part, lanes), lambda i, s: (i, column))

    def packed(self, heads, column=0):
        return self.tile(heads * PACK * HEAD_DIM, column, PACK)

    def call(self, body, name, info, stages, ins, outs, scratch, flops, carried=(), own=None):
        any_spec = pl.BlockSpec(memory_space=pl.ANY)
        groups = self.fetched.stages[:stages]
        weights = list(self.own if own is None else own)
        weights += [a for group in groups for _, arrays in group for a in arrays]
        arrays = [a for a, _ in ins] + list(carried)
        shapes = [o for o, _ in outs]
        size = sum(math.prod(a.shape) * a.dtype.itemsize for a in arrays + shapes)
        aliases = {
            1 + len(ins) + n: len(outs) - len(carried) + n for n in range(len(carried))
        }
        layout = tuple(tuple((kind, len(arrays)) for kind, arrays in group) for group in groups)
        return pl.pallas_call(
            functools.partial(body, layout=layout),
            name=name,
            out_shape=shapes,
            grid_spec=pltpu.PrefetchScalarGridSpec(
                num_scalar_prefetch=1,
                grid=(self.steps,),
                in_specs=[spec for _, spec in ins] + [any_spec] * (len(carried) + len(weights)),
                out_specs=[spec for _, spec in outs],
                scratch_shapes=scratch,
            ),
            input_output_aliases=aliases,
            compiler_params=pltpu.CompilerParams(
                dimension_semantics=("arbitrary",), vmem_limit_bytes=VMEM_LIMIT + self.wide_bytes()
            ),
            cost_estimate=pl.CostEstimate(flops=flops, bytes_accessed=size, transcendentals=0),
        )(info, *arrays, *weights)

    def weight_scratch(self, columns):
        return [
            pltpu.VMEM((self.width, columns * self.width), BF16),
            pltpu.SemaphoreType.DMA((self.n_group * BLOCKS,)),
        ]

    def shape(self, rows, lanes, dtype):
        return jax.ShapeDtypeStruct((rows, lanes), dtype)

    def grad_outs(self):
        any_spec = pl.BlockSpec(memory_space=pl.ANY)
        rows = self.width // self.n_row
        shape = (self.n_row // 2, rows, 2 * self.width)
        return [(jax.ShapeDtypeStruct(shape, self.grad_type()), any_spec)] * 2

    def grad_type(self):
        return BF16 if self.width // self.n_row % 16 == 0 else F32

    def wide_bytes(self):
        return 0 if self.grad_type() == BF16 else 10 * 1024 * 1024

    def grad_scratch(self):
        shape = (self.width, 2 * self.width)
        scratch = [pltpu.VMEM(shape, F32), pltpu.VMEM(shape, self.grad_type())]
        return scratch + [pltpu.SemaphoreType.DMA((self.n_row,))]

    def forward(self, layer, x, prev, top):
        seq, width = self.seq, self.width
        n = self.rows * seq
        hw = HEADS * seq
        score_rows = seq if top is None else 2 * seq
        ins = [(x, self.tile(width)), self.gains]
        outs = [
            (self.shape(n // PACK, 3 * PACK * width, BF16), self.packed(3 * HEADS)),
            (self.shape(score_rows, hw, F32), self.whole(score_rows, hw)),
        ]
        scratch = self.weight_scratch(3)
        if prev is not None:
            ins = [
                (prev[0], self.whole(seq, hw)),
                (prev[1], self.whole(seq, hw)),
                (prev[2], self.packed(HEADS, 2)),
            ] + ins
            outs = [
                (self.shape(seq, hw, BF16), self.whole(seq, hw)),
                (self.shape(n, width, F32), self.tile(width)),
            ] + outs
            scratch += self.weight_scratch(1) + [pltpu.VMEM((self.chunk, width), BF16)]
        if top is not None:
            ins.append((top, self.tile(width)))
            outs.append((self.shape(n // PACK, PACK * width, BF16), self.packed(HEADS)))
            scratch += self.weight_scratch(1)
        body = functools.partial(
            forward_kernel, prev is not None, top is not None, scale=self.scale, seq=seq, width=width
        )
        return self.call(
            body,
            f"layer_in_{layer}",
            self.info(layer, max(layer - 1, 0)),
            self.fetched.first_stages if layer == 0 else None,
            ins,
            outs,
            scratch,
            2 * n * width * width * 5,
        )

    def backward(self, layer, scores, probs, qkv, dmix, x, dy, v_prev, grads):
        seq, width = self.seq, self.width
        n = self.rows * seq
        hw = HEADS * seq
        is_top = probs is None
        score_rows = scores[0].shape[0]
        square = pltpu.VMEM((seq, hw), BF16)
        ins = [(s, self.whole(score_rows, hw)) for s in scores]
        if not is_top:
            ins.append((probs, self.whole(seq, hw)))
        ins += [
            (qkv, self.packed(3 * HEADS)),
            (dmix, self.packed(HEADS)),
            (x, self.tile(width)),
            self.gains,
            (dy, self.tile(width)),
            (v_prev, self.packed(HEADS, 2)),
        ]
        outs = [
            (self.shape(n, width, F32), self.tile(width)),
            (self.shape(n // PACK, PACK * width, BF16), self.packed(HEADS)),
            (self.shape(seq, hw, F32), self.whole(seq, hw)),
            (self.shape(seq, hw, BF16), self.whole(seq, hw)),
            *self.grad_outs(),
            *self.grad_outs(),
        ]
        scratch = [square] * 3
        scratch += [pltpu.VMEM((self.chunk, lanes * width), BF16) for lanes in (3, 1)]
        scratch += self.grad_scratch() * 2 + self.weight_scratch(3) + self.weight_scratch(1)
        if is_top:
            scratch.append(square)
        body = functools.partial(
            backward_kernel, is_top, scale=self.scale, seq=seq, width=width, steps=self.steps
        )
        return self.call(
            body,
            f"layer_back_{layer}",
            self.info(layer, layer - 1),
            None,
            ins,
            outs,
            scratch,
            2 * n * width * width * 5,
            carried=grads,
        )

    def early(self, probs, qkv, dmix, x, dy, grads):
        seq, width = self.seq, self.width
        n, hw = self.rows * seq, HEADS * seq
        ins = [
            (probs, self.whole(seq, hw)),
            (qkv, self.packed(HEADS, 2)),
            (dmix, self.packed(HEADS)),
            (x, self.tile(width)),
            self.gains,
            (dy, self.tile(width)),
        ]
        scratch = [pltpu.VMEM((seq, hw), BF16)] + [pltpu.VMEM((self.chunk, width), BF16)] * 2
        return self.call(
            functools.partial(early_kernel, seq=seq, width=width, steps=self.steps),
            "early_back_0",
            self.info(0, 0),
            0,
            ins,
            self.grad_outs(),
            scratch + self.grad_scratch(),
            2 * n * width * width * 3,
            carried=grads,
            own=(),
        )

    def late(self, scores, probs, qkv, x, grads):
        seq, width = self.seq, self.width
        n, hw = self.rows * seq, HEADS * seq
        ins = [
            (scores[0], self.whole(seq, hw)),
            (scores[1], self.whole(seq, hw)),
            (probs, self.whole(seq, hw)),
            (qkv, self.packed(2 * HEADS)),
            (x, self.tile(width)),
            self.gains,
        ]
        scratch = [pltpu.VMEM((seq, hw), BF16)] * 2 + [pltpu.VMEM((self.chunk, 2 * width), BF16)]
        return self.call(
            functools.partial(
                late_kernel, scale=self.scale, seq=seq, width=width, steps=self.steps
            ),
            "late_back_0",
            self.info(0, 0),
            0,
            ins,
            self.grad_outs(),
            scratch + self.grad_scratch(),
            2 * n * width * width * 3,
            carried=grads,
            own=(),
        )


def group_swap(value, send, n_row, n_group):
    other = jnp.zeros_like(send)
    bit = 1
    while bit < n_group:
        if bit > 1:
            value = value + other
            send = value.astype(send.dtype)
        other = lax.ppermute(send, "row", [(r, r ^ bit) for r in range(n_row)])
        bit *= 2
    return value, other


class RowSum:
    def __init__(self, keep, send, place, n_row):
        self.keep, self.send, self.place, self.n_row, self.bit = keep, send, place, n_row, 1

    def exchange(self):
        perm = [(r, r ^ self.bit) for r in range(self.n_row)]
        return lax.ppermute(self.send.astype(BF16), "row", perm)

    def add(self, other):
        value = self.keep.astype(F32) + other.astype(F32)
        self.bit *= 2
        if self.bit == self.n_row:
            return value[0]
        mine = self.place // self.bit % 2
        pair = value.reshape(value.shape[0] // 2, 2, *value.shape[1:])
        self.keep = lax.dynamic_index_in_dim(pair, mine, 1, keepdims=False)
        self.send = lax.dynamic_index_in_dim(pair, 1 - mine, 1, keepdims=False).astype(BF16)
        return None

    def finish(self):
        value = None
        while value is None:
            value = self.add(self.exchange())
        return value


class Fetched:
    first_stages = 2

    def __init__(self, wqkv, wout, section, place, n_section, n_row, n_group):
        assert n_section == 4 and n_group % 2 == 0
        self.section, self.n_row, self.n_group = section, n_row, n_group
        self.member, self.half = place % n_group, place // n_group % 2
        self.last = n_section - 1
        self.block = wqkv.shape[0] // n_group // BLOCKS
        self.own = (wqkv, wout)
        self.to_last = section == (self.last ^ jnp.where(self.member % 2 == 0, 2, 1))
        self.mine = jnp.concatenate([self.own_block(self.half), self.own_block(2)], axis=0)
        self.got = self.hop(self.mine, 1)
        self.across = self.cross(self.got)
        self.stages = [self.halves(self.got, self.across)]

    def own_block(self, place, count=1):
        start = (self.member * BLOCKS + place) * self.block
        rows = [lax.dynamic_slice_in_dim(w, start, count * self.block, 0) for w in self.own]
        return jnp.concatenate(rows, axis=1)

    def hop(self, value, even_bit):
        perm = [
            (s * self.n_row + r, (s ^ (even_bit if r % 2 == 0 else 3 - even_bit)) * self.n_row + r)
            for s in range(self.last + 1)
            for r in range(self.n_row)
        ]
        return lax.ppermute(value, ("section", "row"), perm)

    def cross(self, value):
        perm = [(r, r ^ self.n_group) for r in range(self.n_row)]
        return lax.ppermute(value[: self.block], "row", perm)

    def halves(self, got, across):
        return [(DIRECT, self.share(got)), (ACROSS, self.share(across))]

    def second(self, x):
        second, x = lax.optimization_barrier((jnp.where(self.to_last, self.got, self.mine), x))
        second = self.hop(second, 2)
        self.stages.append(self.halves(second, self.cross(second)))
        low = jnp.where(self.half == 0, self.got[: self.block], self.across)
        high = jnp.where(self.half == 0, self.across, self.got[: self.block])
        relayed = jnp.concatenate([low, high, self.got[self.block :]], axis=0)
        third = jnp.where(self.to_last, self.own_block(0, BLOCKS), relayed)
        self.third = self.hop(third, 2)
        return x

    def finish(self, ready):
        third, ready = lax.optimization_barrier((self.third, ready))
        self.stages.append([(FULL, self.share(third))])
        return ready

    def share(self, value):
        have = [value[None]]
        bit = 1
        while bit < self.n_group:
            send = have[0] if len(have) == 1 else jnp.concatenate(have, axis=0)
            have.append(lax.ppermute(send, "row", [(r, r ^ bit) for r in range(self.n_row)]))
            bit *= 2
        return have

    def choices(self, layer):
        offset = self.section ^ layer
        at_last = self.section == self.last
        picks = []
        for parity in (self.member % 2, 1 - self.member % 2):
            first = jnp.where(parity == 0, 1, 2)
            second = jnp.where(at_last, 3, 3 - first)
            pick = jnp.where(offset == first, 1, jnp.where(offset == second, 2, 3))
            picks.append(jnp.where(offset == 0, 0, pick))
        return picks


def local(tokens, embed, ln_gain, w_qkv, w_out, out_grad):
    n_section = lax.axis_size("section")
    n_row = lax.axis_size("row")
    section = lax.axis_index("section")
    place = lax.axis_index("row")
    micro, rows_here, seq = tokens.shape
    width = embed.shape[1]
    n_group = n_row // micro
    member = place % n_group
    rows = rows_here * micro
    scale = HEAD_DIM ** (-0.5) / math.sqrt(rows_here * n_row)
    fetched = Fetched(w_qkv[0], w_out[0], section, place, n_section, n_row, n_group)
    same = [[m * n_group + g for m in range(micro)] for g in range(n_group)]
    exchange = functools.partial(
        lax.all_to_all,
        axis_name="row",
        split_axis=0,
        concat_axis=0,
        axis_index_groups=same,
        tiled=True,
    )
    tok = exchange(tokens).reshape(-1)
    top_grad = exchange(out_grad).reshape(rows * seq, width)
    gain_parts = [ln_gain] + [
        lax.ppermute(ln_gain, "section", [(s, s ^ offset) for s in range(n_section)])
        for offset in range(1, n_section)
    ]
    gains = jnp.concatenate(gain_parts, axis=0)
    table = (jnp.arange(embed.shape[0], dtype=jnp.int32)[:, None] == tok[None, :]).astype(BF16)
    x = lax.dot_general(table, embed, TN, preferred_element_type=F32)

    x, gains = fetched.second((x, gains))
    chain = Chain(
        fetched, member, n_row, n_group, (w_qkv, w_out), gains, seq, width, rows, scale
    )
    xs, qkvs, probs = [], [], []
    scores = None
    dmix = None
    for layer in range(n_section):
        prev = None if layer == 0 else (*scores, qkvs[-1])
        top = top_grad if layer == n_section - 1 else None
        outs = list(chain.forward(layer, x, prev, top))
        if prev is not None:
            probs.append(outs.pop(0))
            x = outs.pop(0)
        xs.append(x)
        qkvs.append(outs[0])
        if top is not None:
            dmix = outs[2]
        scores = group_swap(outs[1], outs[1], n_row, n_group)
        if layer == 0:
            scores = (scores[0], fetched.finish(scores[1]))
    probs.append(None)

    dy = top_grad
    grads = ()
    for layer in range(n_section - 1, 0, -1):
        dy, dmix, part, send, *grads = chain.backward(
            layer,
            scores,
            probs[layer],
            qkvs[layer],
            dmix,
            xs[layer],
            dy,
            qkvs[layer - 1],
            grads,
        )
        scores = group_swap(part, send, n_row, n_group)
    early = RowSum(*chain.early(probs[0], qkvs[0], dmix, xs[0], dy, grads[:2]), place, n_row)
    early.add(early.exchange())
    early.send, other = lax.optimization_barrier((early.send, scores[1]))
    moved = early.exchange()
    late = RowSum(*chain.late((scores[0], other), probs[0], qkvs[0], xs[0], grads[2:]), place, n_row)
    late.send, moved = lax.optimization_barrier((late.send, moved))
    early.add(moved)
    g_early = early.finish()
    g_late = late.finish()
    g_qkv = jnp.concatenate([g_late, g_early[:, width:]], axis=1)
    block = width // n_row
    w_here = lax.dynamic_slice_in_dim(w_qkv[0], place * block, block, 0).astype(F32)
    gain_here = lax.dynamic_slice_in_dim(ln_gain, place * block, block, 1)
    g_gain = jnp.sum(g_qkv * w_here, axis=1)[None] / gain_here
    return (g_qkv[None], g_early[None, :, :width], g_gain)


def solution(mesh):
    in_specs = (
        P(None, "row", None),
        P(),
        P("section", None),
        P("section", None, None),
        P("section", None, None),
        P(None, "row", None, None),
    )
    out_specs = (P("section", "row", None), P("section", "row", None), P("section", "row"))
    return jax.shard_map(local, mesh=mesh, in_specs=in_specs, out_specs=out_specs, check_vma=False)
```

```python
import functools
import math

import jax
import jax.numpy as jnp
from jax import lax
from jax.experimental import pallas as pl
from jax.experimental.pallas import tpu as pltpu
from jax.sharding import PartitionSpec as P

HEADS = 12
HEAD_DIM = 64
PACK = 2
BLOCKS = 3
DIRECT, ACROSS, FULL = range(3)
F32 = jnp.float32
BF16 = jnp.bfloat16
VMEM_LIMIT = 50 * 1024 * 1024
NT = (((1,), (1,)), ((), ()))
TN = (((0,), (0,)), ((), ()))


def mm(a, b):
    return jnp.dot(a, b, preferred_element_type=F32)


def mm_nt(a, b):
    return lax.dot_general(a, b, NT, preferred_element_type=F32)


def head_lanes(ref, seq, head):
    width = PACK * HEAD_DIM
    first = head * width
    return jnp.concatenate(
        [ref[r * seq : (r + 1) * seq, first : first + width] for r in range(ref.shape[0] // seq)],
        axis=1,
    )


def regroup(blocks):
    return [
        jnp.concatenate([block[:, n * HEAD_DIM : (n + 1) * HEAD_DIM] for block in blocks], axis=1)
        for n in range(PACK)
    ]


def pack_rows(value, out, first, seq):
    width = PACK * HEAD_DIM
    for pair in range(value.shape[0] // seq // PACK):
        for p in range(value.shape[1] // width):
            blocks = [
                value[(pair * PACK + r) * seq : (pair * PACK + r + 1) * seq, p * width : (p + 1) * width]
                for r in range(PACK)
            ]
            for n, block in enumerate(regroup(blocks)):
                at = (first + p * PACK + n) * width
                out[pair * seq : (pair + 1) * seq, at : at + width] = block


class Weights:
    def __init__(self, info, first, own, stages, columns, dst, sems):
        self.choices = (info[first], info[first + 1])
        self.member, self.half = info[4], info[5]
        self.own, self.stages = own, stages
        self.columns, self.dst, self.sems = columns, dst, sems

    def each(self, act):
        @pl.when(self.choices[0] == 0)
        def _():
            act(pltpu.make_async_copy(self.own.at[0], self.dst, self.sems.at[0]))

        for stage, group in enumerate(self.stages):
            for parity in range(2):

                @pl.when(self.choices[parity] == stage + 1)
                def _(group=group, parity=parity):
                    for kind, refs in group:
                        self.shares(kind, refs, parity, act)

    def shares(self, kind, refs, parity, act):
        group = self.sems.shape[0] // BLOCKS
        block = self.dst.shape[0] // group // BLOCKS
        places = {DIRECT: (self.half, 2), ACROSS: (1 - self.half,), FULL: (0, 1, 2)}[kind]
        sems = {DIRECT: (0, 1), ACROSS: (2,), FULL: (0, 1, 2)}[kind]
        seen = 0
        for ref in refs:
            for n in range(ref.shape[0]):
                if seen % 2 == parity:
                    base = (self.member ^ seen) * BLOCKS
                    for j, place in enumerate(places):
                        start = pl.multiple_of((base + place) * block, block)
                        act(
                            pltpu.make_async_copy(
                                ref.at[n, j * block : (j + 1) * block, self.columns],
                                self.dst.at[pl.ds(start, block)],
                                self.sems.at[seen * BLOCKS + sems[j]],
                            )
                        )
                seen += 1

    def start(self):
        self.each(lambda copy: copy.start())

    def wait(self):
        self.each(lambda copy: copy.wait())


def take_stages(it, layout):
    return [[(kind, [next(it) for _ in range(count)]) for kind, count in group] for group in layout]


def softmax_heads(la, lb, scale, keep):
    seq = la.shape[0]
    for h in range(HEADS):
        at = slice(h * seq, (h + 1) * seq)
        logits = (la[:, at] + lb[:, at]) * scale
        e = jnp.exp(logits - jnp.max(logits, axis=-1, keepdims=True))
        keep(h, e / jnp.sum(e, axis=-1, keepdims=True))


def norm_parts(x):
    centred = x - jnp.mean(x, axis=-1, keepdims=True)
    spread = jnp.mean(centred * centred, axis=-1, keepdims=True)
    rstd = lax.rsqrt(spread + 1e-05)
    return centred * rstd, rstd


def scores(ref_a, first_a, ref_b, first_b, out, out_row, seq, begin):
    parts = [
        mm_nt(head_lanes(ref_a, seq, first_a + h), head_lanes(ref_b, seq, first_b + h))
        for h in range(HEADS)
    ]
    rows = slice(out_row, out_row + seq)

    @pl.when(begin)
    def _():
        for h, part in enumerate(parts):
            out[rows, h * seq : (h + 1) * seq] = part

    @pl.when(jnp.logical_not(begin))
    def _():
        for h, part in enumerate(parts):
            out[rows, h * seq : (h + 1) * seq] += part


def mix(weights, ref_b, first_b, out, first_out, scale, seq):
    width = PACK * HEAD_DIM
    for p in range(HEADS // PACK):
        values = []
        for h in range(p * PACK, (p + 1) * PACK):
            value = mm(weights[:, h * seq : (h + 1) * seq], head_lanes(ref_b, seq, first_b + h))
            values.append((value if scale is None else value * scale).astype(BF16))
        at = first_out + p * width
        for pair in range(ref_b.shape[0] // seq):
            blocks = [value[:, pair * width : (pair + 1) * width] for value in values]
            for n, block in enumerate(regroup(blocks)):
                row = (pair * PACK + n) * seq
                out[row : row + seq, at : at + width] = block


def forward_kernel(has_prev, has_top, info, *refs, layout, scale, seq, width):
    it = iter(refs)
    if has_prev:
        la, lb, v_prev = next(it), next(it), next(it)
    x_in, gain = next(it), next(it)
    top = next(it) if has_top else None
    own_q, own_o = next(it), next(it)
    stages = take_stages(it, layout)
    if has_prev:
        probs_out, x_out = next(it), next(it)
    qkv_out, score_out = next(it), next(it)
    if has_top:
        dmix_out = next(it)
    wq, sem_q = next(it), next(it)
    if has_prev:
        wo, sem_o, mixed = next(it), next(it), next(it)
    if has_top:
        wt, sem_t = next(it), next(it)
    step = pl.program_id(0)
    qcols, ocols = slice(0, 3 * width), slice(3 * width, 4 * width)
    get_q = Weights(info, 0, own_q, stages, qcols, wq, sem_q)
    if has_prev:
        get_o = Weights(info, 2, own_o, stages, ocols, wo, sem_o)
    if has_top:
        get_t = Weights(info, 0, own_o, stages, ocols, wt, sem_t)

    @pl.when(step == 0)
    def _():
        if has_prev:
            get_o.start()
        get_q.start()
        if has_top:
            get_t.start()
        if has_prev:

            def keep(h, value):
                probs_out[:, h * seq : (h + 1) * seq] = value.astype(BF16)

            softmax_heads(la, lb, scale, keep)

    if has_prev:
        mix(probs_out, v_prev, 0, mixed, 0, None, seq)
        pl.when(step == 0)(get_o.wait)
        x = x_in[...] + mm(mixed[...], wo[...])
        x_out[...] = x
    else:
        x = x_in[...]
    hat, _ = norm_parts(x)
    h = (hat * gain[pl.ds(info[6], 1), :]).astype(BF16)
    pl.when(step == 0)(get_q.wait)
    pack_rows(mm(h, wq[...]).astype(BF16), qkv_out, 0, seq)
    begin = step == 0
    scores(qkv_out, 0, qkv_out, HEADS, score_out, 0, seq, begin)
    if has_top:
        pl.when(step == 0)(get_t.wait)
        pack_rows(mm_nt(top[...], wt[...]).astype(BF16), dmix_out, 0, seq)
        scores(dmix_out, 0, qkv_out, 2 * HEADS, score_out, seq, seq, begin)


def add_product(a, b, total, column, step, steps, staged):
    at = slice(column, column + b.shape[1])
    part = lax.dot_general(a, b, TN, preferred_element_type=F32)

    @pl.when(step == 0)
    def _():
        total[:, at] = part

    @pl.when((step > 0) & (step < steps - 1))
    def _():
        total[:, at] += part

    @pl.when(step == steps - 1)
    def _():
        staged[:, at] = ((total[:, at] if steps > 1 else 0.0) + part).astype(staged.dtype)


def logit_grads(probs, sa, sb, first, seq, dl, dlt):
    for h in range(HEADS):
        at = slice(h * seq, (h + 1) * seq)
        prob = probs[:, at].astype(F32)
        d_prob = sa[first : first + seq, at] + sb[first : first + seq, at]
        d_logit = prob * (d_prob - jnp.sum(d_prob * prob, axis=-1, keepdims=True))
        dl[:, at] = d_logit.astype(BF16)
        dlt[:, at] = jnp.transpose(d_logit).astype(BF16)


def turn_probs(probs, seq, pt):
    for h in range(HEADS):
        at = slice(h * seq, (h + 1) * seq)
        pt[:, at] = jnp.transpose(probs[:, at].astype(F32)).astype(BF16)


def ship(staged, keep, send, member, sems):
    count, rows = keep.shape[0], keep.shape[1]
    copies = []
    for n in range(count):
        for k, dst in enumerate((keep, send)):
            start = pl.multiple_of((2 * n + (member + k) % 2) * rows, rows)
            copies.append(
                pltpu.make_async_copy(staged.at[pl.ds(start, rows)], dst.at[n], sems.at[2 * n + k])
            )
    return copies


def run_copies(copies):
    for copy in copies:
        copy.start()
    for copy in copies:
        copy.wait()


def backward_kernel(is_top, info, *refs, **sizes):
    step = pl.program_id(0)

    @pl.when(info[7] == 1)
    def _():
        backward_body(is_top, step, info, *refs, **sizes)


def backward_body(is_top, step, info, *refs, layout, scale, seq, width, steps):
    it = iter(refs)
    sa, sb = next(it), next(it)
    if not is_top:
        probs = next(it)
    qkv, dmix, x_in, gains, dy, v_prev = [next(it) for _ in range(6)]
    if not is_top:
        for _ in range(4):
            next(it)
    own_q, own_o = next(it), next(it)
    stages = take_stages(it, layout)
    dy_out, dmix_out, score_out, send_out = [next(it) for _ in range(4)]
    keep_a, send_a, keep_b, send_b = [next(it) for _ in range(4)]
    dl, dlt, pt, dqkv, mixed = [next(it) for _ in range(5)]
    total_a, staged_a, sem_a, total_b, staged_b, sem_b = [next(it) for _ in range(6)]
    wq, sem_q, wo, sem_o = [next(it) for _ in range(4)]
    if is_top:
        probs = next(it)
    get_q = Weights(info, 0, own_q, stages, slice(0, 3 * width), wq, sem_q)
    get_o = Weights(info, 2, own_o, stages, slice(3 * width, 4 * width), wo, sem_o)
    own, onward = info[0] == 0, info[8] == 1
    gain = gains[pl.ds(info[6], 1), :]

    @pl.when(step == 0)
    def _():
        pl.when(onward)(get_q.start)
        pl.when(onward)(get_o.start)
        if is_top:

            def keep(h, value):
                probs[:, h * seq : (h + 1) * seq] = value.astype(BF16)

            softmax_heads(sa.at[0:seq], sb.at[0:seq], scale, keep)
        logit_grads(probs, sa, sb, seq if is_top else 0, seq, dl, dlt)
        turn_probs(probs, seq, pt)

    mix(dl, qkv, HEADS, dqkv, 0, scale, seq)
    mix(dlt, qkv, 0, dqkv, width, scale, seq)
    mix(pt, dmix, 0, dqkv, 2 * width, None, seq)

    @pl.when(onward)
    def _():
        pl.when(step == 0)(get_q.wait)
        d_hat = mm_nt(dqkv[...], wq[...]).astype(BF16).astype(F32) * gain
        hat, rstd = norm_parts(x_in[...])
        mean_d = jnp.mean(d_hat, axis=-1, keepdims=True)
        mean_dh = jnp.mean(d_hat * hat, axis=-1, keepdims=True)
        d_x = dy[...].astype(F32) + rstd * (d_hat - mean_d - hat * mean_dh)
        dy_out[...] = d_x
        pl.when(step == 0)(get_o.wait)
        pack_rows(mm_nt(d_x.astype(BF16), wo[...]).astype(BF16), dmix_out, 0, seq)
        scores(dmix_out, 0, v_prev, 0, score_out, 0, seq, step == 0)

        @pl.when(step == steps - 1)
        def _():
            send_out[...] = score_out[...].astype(BF16)

    @pl.when(own)
    def _():
        mix(probs, qkv, 2 * HEADS, mixed, 0, None, seq)
        h = (norm_parts(x_in[...])[0] * gain).astype(BF16)
        add_product(mixed[...], dy[...].astype(BF16), total_a, 0, step, steps, staged_a)
        add_product(h, dqkv[:, 2 * width :], total_a, width, step, steps, staged_a)
        add_product(h, dqkv[:, : 2 * width], total_b, 0, step, steps, staged_b)

    @pl.when(own & (step == steps - 1))
    def _():
        copies = ship(staged_a, keep_a, send_a, info[4], sem_a)
        run_copies(copies + ship(staged_b, keep_b, send_b, info[4], sem_b))


def early_kernel(info, *refs, layout, seq, width, steps):
    probs, v, dmix, x_in, gains, dy, _, _, keep, send, pt, mixed, dv, total, staged, sem = refs
    step = pl.program_id(0)
    own = info[0] == 0

    @pl.when(own)
    def _():
        @pl.when(step == 0)
        def _():
            turn_probs(probs, seq, pt)

        mix(probs, v, 0, mixed, 0, None, seq)
        mix(pt, dmix, 0, dv, 0, None, seq)
        h = (norm_parts(x_in[...])[0] * gains[pl.ds(info[6], 1), :]).astype(BF16)
        add_product(mixed[...], dy[...].astype(BF16), total, 0, step, steps, staged)
        add_product(h, dv[...], total, width, step, steps, staged)

    @pl.when(own & (step == steps - 1))
    def _():
        run_copies(ship(staged, keep, send, info[4], sem))


def late_kernel(info, *refs, layout, scale, seq, width, steps):
    sa, sb, probs, qk, x_in, gains, _, _, keep, send, dl, dlt, dqk, total, staged, sem = refs
    step = pl.program_id(0)
    own = info[0] == 0

    @pl.when(own)
    def _():
        @pl.when(step == 0)
        def _():
            logit_grads(probs, sa, sb, 0, seq, dl, dlt)

        mix(dl, qk, HEADS, dqk, 0, scale, seq)
        mix(dlt, qk, 0, dqk, width, scale, seq)
        h = (norm_parts(x_in[...])[0] * gains[pl.ds(info[6], 1), :]).astype(BF16)
        add_product(h, dqk[...], total, 0, step, steps, staged)

    @pl.when(own & (step == steps - 1))
    def _():
        run_copies(ship(staged, keep, send, info[4], sem))


class Chain:
    def __init__(self, fetched, member, n_row, n_group, own, gains, seq, width, rows, scale):
        self.fetched, self.member, self.n_row, self.n_group = fetched, member, n_row, n_group
        self.gains = (gains, self.whole(*gains.shape))
        self.own, self.seq, self.width, self.rows = own, seq, width, rows
        self.scale = scale
        per_step = 4 if rows % 4 == 0 else 2
        self.chunk = per_step * seq
        self.steps = rows // per_step

    def info(self, now, other):
        picks = self.fetched.choices(now) + self.fetched.choices(other)
        picks += [self.member, self.fetched.half, self.fetched.section ^ now]
        picks += [self.fetched.section <= now, self.fetched.section < now]
        return jnp.stack(picks).astype(jnp.int32)

    def whole(self, rows, lanes):
        return pl.BlockSpec((rows, lanes), lambda i, s: (0, 0))

    def tile(self, lanes, column=0, part=1):
        return pl.BlockSpec((self.chunk // part, lanes), lambda i, s: (i, column))

    def packed(self, heads, column=0):
        return self.tile(heads * PACK * HEAD_DIM, column, PACK)

    def call(self, body, name, info, stages, ins, outs, scratch, flops, carried=(), own=None):
        any_spec = pl.BlockSpec(memory_space=pl.ANY)
        groups = self.fetched.stages[:stages]
        weights = list(self.own if own is None else own)
        weights += [a for group in groups for _, arrays in group for a in arrays]
        arrays = [a for a, _ in ins] + list(carried)
        shapes = [o for o, _ in outs]
        size = sum(math.prod(a.shape) * a.dtype.itemsize for a in arrays + shapes)
        aliases = {
            1 + len(ins) + n: len(outs) - len(carried) + n for n in range(len(carried))
        }
        layout = tuple(tuple((kind, len(arrays)) for kind, arrays in group) for group in groups)
        return pl.pallas_call(
            functools.partial(body, layout=layout),
            name=name,
            out_shape=shapes,
            grid_spec=pltpu.PrefetchScalarGridSpec(
                num_scalar_prefetch=1,
                grid=(self.steps,),
                in_specs=[spec for _, spec in ins] + [any_spec] * (len(carried) + len(weights)),
                out_specs=[spec for _, spec in outs],
                scratch_shapes=scratch,
            ),
            input_output_aliases=aliases,
            compiler_params=pltpu.CompilerParams(
                dimension_semantics=("arbitrary",), vmem_limit_bytes=VMEM_LIMIT + self.wide_bytes()
            ),
            cost_estimate=pl.CostEstimate(flops=flops, bytes_accessed=size, transcendentals=0),
        )(info, *arrays, *weights)

    def weight_scratch(self, columns):
        return [
            pltpu.VMEM((self.width, columns * self.width), BF16),
            pltpu.SemaphoreType.DMA((self.n_group * BLOCKS,)),
        ]

    def shape(self, rows, lanes, dtype):
        return jax.ShapeDtypeStruct((rows, lanes), dtype)

    def grad_outs(self):
        any_spec = pl.BlockSpec(memory_space=pl.ANY)
        rows = self.width // self.n_row
        shape = (self.n_row // 2, rows, 2 * self.width)
        return [(jax.ShapeDtypeStruct(shape, self.grad_type()), any_spec)] * 2

    def grad_type(self):
        return BF16 if self.width // self.n_row % 16 == 0 else F32

    def wide_bytes(self):
        return 0 if self.grad_type() == BF16 else 10 * 1024 * 1024

    def grad_scratch(self):
        shape = (self.width, 2 * self.width)
        scratch = [pltpu.VMEM(shape, F32), pltpu.VMEM(shape, self.grad_type())]
        return scratch + [pltpu.SemaphoreType.DMA((self.n_row,))]

    def forward(self, layer, x, prev, top):
        seq, width = self.seq, self.width
        n = self.rows * seq
        hw = HEADS * seq
        score_rows = seq if top is None else 2 * seq
        ins = [(x, self.tile(width)), self.gains]
        outs = [
            (self.shape(n // PACK, 3 * PACK * width, BF16), self.packed(3 * HEADS)),
            (self.shape(score_rows, hw, F32), self.whole(score_rows, hw)),
        ]
        scratch = self.weight_scratch(3)
        if prev is not None:
            ins = [
                (prev[0], self.whole(seq, hw)),
                (prev[1], self.whole(seq, hw)),
                (prev[2], self.packed(HEADS, 2)),
            ] + ins
            outs = [
                (self.shape(seq, hw, BF16), self.whole(seq, hw)),
                (self.shape(n, width, F32), self.tile(width)),
            ] + outs
            scratch += self.weight_scratch(1) + [pltpu.VMEM((self.chunk, width), BF16)]
        if top is not None:
            ins.append((top, self.tile(width)))
            outs.append((self.shape(n // PACK, PACK * width, BF16), self.packed(HEADS)))
            scratch += self.weight_scratch(1)
        body = functools.partial(
            forward_kernel, prev is not None, top is not None, scale=self.scale, seq=seq, width=width
        )
        return self.call(
            body,
            f"layer_in_{layer}",
            self.info(layer, max(layer - 1, 0)),
            self.fetched.first_stages if layer == 0 else None,
            ins,
            outs,
            scratch,
            2 * n * width * width * 5,
        )

    def backward(self, layer, scores, probs, qkv, dmix, x, dy, v_prev, grads):
        seq, width = self.seq, self.width
        n = self.rows * seq
        hw = HEADS * seq
        is_top = probs is None
        score_rows = scores[0].shape[0]
        square = pltpu.VMEM((seq, hw), BF16)
        ins = [(s, self.whole(score_rows, hw)) for s in scores]
        if not is_top:
            ins.append((probs, self.whole(seq, hw)))
        ins += [
            (qkv, self.packed(3 * HEADS)),
            (dmix, self.packed(HEADS)),
            (x, self.tile(width)),
            self.gains,
            (dy, self.tile(width)),
            (v_prev, self.packed(HEADS, 2)),
        ]
        outs = [
            (self.shape(n, width, F32), self.tile(width)),
            (self.shape(n // PACK, PACK * width, BF16), self.packed(HEADS)),
            (self.shape(seq, hw, F32), self.whole(seq, hw)),
            (self.shape(seq, hw, BF16), self.whole(seq, hw)),
            *self.grad_outs(),
            *self.grad_outs(),
        ]
        scratch = [square] * 3
        scratch += [pltpu.VMEM((self.chunk, lanes * width), BF16) for lanes in (3, 1)]
        scratch += self.grad_scratch() * 2 + self.weight_scratch(3) + self.weight_scratch(1)
        if is_top:
            scratch.append(square)
        body = functools.partial(
            backward_kernel, is_top, scale=self.scale, seq=seq, width=width, steps=self.steps
        )
        return self.call(
            body,
            f"layer_back_{layer}",
            self.info(layer, layer - 1),
            None,
            ins,
            outs,
            scratch,
            2 * n * width * width * 5,
            carried=grads,
        )

    def early(self, probs, qkv, dmix, x, dy, grads):
        seq, width = self.seq, self.width
        n, hw = self.rows * seq, HEADS * seq
        ins = [
            (probs, self.whole(seq, hw)),
            (qkv, self.packed(HEADS, 2)),
            (dmix, self.packed(HEADS)),
            (x, self.tile(width)),
            self.gains,
            (dy, self.tile(width)),
        ]
        scratch = [pltpu.VMEM((seq, hw), BF16)] + [pltpu.VMEM((self.chunk, width), BF16)] * 2
        return self.call(
            functools.partial(early_kernel, seq=seq, width=width, steps=self.steps),
            "early_back_0",
            self.info(0, 0),
            0,
            ins,
            self.grad_outs(),
            scratch + self.grad_scratch(),
            2 * n * width * width * 3,
            carried=grads,
            own=(),
        )

    def late(self, scores, probs, qkv, x, grads):
        seq, width = self.seq, self.width
        n, hw = self.rows * seq, HEADS * seq
        ins = [
            (scores[0], self.whole(seq, hw)),
            (scores[1], self.whole(seq, hw)),
            (probs, self.whole(seq, hw)),
            (qkv, self.packed(2 * HEADS)),
            (x, self.tile(width)),
            self.gains,
        ]
        scratch = [pltpu.VMEM((seq, hw), BF16)] * 2 + [pltpu.VMEM((self.chunk, 2 * width), BF16)]
        return self.call(
            functools.partial(
                late_kernel, scale=self.scale, seq=seq, width=width, steps=self.steps
            ),
            "late_back_0",
            self.info(0, 0),
            0,
            ins,
            self.grad_outs(),
            scratch + self.grad_scratch(),
            2 * n * width * width * 3,
            carried=grads,
            own=(),
        )


def group_swap(value, send, n_row, n_group):
    other = jnp.zeros_like(send)
    bit = 1
    while bit < n_group:
        if bit > 1:
            value = value + other
            send = value.astype(send.dtype)
        other = lax.ppermute(send, "row", [(r, r ^ bit) for r in range(n_row)])
        bit *= 2
    return value, other


class RowSum:
    def __init__(self, keep, send, place, n_row):
        self.keep, self.send, self.place, self.n_row, self.bit = keep, send, place, n_row, 1

    def exchange(self):
        perm = [(r, r ^ self.bit) for r in range(self.n_row)]
        return lax.ppermute(self.send.astype(BF16), "row", perm)

    def add(self, other):
        value = self.keep.astype(F32) + other.astype(F32)
        self.bit *= 2
        if self.bit == self.n_row:
            return value[0]
        mine = self.place // self.bit % 2
        pair = value.reshape(value.shape[0] // 2, 2, *value.shape[1:])
        self.keep = lax.dynamic_index_in_dim(pair, mine, 1, keepdims=False)
        self.send = lax.dynamic_index_in_dim(pair, 1 - mine, 1, keepdims=False).astype(BF16)
        return None

    def finish(self):
        value = None
        while value is None:
            value = self.add(self.exchange())
        return value


class Fetched:
    first_stages = 2

    def __init__(self, wqkv, wout, section, place, n_section, n_row, n_group):
        assert n_section == 4 and n_group % 2 == 0
        self.section, self.n_row, self.n_group = section, n_row, n_group
        self.member, self.half = place % n_group, place // n_group % 2
        self.last = n_section - 1
        self.block = wqkv.shape[0] // n_group // BLOCKS
        self.own = (wqkv, wout)
        self.to_last = section == (self.last ^ jnp.where(self.member % 2 == 0, 2, 1))
        self.mine = jnp.concatenate([self.own_block(self.half), self.own_block(2)], axis=0)
        self.got = self.hop(self.mine, 1)
        self.across = self.cross(self.got)
        self.stages = [self.halves(self.got, self.across)]

    def own_block(self, place, count=1):
        start = (self.member * BLOCKS + place) * self.block
        rows = [lax.dynamic_slice_in_dim(w, start, count * self.block, 0) for w in self.own]
        return jnp.concatenate(rows, axis=1)

    def hop(self, value, even_bit):
        perm = [
            (s * self.n_row + r, (s ^ (even_bit if r % 2 == 0 else 3 - even_bit)) * self.n_row + r)
            for s in range(self.last + 1)
            for r in range(self.n_row)
        ]
        return lax.ppermute(value, ("section", "row"), perm)

    def cross(self, value):
        perm = [(r, r ^ self.n_group) for r in range(self.n_row)]
        return lax.ppermute(value[: self.block], "row", perm)

    def halves(self, got, across):
        return [(DIRECT, self.share(got)), (ACROSS, self.share(across))]

    def second(self, x):
        second, x = lax.optimization_barrier((jnp.where(self.to_last, self.got, self.mine), x))
        second = self.hop(second, 2)
        self.stages.append(self.halves(second, self.cross(second)))
        low = jnp.where(self.half == 0, self.got[: self.block], self.across)
        high = jnp.where(self.half == 0, self.across, self.got[: self.block])
        relayed = jnp.concatenate([low, high, self.got[self.block :]], axis=0)
        third = jnp.where(self.to_last, self.own_block(0, BLOCKS), relayed)
        self.third = self.hop(third, 2)
        return x

    def finish(self, ready):
        third, ready = lax.optimization_barrier((self.third, ready))
        self.stages.append([(FULL, self.share(third))])
        return ready

    def share(self, value):
        have = [value[None]]
        bit = 1
        while bit < self.n_group:
            send = have[0] if len(have) == 1 else jnp.concatenate(have, axis=0)
            have.append(lax.ppermute(send, "row", [(r, r ^ bit) for r in range(self.n_row)]))
            bit *= 2
        return have

    def choices(self, layer):
        offset = self.section ^ layer
        at_last = self.section == self.last
        picks = []
        for parity in (self.member % 2, 1 - self.member % 2):
            first = jnp.where(parity == 0, 1, 2)
            second = jnp.where(at_last, 3, 3 - first)
            pick = jnp.where(offset == first, 1, jnp.where(offset == second, 2, 3))
            picks.append(jnp.where(offset == 0, 0, pick))
        return picks


def local(tokens, embed, ln_gain, w_qkv, w_out, out_grad):
    n_section = lax.axis_size("section")
    n_row = lax.axis_size("row")
    section = lax.axis_index("section")
    place = lax.axis_index("row")
    micro, rows_here, seq = tokens.shape
    width = embed.shape[1]
    n_group = n_row // micro
    member = place % n_group
    rows = rows_here * micro
    scale = HEAD_DIM ** (-0.5) / math.sqrt(rows_here * n_row)
    fetched = Fetched(w_qkv[0], w_out[0], section, place, n_section, n_row, n_group)
    same = [[m * n_group + g for m in range(micro)] for g in range(n_group)]
    exchange = functools.partial(
        lax.all_to_all,
        axis_name="row",
        split_axis=0,
        concat_axis=0,
        axis_index_groups=same,
        tiled=True,
    )
    tok = exchange(tokens).reshape(-1)
    top_grad = exchange(out_grad).reshape(rows * seq, width)
    gain_parts = [ln_gain] + [
        lax.ppermute(ln_gain, "section", [(s, s ^ offset) for s in range(n_section)])
        for offset in range(1, n_section)
    ]
    gains = jnp.concatenate(gain_parts, axis=0)
    table = (jnp.arange(embed.shape[0], dtype=jnp.int32)[:, None] == tok[None, :]).astype(BF16)
    x = lax.dot_general(table, embed, TN, preferred_element_type=F32)

    x, gains = fetched.second((x, gains))
    chain = Chain(
        fetched, member, n_row, n_group, (w_qkv, w_out), gains, seq, width, rows, scale
    )
    xs, qkvs, probs = [], [], []
    scores = None
    dmix = None
    for layer in range(n_section):
        prev = None if layer == 0 else (*scores, qkvs[-1])
        top = top_grad if layer == n_section - 1 else None
        outs = list(chain.forward(layer, x, prev, top))
        if prev is not None:
            probs.append(outs.pop(0))
            x = outs.pop(0)
        xs.append(x)
        qkvs.append(outs[0])
        if top is not None:
            dmix = outs[2]
        scores = group_swap(outs[1], outs[1], n_row, n_group)
        if layer == 0:
            scores = (scores[0], fetched.finish(scores[1]))
    probs.append(None)

    dy = top_grad
    grads = ()
    for layer in range(n_section - 1, 0, -1):
        dy, dmix, part, send, *grads = chain.backward(
            layer,
            scores,
            probs[layer],
            qkvs[layer],
            dmix,
            xs[layer],
            dy,
            qkvs[layer - 1],
            grads,
        )
        scores = group_swap(part, send, n_row, n_group)
    early = RowSum(*chain.early(probs[0], qkvs[0], dmix, xs[0], dy, grads[:2]), place, n_row)
    early.add(early.exchange())
    early.send, other = lax.optimization_barrier((early.send, scores[1]))
    moved = early.exchange()
    late = RowSum(*chain.late((scores[0], other), probs[0], qkvs[0], xs[0], grads[2:]), place, n_row)
    late.send, moved = lax.optimization_barrier((late.send, moved))
    early.add(moved)
    g_early = early.finish()
    g_late = late.finish()
    g_qkv = jnp.concatenate([g_late, g_early[:, width:]], axis=1)
    block = width // n_row
    w_here = lax.dynamic_slice_in_dim(w_qkv[0], place * block, block, 0).astype(F32)
    gain_here = lax.dynamic_slice_in_dim(ln_gain, place * block, block, 1)
    g_gain = jnp.sum(g_qkv * w_here, axis=1)[None] / gain_here
    return (g_qkv[None], g_early[None, :, :width], g_gain)


def solution(mesh):
    in_specs = (
        P(None, "row", None),
        P(),
        P("section", None),
        P("section", None, None),
        P("section", None, None),
        P(None, "row", None, None),
    )
    out_specs = (P("section", "row", None), P("section", "row", None), P("section", "row"))
    return jax.shard_map(local, mesh=mesh, in_specs=in_specs, out_specs=out_specs, check_vma=False)
```

```python
import functools
import math

import jax
import jax.numpy as jnp
from jax import lax
from jax.experimental import pallas as pl
from jax.experimental.pallas import tpu as pltpu
from jax.sharding import PartitionSpec as P

HEADS = 12
HEAD_DIM = 64
PACK = 2
BLOCKS = 3
DIRECT, ACROSS, FULL = range(3)
F32 = jnp.float32
BF16 = jnp.bfloat16
VMEM_LIMIT = 50 * 1024 * 1024
NT = (((1,), (1,)), ((), ()))
TN = (((0,), (0,)), ((), ()))


def mm(a, b):
    return jnp.dot(a, b, preferred_element_type=F32)


def mm_nt(a, b):
    return lax.dot_general(a, b, NT, preferred_element_type=F32)


def head_lanes(ref, seq, head):
    width = PACK * HEAD_DIM
    first = head * width
    return jnp.concatenate(
        [ref[r * seq : (r + 1) * seq, first : first + width] for r in range(ref.shape[0] // seq)],
        axis=1,
    )


def regroup(blocks):
    return [
        jnp.concatenate([block[:, n * HEAD_DIM : (n + 1) * HEAD_DIM] for block in blocks], axis=1)
        for n in range(PACK)
    ]


def pack_rows(value, out, first, seq):
    width = PACK * HEAD_DIM
    for pair in range(value.shape[0] // seq // PACK):
        for p in range(value.shape[1] // width):
            blocks = [
                value[(pair * PACK + r) * seq : (pair * PACK + r + 1) * seq, p * width : (p + 1) * width]
                for r in range(PACK)
            ]
            for n, block in enumerate(regroup(blocks)):
                at = (first + p * PACK + n) * width
                out[pair * seq : (pair + 1) * seq, at : at + width] = block


class Weights:
    def __init__(self, info, first, own, stages, columns, dst, sems):
        self.choices = (info[first], info[first + 1])
        self.member, self.half = info[4], info[5]
        self.own, self.stages = own, stages
        self.columns, self.dst, self.sems = columns, dst, sems

    def each(self, act):
        @pl.when(self.choices[0] == 0)
        def _():
            act(pltpu.make_async_copy(self.own.at[0], self.dst, self.sems.at[0]))

        for stage, group in enumerate(self.stages):
            for parity in range(2):

                @pl.when(self.choices[parity] == stage + 1)
                def _(group=group, parity=parity):
                    for kind, refs in group:
                        self.shares(kind, refs, parity, act)

    def shares(self, kind, refs, parity, act):
        group = self.sems.shape[0] // BLOCKS
        block = self.dst.shape[0] // group // BLOCKS
        places = {DIRECT: (self.half, 2), ACROSS: (1 - self.half,), FULL: (0, 1, 2)}[kind]
        sems = {DIRECT: (0, 1), ACROSS: (2,), FULL: (0, 1, 2)}[kind]
        seen = 0
        for ref in refs:
            for n in range(ref.shape[0]):
                if seen % 2 == parity:
                    base = (self.member ^ seen) * BLOCKS
                    for j, place in enumerate(places):
                        start = pl.multiple_of((base + place) * block, block)
                        act(
                            pltpu.make_async_copy(
                                ref.at[n, j * block : (j + 1) * block, self.columns],
                                self.dst.at[pl.ds(start, block)],
                                self.sems.at[seen * BLOCKS + sems[j]],
                            )
                        )
                seen += 1

    def start(self):
        self.each(lambda copy: copy.start())

    def wait(self):
        self.each(lambda copy: copy.wait())


def take_stages(it, layout):
    return [[(kind, [next(it) for _ in range(count)]) for kind, count in group] for group in layout]


def softmax_heads(la, lb, scale, keep):
    seq = la.shape[0]
    for h in range(HEADS):
        at = slice(h * seq, (h + 1) * seq)
        logits = (la[:, at] + lb[:, at]) * scale
        e = jnp.exp(logits - jnp.max(logits, axis=-1, keepdims=True))
        keep(h, e / jnp.sum(e, axis=-1, keepdims=True))


def norm_parts(x):
    centred = x - jnp.mean(x, axis=-1, keepdims=True)
    spread = jnp.mean(centred * centred, axis=-1, keepdims=True)
    rstd = lax.rsqrt(spread + 1e-05)
    return centred * rstd, rstd


def scores(ref_a, first_a, ref_b, first_b, out, out_row, seq, begin):
    parts = [
        mm_nt(head_lanes(ref_a, seq, first_a + h), head_lanes(ref_b, seq, first_b + h))
        for h in range(HEADS)
    ]
    rows = slice(out_row, out_row + seq)

    @pl.when(begin)
    def _():
        for h, part in enumerate(parts):
            out[rows, h * seq : (h + 1) * seq] = part

    @pl.when(jnp.logical_not(begin))
    def _():
        for h, part in enumerate(parts):
            out[rows, h * seq : (h + 1) * seq] += part


def mix(weights, ref_b, first_b, out, first_out, scale, seq):
    width = PACK * HEAD_DIM
    for p in range(HEADS // PACK):
        values = []
        for h in range(p * PACK, (p + 1) * PACK):
            value = mm(weights[:, h * seq : (h + 1) * seq], head_lanes(ref_b, seq, first_b + h))
            values.append((value if scale is None else value * scale).astype(BF16))
        at = first_out + p * width
        for pair in range(ref_b.shape[0] // seq):
            blocks = [value[:, pair * width : (pair + 1) * width] for value in values]
            for n, block in enumerate(regroup(blocks)):
                row = (pair * PACK + n) * seq
                out[row : row + seq, at : at + width] = block


def forward_kernel(has_prev, has_top, info, *refs, layout, scale, seq, width):
    it = iter(refs)
    if has_prev:
        la, lb, v_prev = next(it), next(it), next(it)
    x_in, gain = next(it), next(it)
    top = next(it) if has_top else None
    own_q, own_o = next(it), next(it)
    stages = take_stages(it, layout)
    if has_prev:
        probs_out, x_out = next(it), next(it)
    qkv_out, score_out = next(it), next(it)
    if has_top:
        dmix_out = next(it)
    wq, sem_q = next(it), next(it)
    if has_prev:
        wo, sem_o, mixed = next(it), next(it), next(it)
    if has_top:
        wt, sem_t = next(it), next(it)
    step = pl.program_id(0)
    qcols, ocols = slice(0, 3 * width), slice(3 * width, 4 * width)
    get_q = Weights(info, 0, own_q, stages, qcols, wq, sem_q)
    if has_prev:
        get_o = Weights(info, 2, own_o, stages, ocols, wo, sem_o)
    if has_top:
        get_t = Weights(info, 0, own_o, stages, ocols, wt, sem_t)

    @pl.when(step == 0)
    def _():
        if has_prev:
            get_o.start()
        get_q.start()
        if has_top:
            get_t.start()
        if has_prev:

            def keep(h, value):
                probs_out[:, h * seq : (h + 1) * seq] = value.astype(BF16)

            softmax_heads(la, lb, scale, keep)

    if has_prev:
        mix(probs_out, v_prev, 0, mixed, 0, None, seq)
        pl.when(step == 0)(get_o.wait)
        x = x_in[...] + mm(mixed[...], wo[...])
        x_out[...] = x
    else:
        x = x_in[...]
    hat, _ = norm_parts(x)
    h = (hat * gain[pl.ds(info[6], 1), :]).astype(BF16)
    pl.when(step == 0)(get_q.wait)
    pack_rows(mm(h, wq[...]).astype(BF16), qkv_out, 0, seq)
    begin = step == 0
    scores(qkv_out, 0, qkv_out, HEADS, score_out, 0, seq, begin)
    if has_top:
        pl.when(step == 0)(get_t.wait)
        pack_rows(mm_nt(top[...], wt[...]).astype(BF16), dmix_out, 0, seq)
        scores(dmix_out, 0, qkv_out, 2 * HEADS, score_out, seq, seq, begin)


def add_product(a, b, total, column, step, steps, staged):
    at = slice(column, column + b.shape[1])
    part = lax.dot_general(a, b, TN, preferred_element_type=F32)

    @pl.when(step == 0)
    def _():
        total[:, at] = part

    @pl.when((step > 0) & (step < steps - 1))
    def _():
        total[:, at] += part

    @pl.when(step == steps - 1)
    def _():
        staged[:, at] = ((total[:, at] if steps > 1 else 0.0) + part).astype(staged.dtype)


def logit_grads(probs, sa, sb, first, seq, dl, dlt):
    for h in range(HEADS):
        at = slice(h * seq, (h + 1) * seq)
        prob = probs[:, at].astype(F32)
        d_prob = sa[first : first + seq, at] + sb[first : first + seq, at]
        d_logit = prob * (d_prob - jnp.sum(d_prob * prob, axis=-1, keepdims=True))
        dl[:, at] = d_logit.astype(BF16)
        dlt[:, at] = jnp.transpose(d_logit).astype(BF16)


def turn_probs(probs, seq, pt):
    for h in range(HEADS):
        at = slice(h * seq, (h + 1) * seq)
        pt[:, at] = jnp.transpose(probs[:, at].astype(F32)).astype(BF16)


def ship(staged, keep, send, member, sems):
    count, rows = keep.shape[0], keep.shape[1]
    copies = []
    for n in range(count):
        for k, dst in enumerate((keep, send)):
            start = pl.multiple_of((2 * n + (member + k) % 2) * rows, rows)
            copies.append(
                pltpu.make_async_copy(staged.at[pl.ds(start, rows)], dst.at[n], sems.at[2 * n + k])
            )
    return copies


def run_copies(copies):
    for copy in copies:
        copy.start()
    for copy in copies:
        copy.wait()


def backward_kernel(is_top, info, *refs, **sizes):
    step = pl.program_id(0)

    @pl.when(info[7] == 1)
    def _():
        backward_body(is_top, step, info, *refs, **sizes)


def backward_body(is_top, step, info, *refs, layout, scale, seq, width, steps):
    it = iter(refs)
    sa, sb = next(it), next(it)
    if not is_top:
        probs = next(it)
    qkv, dmix, x_in, gains, dy, v_prev = [next(it) for _ in range(6)]
    if not is_top:
        for _ in range(4):
            next(it)
    own_q, own_o = next(it), next(it)
    stages = take_stages(it, layout)
    dy_out, dmix_out, score_out, send_out = [next(it) for _ in range(4)]
    keep_a, send_a, keep_b, send_b = [next(it) for _ in range(4)]
    dl, dlt, pt, dqkv, mixed = [next(it) for _ in range(5)]
    total_a, staged_a, sem_a, total_b, staged_b, sem_b = [next(it) for _ in range(6)]
    wq, sem_q, wo, sem_o = [next(it) for _ in range(4)]
    if is_top:
        probs = next(it)
    get_q = Weights(info, 0, own_q, stages, slice(0, 3 * width), wq, sem_q)
    get_o = Weights(info, 2, own_o, stages, slice(3 * width, 4 * width), wo, sem_o)
    own, onward = info[0] == 0, info[8] == 1
    gain = gains[pl.ds(info[6], 1), :]

    @pl.when(step == 0)
    def _():
        pl.when(onward)(get_q.start)
        pl.when(onward)(get_o.start)
        if is_top:

            def keep(h, value):
                probs[:, h * seq : (h + 1) * seq] = value.astype(BF16)

            softmax_heads(sa.at[0:seq], sb.at[0:seq], scale, keep)
        logit_grads(probs, sa, sb, seq if is_top else 0, seq, dl, dlt)
        turn_probs(probs, seq, pt)

    mix(dl, qkv, HEADS, dqkv, 0, scale, seq)
    mix(dlt, qkv, 0, dqkv, width, scale, seq)
    mix(pt, dmix, 0, dqkv, 2 * width, None, seq)

    @pl.when(onward)
    def _():
        pl.when(step == 0)(get_q.wait)
        d_hat = mm_nt(dqkv[...], wq[...]).astype(BF16).astype(F32) * gain
        hat, rstd = norm_parts(x_in[...])
        mean_d = jnp.mean(d_hat, axis=-1, keepdims=True)
        mean_dh = jnp.mean(d_hat * hat, axis=-1, keepdims=True)
        d_x = dy[...].astype(F32) + rstd * (d_hat - mean_d - hat * mean_dh)
        dy_out[...] = d_x
        pl.when(step == 0)(get_o.wait)
        pack_rows(mm_nt(d_x.astype(BF16), wo[...]).astype(BF16), dmix_out, 0, seq)
        scores(dmix_out, 0, v_prev, 0, score_out, 0, seq, step == 0)

        @pl.when(step == steps - 1)
        def _():
            send_out[...] = score_out[...].astype(BF16)

    @pl.when(own)
    def _():
        mix(probs, qkv, 2 * HEADS, mixed, 0, None, seq)
        h = (norm_parts(x_in[...])[0] * gain).astype(BF16)
        add_product(mixed[...], dy[...].astype(BF16), total_a, 0, step, steps, staged_a)
        add_product(h, dqkv[:, 2 * width :], total_a, width, step, steps, staged_a)
        add_product(h, dqkv[:, : 2 * width], total_b, 0, step, steps, staged_b)

    @pl.when(own & (step == steps - 1))
    def _():
        copies = ship(staged_a, keep_a, send_a, info[4], sem_a)
        run_copies(copies + ship(staged_b, keep_b, send_b, info[4], sem_b))


def early_kernel(info, *refs, layout, seq, width, steps):
    probs, v, dmix, x_in, gains, dy, _, _, keep, send, pt, mixed, dv, total, staged, sem = refs
    step = pl.program_id(0)
    own = info[0] == 0

    @pl.when(own)
    def _():
        @pl.when(step == 0)
        def _():
            turn_probs(probs, seq, pt)

        mix(probs, v, 0, mixed, 0, None, seq)
        mix(pt, dmix, 0, dv, 0, None, seq)
        h = (norm_parts(x_in[...])[0] * gains[pl.ds(info[6], 1), :]).astype(BF16)
        add_product(mixed[...], dy[...].astype(BF16), total, 0, step, steps, staged)
        add_product(h, dv[...], total, width, step, steps, staged)

    @pl.when(own & (step == steps - 1))
    def _():
        run_copies(ship(staged, keep, send, info[4], sem))


def late_kernel(info, *refs, layout, scale, seq, width, steps):
    sa, sb, probs, qk, x_in, gains, _, _, keep, send, dl, dlt, dqk, total, staged, sem = refs
    step = pl.program_id(0)
    own = info[0] == 0

    @pl.when(own)
    def _():
        @pl.when(step == 0)
        def _():
            logit_grads(probs, sa, sb, 0, seq, dl, dlt)

        mix(dl, qk, HEADS, dqk, 0, scale, seq)
        mix(dlt, qk, 0, dqk, width, scale, seq)
        h = (norm_parts(x_in[...])[0] * gains[pl.ds(info[6], 1), :]).astype(BF16)
        add_product(h, dqk[...], total, 0, step, steps, staged)

    @pl.when(own & (step == steps - 1))
    def _():
        run_copies(ship(staged, keep, send, info[4], sem))


class Chain:
    def __init__(self, fetched, member, n_row, n_group, own, gains, seq, width, rows, scale):
        self.fetched, self.member, self.n_row, self.n_group = fetched, member, n_row, n_group
        self.gains = (gains, self.whole(*gains.shape))
        self.own, self.seq, self.width, self.rows = own, seq, width, rows
        self.scale = scale
        per_step = 4 if rows % 4 == 0 else 2
        self.chunk = per_step * seq
        self.steps = rows // per_step

    def info(self, now, other):
        picks = self.fetched.choices(now) + self.fetched.choices(other)
        picks += [self.member, self.fetched.half, self.fetched.section ^ now]
        picks += [self.fetched.section <= now, self.fetched.section < now]
        return jnp.stack(picks).astype(jnp.int32)

    def whole(self, rows, lanes):
        return pl.BlockSpec((rows, lanes), lambda i, s: (0, 0))

    def tile(self, lanes, column=0, part=1):
        return pl.BlockSpec((self.chunk // part, lanes), lambda i, s: (i, column))

    def packed(self, heads, column=0):
        return self.tile(heads * PACK * HEAD_DIM, column, PACK)

    def call(self, body, name, info, stages, ins, outs, scratch, flops, carried=(), own=None):
        any_spec = pl.BlockSpec(memory_space=pl.ANY)
        groups = self.fetched.stages[:stages]
        weights = list(self.own if own is None else own)
        weights += [a for group in groups for _, arrays in group for a in arrays]
        arrays = [a for a, _ in ins] + list(carried)
        shapes = [o for o, _ in outs]
        size = sum(math.prod(a.shape) * a.dtype.itemsize for a in arrays + shapes)
        aliases = {
            1 + len(ins) + n: len(outs) - len(carried) + n for n in range(len(carried))
        }
        layout = tuple(tuple((kind, len(arrays)) for kind, arrays in group) for group in groups)
        return pl.pallas_call(
            functools.partial(body, layout=layout),
            name=name,
            out_shape=shapes,
            grid_spec=pltpu.PrefetchScalarGridSpec(
                num_scalar_prefetch=1,
                grid=(self.steps,),
                in_specs=[spec for _, spec in ins] + [any_spec] * (len(carried) + len(weights)),
                out_specs=[spec for _, spec in outs],
                scratch_shapes=scratch,
            ),
            input_output_aliases=aliases,
            compiler_params=pltpu.CompilerParams(
                dimension_semantics=("arbitrary",), vmem_limit_bytes=VMEM_LIMIT + self.wide_bytes()
            ),
            cost_estimate=pl.CostEstimate(flops=flops, bytes_accessed=size, transcendentals=0),
        )(info, *arrays, *weights)

    def weight_scratch(self, columns):
        return [
            pltpu.VMEM((self.width, columns * self.width), BF16),
            pltpu.SemaphoreType.DMA((self.n_group * BLOCKS,)),
        ]

    def shape(self, rows, lanes, dtype):
        return jax.ShapeDtypeStruct((rows, lanes), dtype)

    def grad_outs(self):
        any_spec = pl.BlockSpec(memory_space=pl.ANY)
        rows = self.width // self.n_row
        shape = (self.n_row // 2, rows, 2 * self.width)
        return [(jax.ShapeDtypeStruct(shape, self.grad_type()), any_spec)] * 2

    def grad_type(self):
        return BF16 if self.width // self.n_row % 16 == 0 else F32

    def wide_bytes(self):
        return 0 if self.grad_type() == BF16 else 10 * 1024 * 1024

    def grad_scratch(self):
        shape = (self.width, 2 * self.width)
        scratch = [pltpu.VMEM(shape, F32), pltpu.VMEM(shape, self.grad_type())]
        return scratch + [pltpu.SemaphoreType.DMA((self.n_row,))]

    def forward(self, layer, x, prev, top):
        seq, width = self.seq, self.width
        n = self.rows * seq
        hw = HEADS * seq
        score_rows = seq if top is None else 2 * seq
        ins = [(x, self.tile(width)), self.gains]
        outs = [
            (self.shape(n // PACK, 3 * PACK * width, BF16), self.packed(3 * HEADS)),
            (self.shape(score_rows, hw, F32), self.whole(score_rows, hw)),
        ]
        scratch = self.weight_scratch(3)
        if prev is not None:
            ins = [
                (prev[0], self.whole(seq, hw)),
                (prev[1], self.whole(seq, hw)),
                (prev[2], self.packed(HEADS, 2)),
            ] + ins
            outs = [
                (self.shape(seq, hw, BF16), self.whole(seq, hw)),
                (self.shape(n, width, F32), self.tile(width)),
            ] + outs
            scratch += self.weight_scratch(1) + [pltpu.VMEM((self.chunk, width), BF16)]
        if top is not None:
            ins.append((top, self.tile(width)))
            outs.append((self.shape(n // PACK, PACK * width, BF16), self.packed(HEADS)))
            scratch += self.weight_scratch(1)
        body = functools.partial(
            forward_kernel, prev is not None, top is not None, scale=self.scale, seq=seq, width=width
        )
        return self.call(
            body,
            f"layer_in_{layer}",
            self.info(layer, max(layer - 1, 0)),
            self.fetched.first_stages if layer == 0 else None,
            ins,
            outs,
            scratch,
            2 * n * width * width * 5,
        )

    def backward(self, layer, scores, probs, qkv, dmix, x, dy, v_prev, grads):
        seq, width = self.seq, self.width
        n = self.rows * seq
        hw = HEADS * seq
        is_top = probs is None
        score_rows = scores[0].shape[0]
        square = pltpu.VMEM((seq, hw), BF16)
        ins = [(s, self.whole(score_rows, hw)) for s in scores]
        if not is_top:
            ins.append((probs, self.whole(seq, hw)))
        ins += [
            (qkv, self.packed(3 * HEADS)),
            (dmix, self.packed(HEADS)),
            (x, self.tile(width)),
            self.gains,
            (dy, self.tile(width)),
            (v_prev, self.packed(HEADS, 2)),
        ]
        outs = [
            (self.shape(n, width, F32), self.tile(width)),
            (self.shape(n // PACK, PACK * width, BF16), self.packed(HEADS)),
            (self.shape(seq, hw, F32), self.whole(seq, hw)),
            (self.shape(seq, hw, BF16), self.whole(seq, hw)),
            *self.grad_outs(),
            *self.grad_outs(),
        ]
        scratch = [square] * 3
        scratch += [pltpu.VMEM((self.chunk, lanes * width), BF16) for lanes in (3, 1)]
        scratch += self.grad_scratch() * 2 + self.weight_scratch(3) + self.weight_scratch(1)
        if is_top:
            scratch.append(square)
        body = functools.partial(
            backward_kernel, is_top, scale=self.scale, seq=seq, width=width, steps=self.steps
        )
        return self.call(
            body,
            f"layer_back_{layer}",
            self.info(layer, layer - 1),
            None,
            ins,
            outs,
            scratch,
            2 * n * width * width * 5,
            carried=grads,
        )

    def early(self, probs, qkv, dmix, x, dy, grads):
        seq, width = self.seq, self.width
        n, hw = self.rows * seq, HEADS * seq
        ins = [
            (probs, self.whole(seq, hw)),
            (qkv, self.packed(HEADS, 2)),
            (dmix, self.packed(HEADS)),
            (x, self.tile(width)),
            self.gains,
            (dy, self.tile(width)),
        ]
        scratch = [pltpu.VMEM((seq, hw), BF16)] + [pltpu.VMEM((self.chunk, width), BF16)] * 2
        return self.call(
            functools.partial(early_kernel, seq=seq, width=width, steps=self.steps),
            "early_back_0",
            self.info(0, 0),
            0,
            ins,
            self.grad_outs(),
            scratch + self.grad_scratch(),
            2 * n * width * width * 3,
            carried=grads,
            own=(),
        )

    def late(self, scores, probs, qkv, x, grads):
        seq, width = self.seq, self.width
        n, hw = self.rows * seq, HEADS * seq
        ins = [
            (scores[0], self.whole(seq, hw)),
            (scores[1], self.whole(seq, hw)),
            (probs, self.whole(seq, hw)),
            (qkv, self.packed(2 * HEADS)),
            (x, self.tile(width)),
            self.gains,
        ]
        scratch = [pltpu.VMEM((seq, hw), BF16)] * 2 + [pltpu.VMEM((self.chunk, 2 * width), BF16)]
        return self.call(
            functools.partial(
                late_kernel, scale=self.scale, seq=seq, width=width, steps=self.steps
            ),
            "late_back_0",
            self.info(0, 0),
            0,
            ins,
            self.grad_outs(),
            scratch + self.grad_scratch(),
            2 * n * width * width * 3,
            carried=grads,
            own=(),
        )


def group_swap(value, send, n_row, n_group):
    other = jnp.zeros_like(send)
    bit = 1
    while bit < n_group:
        if bit > 1:
            value = value + other
            send = value.astype(send.dtype)
        other = lax.ppermute(send, "row", [(r, r ^ bit) for r in range(n_row)])
        bit *= 2
    return value, other


class RowSum:
    def __init__(self, keep, send, place, n_row):
        self.keep, self.send, self.place, self.n_row, self.bit = keep, send, place, n_row, 1

    def exchange(self):
        perm = [(r, r ^ self.bit) for r in range(self.n_row)]
        return lax.ppermute(self.send.astype(BF16), "row", perm)

    def add(self, other):
        value = self.keep.astype(F32) + other.astype(F32)
        self.bit *= 2
        if self.bit == self.n_row:
            return value[0]
        mine = self.place // self.bit % 2
        pair = value.reshape(value.shape[0] // 2, 2, *value.shape[1:])
        self.keep = lax.dynamic_index_in_dim(pair, mine, 1, keepdims=False)
        self.send = lax.dynamic_index_in_dim(pair, 1 - mine, 1, keepdims=False).astype(BF16)
        return None

    def finish(self):
        value = None
        while value is None:
            value = self.add(self.exchange())
        return value


class Fetched:
    first_stages = 2

    def __init__(self, wqkv, wout, section, place, n_section, n_row, n_group):
        assert n_section == 4 and n_group % 2 == 0
        self.section, self.n_row, self.n_group = section, n_row, n_group
        self.member, self.half = place % n_group, place // n_group % 2
        self.last = n_section - 1
        self.block = wqkv.shape[0] // n_group // BLOCKS
        self.own = (wqkv, wout)
        self.to_last = section == (self.last ^ jnp.where(self.member % 2 == 0, 2, 1))
        self.mine = jnp.concatenate([self.own_block(self.half), self.own_block(2)], axis=0)
        self.got = self.hop(self.mine, 1)
        self.across = self.cross(self.got)
        self.stages = [self.halves(self.got, self.across)]

    def own_block(self, place, count=1):
        start = (self.member * BLOCKS + place) * self.block
        rows = [lax.dynamic_slice_in_dim(w, start, count * self.block, 0) for w in self.own]
        return jnp.concatenate(rows, axis=1)

    def hop(self, value, even_bit):
        perm = [
            (s * self.n_row + r, (s ^ (even_bit if r % 2 == 0 else 3 - even_bit)) * self.n_row + r)
            for s in range(self.last + 1)
            for r in range(self.n_row)
        ]
        return lax.ppermute(value, ("section", "row"), perm)

    def cross(self, value):
        perm = [(r, r ^ self.n_group) for r in range(self.n_row)]
        return lax.ppermute(value[: self.block], "row", perm)

    def halves(self, got, across):
        return [(DIRECT, self.share(got)), (ACROSS, self.share(across))]

    def second(self, x):
        second, x = lax.optimization_barrier((jnp.where(self.to_last, self.got, self.mine), x))
        second = self.hop(second, 2)
        self.stages.append(self.halves(second, self.cross(second)))
        low = jnp.where(self.half == 0, self.got[: self.block], self.across)
        high = jnp.where(self.half == 0, self.across, self.got[: self.block])
        relayed = jnp.concatenate([low, high, self.got[self.block :]], axis=0)
        third = jnp.where(self.to_last, self.own_block(0, BLOCKS), relayed)
        self.third = self.hop(third, 2)
        return x

    def finish(self, ready):
        third, ready = lax.optimization_barrier((self.third, ready))
        self.stages.append([(FULL, self.share(third))])
        return ready

    def share(self, value):
        have = [value[None]]
        bit = 1
        while bit < self.n_group:
            send = have[0] if len(have) == 1 else jnp.concatenate(have, axis=0)
            have.append(lax.ppermute(send, "row", [(r, r ^ bit) for r in range(self.n_row)]))
            bit *= 2
        return have

    def choices(self, layer):
        offset = self.section ^ layer
        at_last = self.section == self.last
        picks = []
        for parity in (self.member % 2, 1 - self.member % 2):
            first = jnp.where(parity == 0, 1, 2)
            second = jnp.where(at_last, 3, 3 - first)
            pick = jnp.where(offset == first, 1, jnp.where(offset == second, 2, 3))
            picks.append(jnp.where(offset == 0, 0, pick))
        return picks


def local(tokens, embed, ln_gain, w_qkv, w_out, out_grad):
    n_section = lax.axis_size("section")
    n_row = lax.axis_size("row")
    section = lax.axis_index("section")
    place = lax.axis_index("row")
    micro, rows_here, seq = tokens.shape
    width = embed.shape[1]
    n_group = n_row // micro
    member = place % n_group
    rows = rows_here * micro
    scale = HEAD_DIM ** (-0.5) / math.sqrt(rows_here * n_row)
    fetched = Fetched(w_qkv[0], w_out[0], section, place, n_section, n_row, n_group)
    same = [[m * n_group + g for m in range(micro)] for g in range(n_group)]
    exchange = functools.partial(
        lax.all_to_all,
        axis_name="row",
        split_axis=0,
        concat_axis=0,
        axis_index_groups=same,
        tiled=True,
    )
    here = place // n_group
    tok = exchange(tokens)[here ^ jnp.arange(micro)].reshape(-1)
    blocks = [lax.dynamic_index_in_dim(out_grad, here, 0)]
    for offset in range(1, micro):
        send = lax.dynamic_index_in_dim(out_grad, here ^ offset, 0)
        perm = [(r, r ^ (offset * n_group)) for r in range(n_row)]
        blocks.append(lax.ppermute(send, "row", perm))
    top_grad = jnp.concatenate(blocks, axis=0).reshape(rows * seq, width)
    gain_parts = [ln_gain] + [
        lax.ppermute(ln_gain, "section", [(s, s ^ offset) for s in range(n_section)])
        for offset in range(1, n_section)
    ]
    gains = jnp.concatenate(gain_parts, axis=0)
    table = (jnp.arange(embed.shape[0], dtype=jnp.int32)[:, None] == tok[None, :]).astype(BF16)
    x = lax.dot_general(table, embed, TN, preferred_element_type=F32)

    x, gains = fetched.second((x, gains))
    chain = Chain(
        fetched, member, n_row, n_group, (w_qkv, w_out), gains, seq, width, rows, scale
    )
    xs, qkvs, probs = [], [], []
    scores = None
    dmix = None
    for layer in range(n_section):
        prev = None if layer == 0 else (*scores, qkvs[-1])
        top = top_grad if layer == n_section - 1 else None
        outs = list(chain.forward(layer, x, prev, top))
        if prev is not None:
            probs.append(outs.pop(0))
            x = outs.pop(0)
        xs.append(x)
        qkvs.append(outs[0])
        if top is not None:
            dmix = outs[2]
        scores = group_swap(outs[1], outs[1], n_row, n_group)
        if layer == 0:
            scores = (scores[0], fetched.finish(scores[1]))
    probs.append(None)

    dy = top_grad
    grads = ()
    for layer in range(n_section - 1, 0, -1):
        dy, dmix, part, send, *grads = chain.backward(
            layer,
            scores,
            probs[layer],
            qkvs[layer],
            dmix,
            xs[layer],
            dy,
            qkvs[layer - 1],
            grads,
        )
        scores = group_swap(part, send, n_row, n_group)
    early = RowSum(*chain.early(probs[0], qkvs[0], dmix, xs[0], dy, grads[:2]), place, n_row)
    early.add(early.exchange())
    early.send, other = lax.optimization_barrier((early.send, scores[1]))
    moved = early.exchange()
    late = RowSum(*chain.late((scores[0], other), probs[0], qkvs[0], xs[0], grads[2:]), place, n_row)
    late.send, moved = lax.optimization_barrier((late.send, moved))
    early.add(moved)
    g_early = early.finish()
    g_late = late.finish()
    g_qkv = jnp.concatenate([g_late, g_early[:, width:]], axis=1)
    block = width // n_row
    w_here = lax.dynamic_slice_in_dim(w_qkv[0], place * block, block, 0).astype(F32)
    gain_here = lax.dynamic_slice_in_dim(ln_gain, place * block, block, 1)
    g_gain = jnp.sum(g_qkv * w_here, axis=1)[None] / gain_here
    return (g_qkv[None], g_early[None, :, :width], g_gain)


def solution(mesh):
    in_specs = (
        P(None, "row", None),
        P(),
        P("section", None),
        P("section", None, None),
        P("section", None, None),
        P(None, "row", None, None),
    )
    out_specs = (P("section", "row", None), P("section", "row", None), P("section", "row"))
    return jax.shard_map(local, mesh=mesh, in_specs=in_specs, out_specs=out_specs, check_vma=False)
```
